32 devices in a mesh: dp: 16 (over z, y, core), tensor: 2 (over x).
Axes of the slice: x: 2, y: 2, z: 4, core: 2. Of those that a mesh axis runs over, the one named last changes fastest.
Arguments:
- tokens: bfloat16 [32, 1024, 768], P('dp', 'tensor'), may hold values from -6 to 6
- segment_ids: int32 [32, 1024], P('dp'), may hold values from 0 to 3, as said below
- timestep: int32 [32], P('dp'), may hold values from 0 to 999
- ln_gain: float32 [768], replicated, may hold values from 0.5 to 1.5
- query_key_value_weight: bfloat16 [3, 768, 768], P(None, None, 'tensor'), may hold values from -0.21875 to 0.21875
- output_projection: bfloat16 [768, 768], P('tensor'), may hold values from -1.75 to 1.75
- up_projection: bfloat16 [768, 3072], P(None, 'tensor'), may hold values from -0.21875 to 0.21875
- down_projection: bfloat16 [3072, 768], P('tensor'), may hold values from -0.109375 to 0.109375
- ada_weight: bfloat16 [128, 2304], replicated, may hold values from -0.5 to 0.5
- ada_bias: float32 [2304], replicated, may hold values from 0.5 to 1.5
- cotangent: bfloat16 [32, 1024, 768], P('dp', 'tensor')
Outputs:
- mixed: bfloat16 [32, 1024, 768], P('dp', 'tensor')
- d_tokens: bfloat16 [32, 1024, 768], P('dp', 'tensor')
- d_ln_gain: float32 [768], replicated
- d_qkv_weight: float32 [3, 768, 768], P(None, None, 'tensor')
- d_out_weight: float32 [768, 768], P('tensor')
- d_up_weight: float32 [768, 3072], P(None, 'tensor')
- d_down_weight: float32 [3072, 768], P('tensor')
- d_ada_weight: float32 [128, 2304], replicated
- d_ada_bias: float32 [2304], replicated
The draws below stay inside these ranges and needn't reach their ends.
Inputs may be any that keep to these rules, and one draw needn't show every extreme that they name: `segment_ids`: within a sequence the ids never fall and start at 0; equal ids mark one document; the last token has id 3; one document of each sequence covers at least its positions 256 to 767.
All inputs are finite; a program needn't handle non-finite values.
Results may differ from the reference program's by a relative error of at most 0.02.
Values may be sent and summed in bfloat16 or wider, within the bound.
A program may use at most 320 MiB of HBM per device.

```python
import math
import jax
import jax.numpy as jnp
from jax import lax

D = 768
HD = 64
FF = 3072
TEMB = 128
LEN = 1024
SEQS = 32


def draw_segment_ids(key, part):
    key = jax.random.fold_in(key, 7)
    key_one, key_two, key_three = jax.random.split(key, 3)
    first_cut = jax.random.randint(key_one, (SEQS, 1), 1, max(LEN // 4, 2))
    other_cut = jax.random.randint(key_three, (SEQS, 1), 1, max(LEN // 4, 2))
    last_cut = jax.random.randint(key_two, (SEQS, 1), 3 * LEN // 4, LEN)
    position = jnp.arange(LEN, dtype=jnp.int32)[None, :]
    ids = (position >= first_cut).astype(jnp.int32) + (position >= other_cut).astype(jnp.int32) + (position >= last_cut).astype(jnp.int32)
    return ids.astype(jnp.int32)


def draw_cotangent(key, part):
    key = jax.random.fold_in(key, 11)
    fraction = jnp.arange(SEQS, dtype=jnp.float32) / max(SEQS - 1, 1)
    base = jax.random.normal(key, (SEQS, LEN, D), jnp.float32)
    factor = 0.6 + 1.2 * fraction
    return (base * factor[:, None, None]).astype(jnp.bfloat16)


def place_ends(drawn, own_key, least, high):
    dims = drawn.shape
    index_at = [jax.random.randint(jax.random.fold_in(own_key, axis), (), 0, dims[axis]) for axis in range(len(dims))]
    drawn = drawn.at[tuple(index_at)].set(least)
    longest = dims.index(max(dims))
    index_at[longest] = (index_at[longest] + 1) % dims[longest]
    return drawn.at[tuple(index_at)].set(high)


def block_levels(own_key, dims, cuts, least, largest):
    level = 1.0
    for dim, blocks in cuts:
        draws = jax.random.uniform(jax.random.fold_in(jax.random.fold_in(own_key, 6), dim), (blocks,), jnp.float32, least / len(cuts), largest / len(cuts))
        level = level * jnp.repeat(jnp.exp(draws), dims[dim] // blocks).reshape((-1,) + (1,) * (len(dims) - 1 - dim))
    return level


def gaussian(key, dims, scale, reach, shards=(), kind=jnp.bfloat16):
    values = scale * jax.random.normal(key, dims, jnp.float32)
    if shards:
        values = values * block_levels(key, dims, shards, -0.22, 0.18)
    return jnp.clip(values, -reach, reach).astype(kind)


def setup_inputs(seed: int = 0) -> dict:
    key_list = jax.random.split(jax.random.key(seed), 12)
    return {
        "tokens": gaussian(key_list[0], (SEQS, LEN, D), 1.0, 6.0, ((0, 16), (1, 2))),
        "segment_ids": draw_segment_ids(jax.random.fold_in(key_list[11], 71), 0),
        "timestep": place_ends(jax.random.randint(key_list[2], (SEQS,), 0, 1000), jax.random.fold_in(key_list[2], 1), 0, 999).astype(jnp.int32),
        "ln_gain": jnp.clip(1.0 + 0.1 * jax.random.normal(key_list[3], (D,), jnp.float32), 0.5, 1.5),
        "query_key_value_weight": gaussian(key_list[4], (3, D, D), D ** -0.5, 0.21875, ((2, 2),)),
        "output_projection": gaussian(key_list[5], (D, D), (max(D // 64, 1)) ** -0.5, 1.75, ((0, 2),)),
        "up_projection": gaussian(key_list[6], (D, FF), D ** -0.5, 0.21875, ((1, 2),)),
        "down_projection": gaussian(key_list[7], (FF, D), FF ** -0.5, 0.109375, ((0, 2),)),
        "ada_weight": gaussian(key_list[8], (TEMB, 3 * D), TEMB ** -0.5, 0.5),
        "ada_bias": jnp.clip(1.0 + 0.1 * jax.random.normal(key_list[9], (3 * D,), jnp.float32), 0.5, 1.5),
        "cotangent": draw_cotangent(jax.random.fold_in(key_list[11], 71), 0),
    }


epsilon = 1e-05
masked_score = -1000000000.0
highest = lax.Precision.HIGHEST

@jax.custom_vjp
def low(v):
    return lax.optimization_barrier(v.astype(jnp.bfloat16)).astype(jnp.float32)

@jax.custom_vjp
def low_back(v):
    return v

def low_keep(v):
    return (low(v), None)

def low_pass(kept, grad):
    return (grad,)

def back_keep(v):
    return (v, None)

def back_low(kept, grad):
    return (low(grad),)
low.defvjp(low_keep, low_pass)
low_back.defvjp(back_keep, back_low)

def layer_norm(values):
    centred = values - lax.optimization_barrier(jnp.mean(values, axis=-1, keepdims=True))
    variance = lax.optimization_barrier(jnp.mean(centred * centred, axis=-1, keepdims=True))
    return centred * lax.rsqrt(variance + epsilon)

def rotary_tables(length, size):
    half_size = size // 2
    position = jnp.arange(length, dtype=jnp.float32)
    frequency = 10000.0 ** (-jnp.arange(half_size, dtype=jnp.float32) / half_size)
    angles = position[:, None] * frequency[None, :]
    return (jnp.cos(angles)[:, None, :], jnp.sin(angles)[:, None, :])

def rotate(values, cosine, sine):
    half_size = values.shape[-1] // 2
    first_half = values[..., :half_size]
    second_half = values[..., half_size:]
    return jnp.concatenate([first_half * cosine - second_half * sine, second_half * cosine + first_half * sine], axis=-1)

def time_embedding(timestep, width):
    half_size = width // 2
    frequency = jnp.exp(-math.log(10000.0) * jnp.arange(half_size, dtype=jnp.float32) / half_size)
    angles = timestep.astype(jnp.float32)[:, None] * frequency[None, :]
    return jnp.concatenate([jnp.cos(angles), jnp.sin(angles)], axis=-1)

def forward(params, values, segments, embedding):
    gain, wqkv, wout, wup, wdown, wada, bada = params
    groups, length, width = values.shape
    heads = width // HD
    score_scale = 1.0 / math.sqrt(HD)
    normed = low(layer_norm(values) * gain)
    unnormed_rows = low_back(jnp.einsum('gld,cde->cgle', normed, wqkv, precision=highest))
    unnormed_rows = unnormed_rows.reshape(3, groups, length, heads, HD)
    cosine, sine = rotary_tables(length, HD)
    queries = low(rotate(unnormed_rows[0], cosine, sine))
    keys_rot = low(rotate(unnormed_rows[1], cosine, sine))
    values_low = low(unnormed_rows[2])
    doc_mask = segments[:, :, None] == segments[:, None, :]
    block_rows = min(512, length)
    count = length // block_rows

    def attend(start_row):
        query_block = lax.dynamic_slice_in_dim(queries, start_row, block_rows, 1)
        mask_block = lax.dynamic_slice_in_dim(doc_mask, start_row, block_rows, 1)
        scores = low_back(jnp.einsum('gqhe,gkhe->ghqk', query_block, keys_rot, precision=highest) * score_scale)
        scores = jnp.where(mask_block[:, None], scores, masked_score)
        weights = low(jax.nn.softmax(scores, axis=-1))
        return jnp.einsum('ghqk,gkhe->gqhe', weights, values_low, precision=highest)
    starts = jnp.arange(count, dtype=jnp.int32) * block_rows
    mixed_heads = lax.map(jax.checkpoint(attend), starts)
    mixed_heads = jnp.moveaxis(mixed_heads, 0, 1).reshape(groups, length, width)
    attention_mixture = low(low_back(mixed_heads))
    attn_out = low_back(jnp.einsum('gle,ed->gld', attention_mixture, wout, precision=highest))
    hidden = values + attn_out
    modulation = jnp.dot(embedding, wada, precision=highest) + bada
    shift = modulation[:, :width]
    scale = modulation[:, width:2 * width]
    gate = modulation[:, 2 * width:]
    modulated = low(layer_norm(hidden) * (1.0 + scale[:, None]) + shift[:, None])
    upward = low_back(jnp.einsum('gld,df->glf', modulated, wup, precision=highest))
    gelu_activation = low(jax.nn.gelu(upward))
    branch = low_back(jnp.einsum('glf,fd->gld', gelu_activation, wdown, precision=highest))
    return hidden + gate[:, None] * branch

def reference(tokens, segment_ids, timestep, ln_gain, query_key_value_weight, output_projection, up_projection, down_projection, ada_weight, ada_bias, cotangent):
    params = tuple((weight_array.astype(jnp.float32) for weight_array in (ln_gain, query_key_value_weight, output_projection, up_projection, down_projection, ada_weight, ada_bias)))
    group = math.gcd(SEQS, max(1, 4096 // LEN))
    steps = SEQS // group

    def shaped(array):
        return array.reshape((steps, group) + array.shape[1:])

    def one_group(totals, items):
        block_tokens, block_segments, block_times, block_cot = items
        embedding = time_embedding(block_times, TEMB)

        def apply(weights, inputs):
            return forward(weights, inputs, block_segments, embedding)
        result, pull = jax.vjp(apply, params, block_tokens.astype(jnp.float32))
        grads, input_grad = pull(block_cot.astype(jnp.float32))
        totals = jax.tree.map(jnp.add, totals, grads)
        return (totals, (result.astype(jnp.bfloat16), input_grad.astype(jnp.bfloat16)))
    zeros = jax.tree.map(jnp.zeros_like, params)
    totals, (mixed, d_tokens) = lax.scan(one_group, zeros, (shaped(tokens), shaped(segment_ids), shaped(timestep), shaped(cotangent)))
    return (mixed.reshape(tokens.shape), d_tokens.reshape(tokens.shape), totals[0], totals[1], totals[2], totals[3], totals[4], totals[5], totals[6])
```

```python
import functools
import math

import jax
import jax.numpy as jnp
import numpy as np
from jax import lax
from jax.experimental import pallas as pl
from jax.experimental.pallas import tpu as pltpu
from jax.sharding import PartitionSpec as P

HD = 64
TEMB = 128
EPS = 1e-05
MASKED = -1000000000.0
f32 = jnp.float32
bf16 = jnp.bfloat16
VMEM_LIMIT = 56 * 1024 * 1024


def dot_nn(a, b):
    return lax.dot_general(a, b, (((1,), (0,)), ((), ())), preferred_element_type=f32)


def dot_nt(a, b):
    return lax.dot_general(a, b, (((1,), (1,)), ((), ())), preferred_element_type=f32)


def dot_tn(a, b):
    return lax.dot_general(a, b, (((0,), (0,)), ((), ())), preferred_element_type=f32)


def norm_parts(values):
    centred = values - jnp.mean(values, axis=-1, keepdims=True)
    variance = jnp.mean(centred * centred, axis=-1, keepdims=True)
    inverse = lax.rsqrt(variance + EPS)
    return centred * inverse, inverse


def norm_back(grad, normed, inverse):
    return inverse * (
        grad
        - jnp.mean(grad, axis=-1, keepdims=True)
        - normed * jnp.mean(grad * normed, axis=-1, keepdims=True)
    )


def rotary_np(length):
    half = HD // 2
    position = np.arange(length, dtype=np.float32)
    frequency = (10000.0 ** (-np.arange(half, dtype=np.float32) / half)).astype(np.float32)
    angles = position[:, None] * frequency[None, :]
    cosine, sine = np.cos(angles), np.sin(angles)
    cosine = np.concatenate([cosine, cosine] * 2, axis=1).astype(np.float32)
    sine = np.concatenate([-sine, sine] * 2, axis=1).astype(np.float32)
    return cosine, sine


def swap_halves(values):
    lane = lax.broadcasted_iota(jnp.int32, values.shape, 1)
    first = (lane % HD) < (HD // 2)
    return jnp.where(first, pltpu.roll(values, 128 - HD // 2, 1), pltpu.roll(values, HD // 2, 1))


def params(**kw):
    return pltpu.CompilerParams(vmem_limit_bytes=VMEM_LIMIT, **kw)


def cost(flops, nbytes, trans=0):
    return pl.CostEstimate(flops=int(flops), bytes_accessed=int(nbytes), transcendentals=int(trans))


def qkv_kernel(x_ref, gain_ref, w_ref, cos_ref, sin_ref, n_ref, q_ref, k_ref, v_ref):
    normed, _ = norm_parts(x_ref[...].astype(f32))
    normed = (normed * gain_ref[...]).astype(bf16)
    n_ref[...] = normed
    cosine, sine = cos_ref[...], sin_ref[...]
    width = q_ref.shape[1]
    for which, out in ((0, q_ref), (1, k_ref)):
        raw = dot_nn(normed, w_ref[which])
        for pair in range(width // 128):
            part = raw[:, pair * 128 : pair * 128 + 128]
            turned = (part * cosine + swap_halves(part) * sine).astype(bf16)
            if which == 0:
                turned = turned * jnp.asarray(0.125, bf16)
            out[:, pair * 128 : pair * 128 + 128] = turned
    v_ref[...] = dot_nn(normed, w_ref[2]).astype(bf16)


def qkv_call(x, gain, w, cosine, sine):
    length, width = x.shape
    out = w.shape[2]
    rows = 256
    row = lambda n: pl.BlockSpec((rows, n), lambda i: (i, 0))
    return pl.pallas_call(
        qkv_kernel,
        grid=(length // rows,),
        in_specs=[
            row(width),
            pl.BlockSpec((1, width), lambda i: (0, 0)),
            pl.BlockSpec((3, width, out), lambda i: (0, 0, 0)),
            row(128),
            row(128),
        ],
        out_specs=[row(width), row(out), row(out), row(out)],
        out_shape=[jax.ShapeDtypeStruct((length, width), bf16)]
        + [jax.ShapeDtypeStruct((length, out), bf16)] * 3,
        compiler_params=params(),
        cost_estimate=cost(2 * length * width * 3 * out, 2 * length * width + 6 * width * out),
    )(x, gain, w, cosine, sine)


def attend_kernel(q_ref, k_ref, v_ref, segc_ref, segr_ref, o_ref, lse_ref):
    rows = q_ref.shape[0]
    lane = lax.broadcasted_iota(jnp.int32, (1, 128), 1)
    q, k, v = q_ref[...], k_ref[...], v_ref[...]
    mask = segc_ref[...] == segr_ref[...]
    low = lane < HD
    parts = []
    for head in range(2):
        mine = low if head == 0 else jnp.logical_not(low)
        scores = dot_nt(jnp.where(mine, q, jnp.zeros_like(q)), k)
        scores = jnp.where(mask, scores, MASKED)
        largest = jnp.max(scores, axis=1, keepdims=True)
        weights = jnp.exp(scores - largest).astype(bf16)
        mixed = dot_nn(weights, jnp.where(mine, v, jnp.ones_like(v)))
        total = pltpu.roll(mixed, HD, 1)
        parts.append((mixed / total, largest + jnp.log(total)))
    o_ref[...] = jnp.where(low, parts[0][0], parts[1][0]).astype(bf16)
    lse = jnp.where(low, parts[0][1], parts[1][1]).T
    lse_ref[0, 0:1, :] = lse[0:1, :]
    lse_ref[0, 1:2, :] = lse[HD : HD + 1, :]


def attend_call(q, k, v, segc, segr):
    length, width = q.shape
    pairs = width // 128
    rows = 256
    return pl.pallas_call(
        attend_kernel,
        grid=(pairs, length // rows),
        in_specs=[
            pl.BlockSpec((rows, 128), lambda p, i: (i, p)),
            pl.BlockSpec((length, 128), lambda p, i: (0, p)),
            pl.BlockSpec((length, 128), lambda p, i: (0, p)),
            pl.BlockSpec((rows, 1), lambda p, i: (i, 0)),
            pl.BlockSpec((1, length), lambda p, i: (0, 0)),
        ],
        out_specs=[
            pl.BlockSpec((rows, 128), lambda p, i: (i, p)),
            pl.BlockSpec((1, 8, rows), lambda p, i: (p, 0, i)),
        ],
        out_shape=[
            jax.ShapeDtypeStruct((length, width), bf16),
            jax.ShapeDtypeStruct((pairs, 8, length), f32),
        ],
        compiler_params=params(),
        cost_estimate=cost(
            4 * 4 * length * length * width, 8 * length * width, length * length * width // HD
        ),
    )(q, k, v, segc, segr)


def attend_back_kernel(
    q_ref, k_ref, v_ref, o_ref, do_ref, lse_ref, segc_ref, segr_ref, cos_ref, sin_ref,
    dq_ref, dk_ref, dv_ref, acc_ref,
):
    length = q_ref.shape[0]
    rows = 256
    lane = lax.broadcasted_iota(jnp.int32, (1, 128), 1)
    low = lane < HD
    q, do = q_ref[...], do_ref[...]
    product = do.astype(f32) * o_ref[...].astype(f32)
    high_part = product.astype(bf16)
    low_part = (product - high_part.astype(f32)).astype(bf16)
    row8 = lax.broadcasted_iota(jnp.int32, (8, 128), 0)
    lane8 = lax.broadcasted_iota(jnp.int32, (8, 128), 1)
    select = jnp.where((lane8 // HD) == row8, 1.0, 0.0).astype(bf16)
    delta = dot_nt(select, high_part) + dot_nt(select, low_part)
    lse = lse_ref[0]
    segr = segr_ref[...]
    zero = jnp.zeros_like(q)
    q_heads = (jnp.where(low, q, zero), jnp.where(low, zero, q))
    do_heads = (jnp.where(low, do, zero), jnp.where(low, zero, do))
    acc_ref[...] = jnp.zeros_like(acc_ref)
    for block in range(length // rows):
        span = pl.ds(block * rows, rows)
        k, v = k_ref[span, :], v_ref[span, :]
        mask = segc_ref[span, :] == segr
        dv = jnp.zeros((rows, 128), f32)
        dk = jnp.zeros((rows, 128), f32)
        dq = jnp.zeros((128, length), f32)
        for head in range(2):
            mine = low if head == 0 else jnp.logical_not(low)
            kh = jnp.where(mine, k, jnp.zeros_like(k))
            vh = jnp.where(mine, v, jnp.zeros_like(v))
            scores = jnp.where(mask, dot_nt(kh, q), MASKED)
            probs = jnp.exp(scores - lse[head : head + 1, :])
            dv = dv + dot_nn(probs.astype(bf16), do_heads[head])
            d_probs = dot_nt(vh, do)
            d_scores = (probs * (d_probs - delta[head : head + 1, :])).astype(bf16)
            dk = dk + dot_nn(d_scores, q_heads[head])
            dq = dq + dot_tn(kh, d_scores)
        acc_ref[...] += dq
        cosine, sine = cos_ref[span, :], sin_ref[span, :]
        dk_ref[span, :] = (dk * cosine - swap_halves(dk) * sine).astype(bf16)
        dv_ref[span, :] = dv.astype(bf16)
    dq = acc_ref[...].T * 0.125
    dq_ref[...] = (dq * cos_ref[...] - swap_halves(dq) * sin_ref[...]).astype(bf16)


def attend_back_call(q, k, v, o, do, lse, segc, segr, cosine, sine):
    length, width = q.shape
    pairs = width // 128
    whole = pl.BlockSpec((length, 128), lambda p: (0, p))
    fixed = pl.BlockSpec((length, 128), lambda p: (0, 0))
    return pl.pallas_call(
        attend_back_kernel,
        grid=(pairs,),
        in_specs=[whole] * 5
        + [
            pl.BlockSpec((1, 8, length), lambda p: (p, 0, 0)),
            pl.BlockSpec((length, 1), lambda p: (0, 0)),
            pl.BlockSpec((1, length), lambda p: (0, 0)),
            fixed,
            fixed,
        ],
        out_specs=[whole] * 3,
        out_shape=[jax.ShapeDtypeStruct((length, width), bf16)] * 3,
        scratch_shapes=[pltpu.VMEM((128, length), f32)],
        compiler_params=params(),
        cost_estimate=cost(
            10 * 4 * length * length * width, 16 * length * width, length * length * width // HD
        ),
    )(q, k, v, o, do, lse, segc, segr, cosine, sine)


def middle_kernel(
    x_ref, cot_ref, oa_ref, ob_ref, wa_ref, wb_ref, mod_ref, hidden_ref, modul_ref, dbranch_ref
):
    hidden = x_ref[...].astype(f32) + (
        dot_nn(oa_ref[...], wa_ref[...]) + dot_nn(ob_ref[...], wb_ref[...])
    )
    hidden_ref[...] = hidden
    normed, _ = norm_parts(hidden)
    shift, scale, gate = mod_ref[0:1, :], mod_ref[1:2, :], mod_ref[2:3, :]
    modul_ref[...] = (normed * (1.0 + scale) + shift).astype(bf16)
    dbranch_ref[...] = (cot_ref[...].astype(f32) * gate).astype(bf16)


def middle_call(x, cot, oa, ob, wa, wb, mod):
    length, width = x.shape
    rows = 256
    row = lambda n: pl.BlockSpec((rows, n), lambda i: (i, 0))
    full = lambda a: pl.BlockSpec(a.shape, lambda i: (0, 0))
    return pl.pallas_call(
        middle_kernel,
        grid=(length // rows,),
        in_specs=[row(width), row(width), row(oa.shape[1]), row(ob.shape[1]), full(wa), full(wb), full(mod)],
        out_specs=[row(width)] * 3,
        out_shape=[
            jax.ShapeDtypeStruct((length, width), f32),
            jax.ShapeDtypeStruct((length, width), bf16),
            jax.ShapeDtypeStruct((length, width), bf16),
        ],
        compiler_params=params(),
        cost_estimate=cost(2 * length * width * width, 14 * length * width),
    )(x, cot, oa, ob, wa, wb, mod)


def gelu_both(u):
    c0 = math.sqrt(2.0 / math.pi)
    square = u * u
    t = jnp.tanh(u * (c0 + (c0 * 0.044715) * square))
    half = 0.5 + 0.5 * t
    act = u * half
    slope = half + (0.5 * u) * (1.0 - t * t) * (c0 + (3.0 * c0 * 0.044715) * square)
    return act, slope


def feed_kernel(
    modul_ref, dbranch_ref, up_ref, down_ref, bin_ref, din_ref,
    branch_ref, dmod_ref, dup_ref, ddown_ref, act_scr, dupw_scr,
):
    step = pl.program_id(0)

    @pl.when(step == 0)
    def _():
        branch_ref[...] = bin_ref[...]
        dmod_ref[...] = din_ref[...]

    length = modul_ref.shape[0]
    rows = 256
    for block in range(length // rows):
        span = pl.ds(block * rows, rows)
        u = dot_nn(modul_ref[span, :], up_ref[...])
        act, slope = gelu_both(u)
        act = act.astype(bf16)
        act_scr[span, :] = act
        d_act = dot_nt(dbranch_ref[span, :], down_ref[...])
        d_up = (d_act * slope).astype(bf16)
        dupw_scr[span, :] = d_up
        branch_ref[span, :] += dot_nn(act, down_ref[...])
        dmod_ref[span, :] += dot_nt(d_up, up_ref[...])
    dup_ref[...] = dot_tn(modul_ref[...], dupw_scr[...]).astype(bf16)
    ddown_ref[...] = dot_tn(act_scr[...], dbranch_ref[...]).astype(bf16)


def feed_call(modul, dbranch, up, down, branch_in, dmod_in):
    length, width = modul.shape
    hidden = up.shape[1]
    block = 512
    full = pl.BlockSpec((length, width), lambda j: (0, 0))
    return pl.pallas_call(
        feed_kernel,
        grid=(hidden // block,),
        in_specs=[
            full,
            full,
            pl.BlockSpec((width, block), lambda j: (0, j)),
            pl.BlockSpec((block, width), lambda j: (j, 0)),
            full,
            full,
        ],
        out_specs=[
            full,
            full,
            pl.BlockSpec((width, block), lambda j: (0, j)),
            pl.BlockSpec((block, width), lambda j: (j, 0)),
        ],
        out_shape=[
            jax.ShapeDtypeStruct((length, width), f32),
            jax.ShapeDtypeStruct((length, width), f32),
            jax.ShapeDtypeStruct((width, hidden), bf16),
            jax.ShapeDtypeStruct((hidden, width), bf16),
        ],
        scratch_shapes=[pltpu.VMEM((length, block), bf16), pltpu.VMEM((length, block), bf16)],
        compiler_params=params(),
        cost_estimate=cost(12 * length * width * hidden, 16 * length * width + 8 * width * hidden),
    )(modul, dbranch, up, down, branch_in, dmod_in)


def between_kernel(
    hidden_ref, cot_ref, branch_ref, dmod_ref, mod_ref, oa_ref, ob_ref, wa_ref, wb_ref,
    mixed_ref, dhidden_ref, doa_ref, dob_ref, dwa_ref, dwb_ref, sums_ref, dattn_scr,
):
    length = hidden_ref.shape[0]
    rows = 256
    scale, gate = mod_ref[1:2, :], mod_ref[2:3, :]
    sums_ref[...] = jnp.zeros_like(sums_ref)
    for block in range(length // rows):
        span = pl.ds(block * rows, rows)
        hidden = hidden_ref[span, :]
        dout = cot_ref[span, :].astype(f32)
        branch = branch_ref[span, :]
        mixed_ref[span, :] = (hidden + gate * branch).astype(bf16)
        normed, inverse = norm_parts(hidden)
        dmod = dmod_ref[span, :]
        sums_ref[0:1, :] += jnp.sum(dmod, axis=0, keepdims=True)
        sums_ref[1:2, :] += jnp.sum(dmod * normed, axis=0, keepdims=True)
        sums_ref[2:3, :] += jnp.sum(dout * branch, axis=0, keepdims=True)
        dhidden = dout + norm_back(dmod * (1.0 + scale), normed, inverse)
        dhidden_ref[span, :] = dhidden
        dattn = dhidden.astype(bf16)
        dattn_scr[span, :] = dattn
        doa_ref[span, :] = dot_nt(dattn, wa_ref[...]).astype(bf16)
        dob_ref[span, :] = dot_nt(dattn, wb_ref[...]).astype(bf16)
    dwa_ref[...] = dot_tn(oa_ref[...], dattn_scr[...]).astype(bf16)
    dwb_ref[...] = dot_tn(ob_ref[...], dattn_scr[...]).astype(bf16)


def between_call(hidden, cot, branch, dmod, mod, oa, ob, wa, wb):
    length, width = hidden.shape
    spec = pl.BlockSpec(memory_space=pltpu.VMEM)
    half = oa.shape[1]
    return pl.pallas_call(
        between_kernel,
        in_specs=[spec] * 9,
        out_specs=[spec] * 7,
        out_shape=[
            jax.ShapeDtypeStruct((length, width), bf16),
            jax.ShapeDtypeStruct((length, width), f32),
            jax.ShapeDtypeStruct((length, half), bf16),
            jax.ShapeDtypeStruct((length, half), bf16),
            jax.ShapeDtypeStruct((half, width), bf16),
            jax.ShapeDtypeStruct((half, width), bf16),
            jax.ShapeDtypeStruct((8, width), f32),
        ],
        scratch_shapes=[pltpu.VMEM((length, width), bf16)],
        compiler_params=params(),
        cost_estimate=cost(4 * length * width * width, 24 * length * width),
    )(hidden, cot, branch, dmod, mod, oa, ob, wa, wb)


def last_kernel(
    x_ref, n_ref, gain_ref, dhidden_ref,
    dqa_ref, dka_ref, dva_ref, dqb_ref, dkb_ref, dvb_ref, wa_ref, wb_ref,
    dtok_ref, dgain_ref, dwa_ref, dwb_ref,
):
    length = x_ref.shape[0]
    rows = 256
    dgain_ref[...] = jnp.zeros_like(dgain_ref)
    sides = (((dqa_ref, dka_ref, dva_ref), wa_ref, dwa_ref), ((dqb_ref, dkb_ref, dvb_ref), wb_ref, dwb_ref))
    for block in range(length // rows):
        span = pl.ds(block * rows, rows)
        dnormed = jnp.zeros((rows, x_ref.shape[1]), f32)
        for grads, w_ref, _ in sides:
            for which in range(3):
                dnormed = dnormed + dot_nt(grads[which][span, :], w_ref[which])
        normed, inverse = norm_parts(x_ref[span, :].astype(f32))
        dgain_ref[0:1, :] += jnp.sum(dnormed * normed, axis=0, keepdims=True)
        dtok_ref[span, :] = (
            dhidden_ref[span, :] + norm_back(dnormed * gain_ref[...], normed, inverse)
        ).astype(bf16)
    for grads, _, dw_ref in sides:
        for which in range(3):
            dw_ref[which] = dot_tn(n_ref[...], grads[which][...]).astype(bf16)


def last_call(x, n, gain, dhidden, grads_a, grads_b, wa, wb):
    length, width = x.shape
    spec = pl.BlockSpec(memory_space=pltpu.VMEM)
    return pl.pallas_call(
        last_kernel,
        in_specs=[spec] * 12,
        out_specs=[spec] * 4,
        out_shape=[
            jax.ShapeDtypeStruct((length, width), bf16),
            jax.ShapeDtypeStruct((8, width), f32),
            jax.ShapeDtypeStruct(wa.shape, bf16),
            jax.ShapeDtypeStruct(wb.shape, bf16),
        ],
        compiler_params=params(),
        cost_estimate=cost(12 * length * width * width, 30 * length * width),
    )(x, n, gain, dhidden, *grads_a, *grads_b, wa, wb)


def time_embedding(timestep):
    half = TEMB // 2
    frequency = jnp.exp(-math.log(10000.0) * jnp.arange(half, dtype=f32) / half)
    angles = timestep.astype(f32)[:, None] * frequency[None, :]
    return jnp.concatenate([jnp.cos(angles), jnp.sin(angles)], axis=-1)


SWAP = ((0, 1), (1, 0))


def per_device(
    tokens, segment_ids, timestep, ln_gain, w_qkv, w_out, w_up, w_down, ada_weight, ada_bias, cotangent
):
    half, width = tokens.shape[1], tokens.shape[2]
    length = 2 * half
    side = lax.axis_index("tensor")
    pick = lambda a, i: lax.dynamic_index_in_dim(a, i, 0, keepdims=False)

    def swap(a):
        return lax.ppermute(a, "tensor", SWAP)

    def whole_sequence(a):
        mine, came = pick(a, side), swap(pick(a, 1 - side))
        first = jnp.where(side == 0, mine, came)
        second = jnp.where(side == 0, came, mine)
        return jnp.concatenate([first, second], axis=0)

    def split_sequence(a):
        halves = a.reshape(2, half, width)
        came = swap(pick(halves, 1 - side))
        mine = pick(halves, side)
        first = jnp.where(side == 0, mine, came)
        second = jnp.where(side == 0, came, mine)
        return jnp.stack([first, second])

    x = whole_sequence(tokens)
    cot = whole_sequence(cotangent)
    o_qkv, o_out, o_up, o_down = swap(w_qkv), swap(w_out), swap(w_up), swap(w_down)
    segments = pick(segment_ids, side)
    segc, segr = segments.reshape(length, 1), segments.reshape(1, length)
    gain = ln_gain.reshape(1, width)
    cosine, sine = (jnp.asarray(a) for a in rotary_np(length))

    embedding = time_embedding(timestep)
    mine = pick(embedding, side)
    mod = jnp.sum(mine[:, None] * ada_weight.astype(f32), axis=0) + ada_bias
    mod = mod.reshape(3, width)

    n, qa, ka, va = qkv_call(x, gain, w_qkv, cosine, sine)
    oa, lsea = attend_call(qa, ka, va, segc, segr)
    _, qb, kb, vb = qkv_call(x, gain, o_qkv, cosine, sine)
    ob, lseb = attend_call(qb, kb, vb, segc, segr)
    hidden, modul, dbranch = middle_call(x, cot, oa, ob, w_out, o_out, mod)
    zero = jnp.zeros((length, width), f32)
    branch, dmod, dup_a, ddown_a = feed_call(modul, dbranch, w_up, w_down, zero, zero)
    branch, dmod, dup_b, ddown_b = feed_call(modul, dbranch, o_up, o_down, branch, dmod)
    mixed, dhidden, doa, dob, dwo_a, dwo_b, sums = between_call(
        hidden, cot, branch, dmod, mod, oa, ob, w_out, o_out
    )
    grads_a = attend_back_call(qa, ka, va, oa, doa, lsea, segc, segr, cosine, sine)
    grads_b = attend_back_call(qb, kb, vb, ob, dob, lseb, segc, segr, cosine, sine)
    dtok, dgain, dwq_a, dwq_b = last_call(x, n, gain, dhidden, grads_a, grads_b, w_qkv, o_qkv)

    def total(own, other):
        return lax.psum(own + swap(other), "dp").astype(f32)

    d_qkv = total(dwq_a, dwq_b)
    d_out = total(dwo_a, dwo_b)
    d_up = total(dup_a, dup_b)
    d_down = total(ddown_a, ddown_b)

    small = jnp.concatenate([sums[:3].reshape(3 * width), dgain[0], mine])
    every = lax.all_gather(small, ("dp", "tensor"), axis=0)
    d_mods = every[:, : 3 * width]
    d_gain = jnp.sum(every[:, 3 * width : 4 * width], axis=0)
    d_ada_weight = jnp.dot(every[:, 4 * width :].T, d_mods, precision=lax.Precision.HIGHEST)
    d_ada_bias = jnp.sum(d_mods, axis=0)
    return (
        split_sequence(mixed),
        split_sequence(dtok),
        d_gain,
        d_qkv,
        d_out,
        d_up,
        d_down,
        d_ada_weight,
        d_ada_bias,
    )


def solution(mesh):
    in_specs = (
        P("dp", "tensor", None),
        P("dp", None),
        P("dp"),
        P(),
        P(None, None, "tensor"),
        P("tensor", None),
        P(None, "tensor"),
        P("tensor", None),
        P(),
        P(),
        P("dp", "tensor", None),
    )
    out_specs = (
        P("dp", "tensor", None),
        P("dp", "tensor", None),
        P(),
        P(None, None, "tensor"),
        P("tensor", None),
        P(None, "tensor"),
        P("tensor", None),
        P(),
        P(),
    )
    return jax.shard_map(
        per_device, mesh=mesh, in_specs=in_specs, out_specs=out_specs, check_vma=False
    )
```

```python
import functools
import math

import jax
import jax.numpy as jnp
import numpy as np
from jax import lax
from jax.experimental import pallas as pl
from jax.experimental.pallas import tpu as pltpu
from jax.sharding import PartitionSpec as P

HD = 64
TEMB = 128
EPS = 1e-05
MASKED = -1000000000.0
f32 = jnp.float32
bf16 = jnp.bfloat16
VMEM_LIMIT = 56 * 1024 * 1024


def dot_nn(a, b):
    return lax.dot_general(a, b, (((1,), (0,)), ((), ())), preferred_element_type=f32)


def dot_nt(a, b):
    return lax.dot_general(a, b, (((1,), (1,)), ((), ())), preferred_element_type=f32)


def dot_tn(a, b):
    return lax.dot_general(a, b, (((0,), (0,)), ((), ())), preferred_element_type=f32)


def norm_parts(values):
    centred = values - jnp.mean(values, axis=-1, keepdims=True)
    variance = jnp.mean(centred * centred, axis=-1, keepdims=True)
    inverse = lax.rsqrt(variance + EPS)
    return centred * inverse, inverse


def norm_back(grad, normed, inverse):
    return inverse * (
        grad
        - jnp.mean(grad, axis=-1, keepdims=True)
        - normed * jnp.mean(grad * normed, axis=-1, keepdims=True)
    )


def rotary_np(length):
    half = HD // 2
    position = np.arange(length, dtype=np.float32)
    frequency = (10000.0 ** (-np.arange(half, dtype=np.float32) / half)).astype(np.float32)
    angles = position[:, None] * frequency[None, :]
    cosine, sine = np.cos(angles), np.sin(angles)
    cosine = np.concatenate([cosine, cosine] * 2, axis=1).astype(np.float32)
    sine = np.concatenate([-sine, sine] * 2, axis=1).astype(np.float32)
    return cosine, sine


def swap_halves(values):
    lane = lax.broadcasted_iota(jnp.int32, values.shape, 1)
    first = (lane % HD) < (HD // 2)
    return jnp.where(first, pltpu.roll(values, 128 - HD // 2, 1), pltpu.roll(values, HD // 2, 1))


def params(**kw):
    return pltpu.CompilerParams(vmem_limit_bytes=VMEM_LIMIT, **kw)


def cost(flops, nbytes, trans=0):
    return pl.CostEstimate(flops=int(flops), bytes_accessed=int(nbytes), transcendentals=int(trans))


BITS = (1, 2, 4, 8)
MESH = pl.DeviceIdType.MESH


class Place:
    def __init__(self):
        self.me = lax.axis_index("dp")
        self.side = lax.axis_index("tensor")
        self.bits = [(self.me // bit) % 2 for bit in BITS]
        self.partners = [{"dp": self.me + bit * (1 - 2 * b)} for bit, b in zip(BITS, self.bits)]
        self.across = {"tensor": 1 - self.side}

    def greet(self, partners):
        barrier = pltpu.get_barrier_semaphore()
        for partner in partners:
            pl.semaphore_signal(barrier, inc=1, device_id=partner, device_id_type=MESH)
        pl.semaphore_wait(barrier, len(partners))


def remote(src, dst, send, recv, partner):
    return pltpu.make_async_remote_copy(
        src_ref=src, dst_ref=dst, send_sem=send, recv_sem=recv, device_id=partner, device_id_type=MESH
    )


class Reducer:
    STAGES = 5

    def __init__(self, place, chunks, received, sends, recvs):
        self.place, self.chunks, self.received = place, chunks, received
        self.sends, self.recvs = sends, recvs
        self.rows = chunks.shape[2]

    @staticmethod
    def scratch(count, rows, cols):
        shapes = [
            (count, 2, rows // 2, cols),
            (count, 2, rows // 4, cols),
            (count, rows // 4, cols),
            (count, rows // 8, cols),
            (count, rows // 16, cols),
        ]
        return (
            [pltpu.VMEM((count, 2, rows, cols), bf16)]
            + [pltpu.VMEM(shape, bf16) for shape in shapes]
            + [pltpu.SemaphoreType.DMA((count, 5)), pltpu.SemaphoreType.DMA((count, 5))]
        )

    def spans(self, stage):
        core, y, zl, zh = self.place.bits
        r = self.rows
        base = 0
        bits = {0: core, 1: y, 3: zl, 4: zh}
        sizes = {0: r // 2, 1: r // 4, 3: r // 8, 4: r // 16}
        for s in (0, 1, 3, 4):
            if s < stage:
                base = base + bits[s] * sizes[s]
        if stage == 2:
            span = pl.ds(pl.multiple_of(base, 16), r // 4)
            return span, span, self.place.across
        n = sizes[stage]
        keep = pl.ds(pl.multiple_of(base + bits[stage] * n, 16), n)
        send = pl.ds(pl.multiple_of(base + (1 - bits[stage]) * n, 16), n)
        return keep, send, self.place.partners[{0: 0, 1: 1, 3: 2, 4: 3}[stage]]

    def copy(self, stage, c):
        _, send, partner = self.spans(stage)
        if stage < 2:
            source = self.chunks.at[c, :, send, :]
        else:
            source = self.chunks.at[c, 1 if stage == 2 else 0, send, :]
        return remote(
            source, self.received[stage].at[c], self.sends.at[c, stage], self.recvs.at[c, stage], partner
        )

    def start(self, stage, c):
        self.copy(stage, c).start()

    def finish(self, stage, c, put=None):
        self.copy(stage, c).wait()
        keep, _, _ = self.spans(stage)
        came = self.received[stage]
        if stage < 2:
            for half in range(2):
                self.chunks[c, half, keep, :] += came[c, half]
        elif stage < 4:
            self.chunks[c, 0, keep, :] += came[c]
        else:
            put(c, self.chunks[c, 0, keep, :] + came[c])


class Gatherer:
    STAGES = 4

    def __init__(self, place, array, dim, sends, recvs):
        self.place, self.array, self.dim, self.sends, self.recvs = place, array, dim, sends, recvs
        core, y, zl, zh = place.bits
        n = array.shape[dim] // 16
        self.size = n
        self.bases = [
            core * 8 + y * 4 + zl * 2 + zh,
            core * 8 + y * 4 + zl * 2,
            core * 8 + y * 4,
            core * 8,
        ]

    def view(self, stage):
        n = self.size
        span = pl.ds(pl.multiple_of(self.bases[stage] * n, 16), 2**stage * n)
        return self.array.at[(slice(None),) * self.dim + (span,)]

    def copy(self, stage):
        span = self.view(stage)
        return remote(
            span, span, self.sends.at[stage], self.recvs.at[stage], self.place.partners[3 - stage]
        )

    def start(self, stage):
        self.copy(stage).start()

    def finish(self, stage):
        self.copy(stage).wait()


def qkv_rows(row, rows, x_ref, gain_ref, w_ref, cos_ref, sin_ref, n_ref, q_ref, k_ref, v_ref, first):
    span = pl.ds(row, rows)
    pairs = w_ref.shape[2] // 128
    if n_ref is None:
        normed = x_ref[span, :]
    else:
        normed, _ = norm_parts(x_ref[span, :].astype(f32))
        normed = (normed * gain_ref[...]).astype(bf16)
        n_ref[span, :] = normed
    cosine, sine = cos_ref[span, :], sin_ref[span, :]
    for which, out in ((0, q_ref), (1, k_ref)):
        raw = dot_nn(normed, w_ref[which])
        for pair in range(pairs):
            part = raw[:, pair * 128 : pair * 128 + 128]
            turned = (part * cosine + swap_halves(part) * sine).astype(bf16)
            if which == 0:
                turned = turned * jnp.asarray(0.125, bf16)
            out[first + pair, span, :] = turned
    raw = dot_nn(normed, w_ref[2]).astype(bf16)
    for pair in range(pairs):
        v_ref[first + pair, span, :] = raw[:, pair * 128 : pair * 128 + 128]


def attend_rows(pair, row, rows, q_ref, k_ref, v_ref, segc_ref, segr_ref, o_ref, lse_ref):
    lane = lax.broadcasted_iota(jnp.int32, (1, 128), 1)
    low = lane < HD
    span = pl.ds(row, rows)
    q, k, v = q_ref[pair, span, :], k_ref[pair], v_ref[pair]
    mask = segc_ref[span, :] == segr_ref[...]
    parts = []
    for head in range(2):
        mine = low if head == 0 else jnp.logical_not(low)
        scores = dot_nt(jnp.where(mine, q, jnp.zeros_like(q)), k)
        scores = jnp.where(mask, scores, MASKED)
        largest = jnp.max(scores, axis=1, keepdims=True)
        weights = jnp.exp(scores - largest).astype(bf16)
        mixed = dot_nn(weights, jnp.where(mine, v, jnp.ones_like(v)))
        total = pltpu.roll(mixed, HD, 1)
        parts.append((mixed / total, largest + jnp.log(total)))
    o_ref[span, pl.ds(pl.multiple_of(pair * 128, 128), 128)] = jnp.where(
        low, parts[0][0], parts[1][0]
    ).astype(bf16)
    lse = jnp.where(low, parts[0][1], parts[1][1]).T
    lse_ref[pair, 0:1, span] = lse[0:1, :]
    lse_ref[pair, 1:2, span] = lse[HD : HD + 1, :]


def front_kernel(
    tok, cot, wq, wo, wu, wd, gain_ref, segc_ref, segr_ref, cos_ref, sin_ref,
    x_out, cot_out, n_out, q_out, k_out, v_out, o_out, lse_out, oq, oo, ou, od,
    xs, ns, qs, ks, vs, os, ls, wbuf, local, xsend, xrecv, wsend, wrecv,
):
    place = Place()
    core, y = place.bits[0], place.bits[1]
    side = place.side
    length, half = xs.shape[0], xs.shape[0] // 2
    rows = 256
    place.greet([place.across, place.partners[0], place.partners[1]])

    own_rows = pl.ds(pl.multiple_of(side * half, half), half)
    send_tok = remote(tok.at[1 - side], xs.at[own_rows, :], xsend.at[0], xrecv.at[0], place.across)
    send_tok.start()
    send_cot = remote(cot.at[1 - side], cot_out.at[own_rows, :], xsend.at[1], xrecv.at[1], place.across)

    groups = ((wq, oq), (wo, oo), (wu, ou), (wd, od))

    def quarter(ref, index):
        if len(ref.shape) == 3:
            n = ref.shape[1] // 4
            return ref.at[:, pl.ds(pl.multiple_of(index * n, 16), n), :]
        n = ref.shape[0] // 4
        return ref.at[pl.ds(pl.multiple_of(index * n, 16), n), :]

    mine = core + 2 * y
    facing = core + 2 * (1 - y)

    def fetch(group, stage):
        own, other = groups[group]
        if stage == 0:
            src, dst, partner = quarter(own, mine), quarter(other, mine), place.across
        elif stage == 1:
            src, dst, partner = quarter(other, mine), quarter(other, mine), place.partners[1]
        elif stage == 2:
            src, dst, partner = quarter(other, mine), quarter(other, mine), place.partners[0]
        else:
            src, dst, partner = quarter(other, facing), quarter(other, facing), place.partners[0]
        return remote(src, dst, wsend.at[group, stage], wrecv.at[group, stage], partner)

    locals_ = []

    def copy_here(src, dst, index):
        c = pltpu.make_async_copy(src, dst, local.at[index])
        c.start()
        return c

    get_x = copy_here(tok.at[side], xs.at[own_rows, :], 0)
    get_w = copy_here(wq, wbuf, 1)
    put_cot = copy_here(cot.at[side], cot_out.at[own_rows, :], 2)
    fetch(0, 0).start()
    get_x.wait()
    get_w.wait()

    def qkv_half(base, w_first, n_ref):
        def step(i, carry):
            row = pl.multiple_of(base + i * rows, rows)
            qkv_rows(
                row, rows, xs if n_ref is not None else ns, gain_ref, wbuf, cos_ref, sin_ref,
                n_ref, qs, ks, vs, w_first,
            )
            return carry

        lax.fori_loop(0, half // rows, step, 0)

    qkv_half(side * half, 0, ns)
    send_tok.wait()
    fetch(1, 0).start()
    fetch(2, 0).start()
    qkv_half((1 - side) * half, 0, ns)
    put_x = copy_here(xs, x_out, 3)
    put_n = copy_here(ns, n_out, 4)
    fetch(0, 0).wait()
    fetch(0, 1).start()
    fetch(0, 2).start()

    def attend(pair, carry):
        @pl.when(pair == 1)
        def _():
            fetch(0, 1).wait()
            fetch(0, 3).start()
            fetch(1, 0).wait()
            fetch(1, 1).start()
            fetch(1, 2).start()

        @pl.when(pair == 2)
        def _():
            fetch(2, 0).wait()
            fetch(2, 1).start()
            fetch(2, 2).start()
            fetch(3, 0).start()

        @pl.when(pair == 3)
        def _():
            fetch(0, 2).wait()
            fetch(0, 3).wait()
            copy = pltpu.make_async_copy(oq, wbuf, local.at[1])
            copy.start()
            copy.wait()
            qkv_half(0, 3, None)
            qkv_half(half, 3, None)

        @pl.when(pair == 4)
        def _():
            send_cot.start()
            fetch(1, 1).wait()
            fetch(1, 3).start()
            fetch(2, 1).wait()
            fetch(2, 3).start()
            fetch(3, 0).wait()
            fetch(3, 1).start()
            fetch(3, 2).start()

        for block in range(length // rows):
            attend_rows(pair, block * rows, rows, qs, ks, vs, segc_ref, segr_ref, os, ls)
        return carry

    lax.fori_loop(0, 6, attend, 0)
    fetch(3, 1).wait()
    fetch(3, 3).start()
    ends = [
        copy_here(qs, q_out, 5),
        copy_here(ks, k_out, 6),
        copy_here(vs, v_out, 7),
        copy_here(os, o_out, 8),
        copy_here(ls, lse_out, 9),
    ]
    for c in [put_cot, put_x, put_n] + ends:
        c.wait()
    fetch(1, 2).wait()
    fetch(1, 3).wait()
    fetch(2, 2).wait()
    fetch(2, 3).wait()
    fetch(3, 2).wait()
    fetch(3, 3).wait()
    send_cot.wait()


def front_call(tokens, cot, wq, wo, wu, wd, gain, segc, segr, cosine, sine):
    length, width = 2 * tokens.shape[1], tokens.shape[2]
    any_ = pl.BlockSpec(memory_space=pl.ANY)
    vm = pl.BlockSpec(memory_space=pltpu.VMEM)
    shape = jax.ShapeDtypeStruct
    pairs = width // 128
    return pl.pallas_call(
        front_kernel,
        in_specs=[any_] * 6 + [vm] * 5,
        out_specs=[any_] * 12,
        out_shape=[
            shape((length, width), bf16),
            shape((length, width), bf16),
            shape((length, width), bf16),
            shape((pairs, length, 128), bf16),
            shape((pairs, length, 128), bf16),
            shape((pairs, length, 128), bf16),
            shape((length, width), bf16),
            shape((pairs, 8, length), f32),
            shape(wq.shape, bf16),
            shape(wo.shape, bf16),
            shape(wu.shape, bf16),
            shape(wd.shape, bf16),
        ],
        scratch_shapes=[
            pltpu.VMEM((length, width), bf16),
            pltpu.VMEM((length, width), bf16),
            pltpu.VMEM((pairs, length, 128), bf16),
            pltpu.VMEM((pairs, length, 128), bf16),
            pltpu.VMEM((pairs, length, 128), bf16),
            pltpu.VMEM((length, width), bf16),
            pltpu.VMEM((pairs, 8, length), f32),
            pltpu.VMEM(wq.shape, bf16),
            pltpu.SemaphoreType.DMA((10,)),
            pltpu.SemaphoreType.DMA((2,)),
            pltpu.SemaphoreType.DMA((2,)),
            pltpu.SemaphoreType.DMA((4, 4)),
            pltpu.SemaphoreType.DMA((4, 4)),
        ],
        compiler_params=params(collective_id=0, has_side_effects=True),
        name="front",
    )(tokens, cot, wq, wo, wu, wd, gain, segc, segr, cosine, sine)


def gelu_both(u):
    c0 = math.sqrt(2.0 / math.pi)
    square = u * u
    t = jnp.tanh(u * (c0 + (c0 * 0.044715) * square))
    half = 0.5 + 0.5 * t
    act = u * half
    slope = half + (0.5 * u) * (1.0 - t * t) * (c0 + (3.0 * c0 * 0.044715) * square)
    return act, slope


FEED_STEPS = 6


def feed_kernel(
    x_ref, cot_ref, o_ref, woa_ref, wob_ref, mod_ref, upa_ref, upb_ref, downa_ref, downb_ref,
    mixed_ref, dhidden_ref, do_ref, dwo_ref, sums_ref, finup_ref, findown_ref,
    hidden, modul, dbranch, modul_t, branch, dmod, acts, dups, *reducing,
):
    step = pl.program_id(0)
    place = Place()
    length, width = x_ref.shape
    block = upa_ref.shape[1]
    rows = 256
    blocks = length // rows
    half = woa_ref.shape[0]
    ups, downs = reducing[0], reducing[8]
    reducers = [Reducer(place, a[0], a[1:6], a[6], a[7]) for a in (reducing[:8], reducing[8:])]

    def put_up(c, value):
        finup_ref[:, pl.ds(pl.multiple_of(c * block, 128), block)] = value

    def put_down(c, value):
        findown_ref[c] = value

    puts = (put_up, put_down)

    @pl.when(step == 0)
    def _():
        place.greet(place.partners + [place.across])
        shift, scale, gate = mod_ref[0:1, :], mod_ref[1:2, :], mod_ref[2:3, :]

        def rows_of(i, carry):
            span = pl.ds(pl.multiple_of(i * rows, rows), rows)
            h = x_ref[span, :].astype(f32) + (
                dot_nn(o_ref[span, :half], woa_ref[...]) + dot_nn(o_ref[span, half:], wob_ref[...])
            )
            hidden[span, :] = h
            normed, _ = norm_parts(h)
            m = (normed * (1.0 + scale) + shift).astype(bf16)
            modul[span, :] = m
            modul_t[:, span] = m.T
            d = (cot_ref[span, :].astype(f32) * gate).astype(bf16)
            dbranch[span, :] = d
            branch[span, :] = jnp.zeros((rows, width), f32)
            dmod[span, :] = jnp.zeros((rows, width), f32)
            return carry

        lax.fori_loop(0, blocks, rows_of, 0)

    for stage in range(Reducer.STAGES):
        c = step - 1 - stage

        @pl.when(jnp.logical_and(c >= 0, c < FEED_STEPS))
        def _(stage=stage, c=c):
            for reducer, put in zip(reducers, puts):
                reducer.finish(stage, c, put)
                if stage + 1 < Reducer.STAGES:
                    reducer.start(stage + 1, c)

    @pl.when(step < FEED_STEPS)
    def _():
        up = jnp.concatenate([upa_ref[...], upb_ref[...]], axis=1)
        down = jnp.concatenate([downa_ref[...], downb_ref[...]], axis=0)
        for i in range(blocks):
            span = pl.ds(i * rows, rows)
            u = dot_nn(modul[span, :], up)
            act, slope = gelu_both(u)
            act = act.astype(bf16)
            acts[span, :] = act
            d_act = dot_nt(dbranch[span, :], down)
            d_up = (d_act * slope).astype(bf16)
            dups[span, :] = d_up
            branch[span, :] += dot_nn(act, down)
            dmod[span, :] += dot_nt(d_up, up)
        grad = dot_nn(modul_t[...], dups[...]).astype(bf16)
        ups[step, 0] = grad[:, :block]
        ups[step, 1] = grad[:, block:]
        reducers[0].start(0, step)
        grad = dot_tn(acts[...], dbranch[...]).astype(bf16)
        downs[step, 0] = grad[:block]
        downs[step, 1] = grad[block:]
        reducers[1].start(0, step)

    @pl.when(step == FEED_STEPS)
    def _():
        sums_ref[...] = jnp.zeros_like(sums_ref)

    @pl.when(jnp.logical_and(step >= FEED_STEPS, step < FEED_STEPS + blocks))
    def _():
        span = pl.ds(pl.multiple_of((step - FEED_STEPS) * rows, rows), rows)
        scale, gate = mod_ref[1:2, :], mod_ref[2:3, :]
        h = hidden[span, :]
        dout = cot_ref[span, :].astype(f32)
        br = branch[span, :]
        mixed_ref[span, :] = (h + gate * br).astype(bf16)
        normed, inverse = norm_parts(h)
        dm = dmod[span, :]
        sums_ref[0:1, :] += jnp.sum(dm, axis=0, keepdims=True)
        sums_ref[1:2, :] += jnp.sum(dm * normed, axis=0, keepdims=True)
        sums_ref[2:3, :] += jnp.sum(dout * br, axis=0, keepdims=True)
        dh = dout + norm_back(dm * (1.0 + scale), normed, inverse)
        dhidden_ref[span, :] = dh
        dattn = dh.astype(bf16)
        modul[span, :] = dattn
        do_ref[span, :half] = dot_nt(dattn, woa_ref[...]).astype(bf16)
        do_ref[span, half:] = dot_nt(dattn, wob_ref[...]).astype(bf16)

    @pl.when(step == FEED_STEPS + blocks)
    def _():
        for i in range(2):
            grad = dot_tn(o_ref[:, i * half : (i + 1) * half], modul[...]).astype(bf16)
            dwo_ref[i, :half, :] = grad[:, :half]
            dwo_ref[i, half:, :] = grad[:, half:]


def feed_call(x, cot, o, woa, wob, mod, upa, upb, downa, downb):
    length, width = x.shape
    hidden = upa.shape[1]
    block = hidden // FEED_STEPS
    half = woa.shape[0]
    last = FEED_STEPS - 1

    def const(shape):
        zeros = (0,) * len(shape)
        return pl.BlockSpec(shape, lambda j: zeros, pipeline_mode=pl.Buffered(1))

    ups = pl.BlockSpec((width, block), lambda j: (0, jnp.minimum(j, last)))
    downs = pl.BlockSpec((block, width), lambda j: (jnp.minimum(j, last), 0))
    shape = jax.ShapeDtypeStruct
    outs = [
        shape((length, width), bf16),
        shape((length, width), f32),
        shape((length, width), bf16),
        shape((2, width, half), bf16),
        shape((8, width), f32),
        shape((width // 16, hidden), bf16),
        shape((FEED_STEPS, block // 16, width), bf16),
    ]
    return pl.pallas_call(
        feed_kernel,
        grid=(FEED_STEPS + length // 256 + 1,),
        in_specs=[const(a.shape) for a in (x, cot, o, woa, wob, mod)] + [ups, ups, downs, downs],
        out_specs=[const(o.shape) for o in outs],
        out_shape=outs,
        scratch_shapes=[
            pltpu.VMEM((length, width), f32),
            pltpu.VMEM((length, width), bf16),
            pltpu.VMEM((length, width), bf16),
            pltpu.VMEM((width, length), bf16),
            pltpu.VMEM((length, width), f32),
            pltpu.VMEM((length, width), f32),
            pltpu.VMEM((length, 2 * block), bf16),
            pltpu.VMEM((length, 2 * block), bf16),
        ]
        + Reducer.scratch(FEED_STEPS, width, block)
        + Reducer.scratch(FEED_STEPS, block, width),
        compiler_params=params(collective_id=1, has_side_effects=True),
        name="feed",
    )(x, cot, o, woa, wob, mod, upa, upb, downa, downb)


def attend_back(
    q_ref, k_ref, v_ref, o_ref, do_ref, lse_ref, segc_ref, segr_ref, cos_ref, sin_ref, acc_ref, put
):
    length = o_ref.shape[0]
    rows = 256
    lane = lax.broadcasted_iota(jnp.int32, (1, 128), 1)
    low = lane < HD
    q, do = q_ref[0], do_ref[...]
    product = do.astype(f32) * o_ref[...].astype(f32)
    high_part = product.astype(bf16)
    low_part = (product - high_part.astype(f32)).astype(bf16)
    row8 = lax.broadcasted_iota(jnp.int32, (8, 128), 0)
    lane8 = lax.broadcasted_iota(jnp.int32, (8, 128), 1)
    select = jnp.where((lane8 // HD) == row8, 1.0, 0.0).astype(bf16)
    delta = dot_nt(select, high_part) + dot_nt(select, low_part)
    lse = lse_ref[0]
    segr = segr_ref[...]
    zero = jnp.zeros_like(q)
    q_heads = (jnp.where(low, q, zero), jnp.where(low, zero, q))
    do_heads = (jnp.where(low, do, zero), jnp.where(low, zero, do))
    acc_ref[...] = jnp.zeros_like(acc_ref)
    for block in range(length // rows):
        span = pl.ds(block * rows, rows)
        k, v = k_ref[0, span, :], v_ref[0, span, :]
        mask = segc_ref[span, :] == segr
        dv = jnp.zeros((rows, 128), f32)
        dk = jnp.zeros((rows, 128), f32)
        dq = jnp.zeros((128, length), f32)
        for head in range(2):
            mine = low if head == 0 else jnp.logical_not(low)
            kh = jnp.where(mine, k, jnp.zeros_like(k))
            vh = jnp.where(mine, v, jnp.zeros_like(v))
            scores = jnp.where(mask, dot_nt(kh, q), MASKED)
            probs = jnp.exp(scores - lse[head : head + 1, :])
            dv = dv + dot_nn(probs.astype(bf16), do_heads[head])
            d_probs = dot_nt(vh, do)
            d_scores = (probs * (d_probs - delta[head : head + 1, :])).astype(bf16)
            dk = dk + dot_nn(d_scores, q_heads[head])
            dq = dq + dot_tn(kh, d_scores)
        acc_ref[...] += dq
        cosine, sine = cos_ref[span, :], sin_ref[span, :]
        put(1, span, (dk * cosine - swap_halves(dk) * sine).astype(bf16))
        put(2, span, dv.astype(bf16))
    dq = acc_ref[...].T * 0.125
    put(0, slice(None), (dq * cos_ref[...] - swap_halves(dq) * sin_ref[...]).astype(bf16))


def back_kernel(
    q_ref, k_ref, v_ref, o_ref, do_ref, lse_ref, segc_ref, segr_ref, cos_ref, sin_ref,
    n_ref, x_ref, gain_ref, dhidden_ref, wa_ref, wb_ref, dwo_ref, small_ref, mixed_in, up_in, down_in,
    up_out, down_out, out_out, qkv_out, mixed_out, dtok_out, every_out, dgain_ref,
    n_t, draw, acc, dtok, fin_out, fin_qkv, every_ref, gains, gains_in,
    chunks, r0, r1, r2, r3, r4, sends, recvs,
    fsend, frecv, asend, arecv, gsend, grecv, ssend, srecv, xsend, xrecv, local,
):
    step = pl.program_id(0)
    place = Place()
    side = place.side
    length, width = x_ref.shape
    half_len = length // 2
    rows = 256
    blocks = length // rows
    half = wa_ref.shape[2]
    reducer = Reducer(place, chunks, (r0, r1, r2, r3, r4), sends, recvs)
    gather_ffn = [
        Gatherer(place, up_out, 0, fsend.at[0], frecv.at[0]),
        Gatherer(place, down_out, 1, fsend.at[1], frecv.at[1]),
    ]
    gather_att = [
        Gatherer(place, out_out, 0, asend.at[0], arecv.at[0]),
        Gatherer(place, qkv_out, 1, asend.at[1], arecv.at[1]),
    ]
    own_rows = pl.ds(pl.multiple_of(side * half_len, half_len), half_len)
    other_rows = pl.ds(pl.multiple_of((1 - side) * half_len, half_len), half_len)
    order = [place.across] + place.partners

    send_mixed = remote(mixed_in.at[other_rows, :], mixed_out.at[side], xsend.at[0], xrecv.at[0], place.across)
    keep_mixed = pltpu.make_async_copy(mixed_in.at[own_rows, :], mixed_out.at[side], local.at[0])
    send_dtok = remote(dtok.at[other_rows, :], dtok_out.at[side], xsend.at[1], xrecv.at[1], place.across)
    keep_dtok = pltpu.make_async_copy(dtok.at[own_rows, :], dtok_out.at[side], local.at[1])
    put_ffn = [
        pltpu.make_async_copy(up_in, gather_ffn[0].view(0), local.at[2]),
        pltpu.make_async_copy(down_in, gather_ffn[1].view(0), local.at[3]),
    ]
    put_att = [
        pltpu.make_async_copy(fin_out, gather_att[0].view(0), local.at[4]),
        pltpu.make_async_copy(fin_qkv, gather_att[1].view(0), local.at[5]),
    ]
    put_every = pltpu.make_async_copy(every_ref, every_out, local.at[6])

    def put_final(c, value):
        if c == 0:
            fin_out[...] = value
        else:
            for which in range(3):
                fin_qkv[which, :, (c - 1) * 128 : c * 128] = value[:, which * 128 : which * 128 + 128]

    number = 2 * place.me % 32 + side

    def spread(stage):
        span = every_ref.at[pl.ds(number - number % 2**stage, 2**stage)]
        return remote(span, span, ssend.at[stage], srecv.at[stage], order[stage])

    def gain_copy(stage):
        return remote(gains.at[stage], gains_in.at[stage], gsend.at[stage], grecv.at[stage], order[stage])

    @pl.when(step == 0)
    def _():
        place.greet(place.partners + [place.across])
        for copy in put_ffn:
            copy.start()
        send_mixed.start()
        keep_mixed.start()
        every_ref[pl.ds(number, 1)] = small_ref[...]
        spread(0).start()
        chunks[0] = dwo_ref[...]
        reducer.start(0, 0)
        for copy, gather in zip(put_ffn, gather_ffn):
            copy.wait()
            gather.start(0)
        n_t[...] = n_ref[...].T

    starts = (0, 1, 3, 5)
    for c in range(4):
        for stage in range(Reducer.STAGES):

            @pl.when(step == starts[c] + 1 + stage)
            def _(c=c, stage=stage):
                reducer.finish(stage, c, put_final)
                if stage + 1 < Reducer.STAGES:
                    reducer.start(stage + 1, c)

    for stage, at in enumerate((1, 3, 5, 7)):

        @pl.when(step == at)
        def _(stage=stage):
            for gather in gather_ffn:
                gather.finish(stage)
                if stage + 1 < Gatherer.STAGES:
                    gather.start(stage + 1)

    for stage in range(5):

        @pl.when(step == stage + 1)
        def _(stage=stage):
            spread(stage).wait()
            if stage < 4:
                spread(stage + 1).start()
            else:
                put_every.start()

    @pl.when(step < 6)
    def _():
        pair = step // 2 + 3 * (step % 2)
        lanes = pl.ds(pl.multiple_of(pair * 128, 128), 128)

        def put(which, span, value):
            draw[which, span, lanes] = value

        attend_back(
            q_ref, k_ref, v_ref, o_ref, do_ref, lse_ref, segc_ref, segr_ref, cos_ref, sin_ref, acc, put
        )
        for which in range(3):
            grad = dot_nn(n_t[...], draw[which, :, lanes]).astype(bf16)
            chunks[1 + step // 2, step % 2, :, which * 128 : which * 128 + 128] = grad

    for c in range(1, 4):

        @pl.when(step == starts[c])
        def _(c=c):
            reducer.start(0, c)

    @pl.when(step == 6)
    def _():
        dgain_ref[...] = jnp.zeros_like(dgain_ref)

    @pl.when(jnp.logical_and(step >= 6, step < 6 + blocks))
    def _():
        span = pl.ds(pl.multiple_of((step - 6) * rows, rows), rows)
        dnormed = jnp.zeros((rows, width), f32)
        for which in range(3):
            dnormed = dnormed + dot_nt(draw[which, span, :half], wa_ref[which])
            dnormed = dnormed + dot_nt(draw[which, span, half:], wb_ref[which])
        normed, inverse = norm_parts(x_ref[span, :].astype(f32))
        dgain_ref[0:1, :] += jnp.sum(dnormed * normed, axis=0, keepdims=True)
        dtok[span, :] = (
            dhidden_ref[span, :] + norm_back(dnormed * gain_ref[...], normed, inverse)
        ).astype(bf16)

    @pl.when(step == 6 + blocks)
    def _():
        send_dtok.start()
        keep_dtok.start()
        for copy in put_att:
            copy.start()
        gains[0] = dgain_ref[...]
        gain_copy(0).start()
        for copy in put_att:
            copy.wait()
        for stage in range(5):
            if stage < 4:
                for gather in gather_att:
                    gather.start(stage)
            gain_copy(stage).wait()
            total = gains[stage] + gains_in[stage]
            if stage < 4:
                gains[stage + 1] = total
                gain_copy(stage + 1).start()
                for gather in gather_att:
                    gather.finish(stage)
            else:
                dgain_ref[...] = total
        send_mixed.wait()
        keep_mixed.wait()
        send_dtok.wait()
        keep_dtok.wait()
        put_every.wait()


def back_call(
    q, k, v, o, do, lse, segc, segr, cosine, sine, n, x, gain, dhidden, wa, wb, dwo, small, mixed, ups, downs
):
    length, width = x.shape
    pairs = width // 128
    half = wa.shape[2]
    shape = jax.ShapeDtypeStruct

    def const(a):
        zeros = (0,) * len(a.shape)
        return pl.BlockSpec(a.shape, lambda s: zeros, pipeline_mode=pl.Buffered(1))

    def pair_of(s):
        s = jnp.minimum(s, 5)
        return s // 2 + 3 * (s % 2)

    any_ = pl.BlockSpec(memory_space=pl.ANY)
    major = pl.BlockSpec((1, length, 128), lambda s: (pair_of(s), 0, 0))
    minor = pl.BlockSpec((length, 128), lambda s: (0, pair_of(s)))
    every = shape((32,) + small.shape[1:], f32)
    dgain = shape((8, width), f32)
    up_all = shape((width, ups.shape[1]), bf16)
    down_all = shape((downs.shape[0], 16 * downs.shape[1], width), bf16)
    out_all = shape((width, half), bf16)
    qkv_all = shape(wa.shape, bf16)
    tok = shape((2, length // 2, width), bf16)
    dma = pltpu.SemaphoreType.DMA
    return pl.pallas_call(
        back_kernel,
        grid=(6 + length // 256 + 1,),
        in_specs=[major] * 3
        + [minor] * 2
        + [pl.BlockSpec((1, 8, length), lambda s: (pair_of(s), 0, 0))]
        + [const(a) for a in (segc, segr, cosine, sine, n, x, gain, dhidden, wa, wb, dwo, small)]
        + [any_, const(ups), const(downs)],
        out_specs=[any_] * 7 + [const(dgain)],
        out_shape=[up_all, down_all, out_all, qkv_all, tok, tok, every, dgain],
        scratch_shapes=[
            pltpu.VMEM((width, length), bf16),
            pltpu.VMEM((3, length, width), bf16),
            pltpu.VMEM((128, length), f32),
            pltpu.VMEM((length, width), bf16),
            pltpu.VMEM((width // 16, half), bf16),
            pltpu.VMEM((3, width // 16, half), bf16),
            pltpu.VMEM(every.shape, f32),
            pltpu.VMEM((5, 8, width), f32),
            pltpu.VMEM((5, 8, width), f32),
        ]
        + Reducer.scratch(4, width, half)
        + [dma((2, 4))] * 4
        + [dma((5,))] * 4
        + [dma((2,)), dma((2,)), dma((7,))],
        compiler_params=params(collective_id=2, has_side_effects=True),
        name="back",
    )(q, k, v, o, do, lse, segc, segr, cosine, sine, n, x, gain, dhidden, wa, wb, dwo, small, mixed, ups, downs)


def time_embedding(timestep):
    half = TEMB // 2
    frequency = jnp.exp(-math.log(10000.0) * jnp.arange(half, dtype=f32) / half)
    angles = timestep.astype(f32)[:, None] * frequency[None, :]
    return jnp.concatenate([jnp.cos(angles), jnp.sin(angles)], axis=-1)


def per_device(
    groups, tokens, segment_ids, timestep, ln_gain, w_qkv, w_out, w_up, w_down, ada_weight, ada_bias, cotangent
):
    half, width = tokens.shape[1], tokens.shape[2]
    length = 2 * half
    side = lax.axis_index("tensor")
    pick = lambda a, i: lax.dynamic_index_in_dim(a, i, 0, keepdims=False)

    segments = pick(segment_ids, side)
    segc, segr = segments.reshape(length, 1), segments.reshape(1, length)
    gain = ln_gain.reshape(1, width)
    cosine, sine = (jnp.asarray(a) for a in rotary_np(length))

    embedding = time_embedding(timestep)
    mine = pick(embedding, side)
    mod = jnp.sum(mine[:, None] * ada_weight.astype(f32), axis=0) + ada_bias
    mod = mod.reshape(3, width)

    x, cot, n, q, k, v, o, lse, o_qkv, o_out, o_up, o_down = front_call(
        tokens, cotangent, w_qkv, w_out, w_up, w_down, gain, segc, segr, cosine, sine
    )
    mixed, dhidden, do, dwo, sums, ups, downs = feed_call(
        x, cot, o, w_out, o_out, mod, w_up, o_up, w_down, o_down
    )
    small = jnp.concatenate(
        [sums[:3].reshape(3 * width // 128, 128), mine[None, :], jnp.zeros((5, 128), f32)]
    )[None]
    d_up, d_down, d_out, d_qkv, mixed, dtok, every, dgain = back_call(
        q, k, v, o, do, lse, segc, segr, cosine, sine, n, x, gain, dhidden, w_qkv, o_qkv, dwo, small, mixed, ups, downs
    )
    rows = 3 * width // 128
    d_mods = every[:, :rows].reshape(32, 3 * width)
    d_ada_weight = jnp.dot(every[:, rows].T, d_mods, precision=lax.Precision.HIGHEST)
    d_ada_bias = jnp.sum(d_mods, axis=0)
    d_gain = dgain[0]

    d_up, d_qkv = d_up.astype(f32), d_qkv.astype(f32)
    d_down = d_down.reshape(-1, width).astype(f32)
    heads = d_out.shape[1]
    d_out = jnp.concatenate([d_out[:heads], d_out[heads:]], axis=1).astype(f32)

    def rest(a):
        bit = 16
        while bit < groups:
            a = a + lax.ppermute(a, "dp", [(i, i ^ bit) for i in range(groups)])
            bit *= 2
        return a

    return (
        mixed,
        dtok,
        rest(d_gain),
        rest(d_qkv),
        rest(d_out),
        rest(d_up),
        rest(d_down),
        rest(d_ada_weight),
        rest(d_ada_bias),
    )


def solution(mesh):
    in_specs = (
        P("dp", "tensor", None),
        P("dp", None),
        P("dp"),
        P(),
        P(None, None, "tensor"),
        P("tensor", None),
        P(None, "tensor"),
        P("tensor", None),
        P(),
        P(),
        P("dp", "tensor", None),
    )
    out_specs = (
        P("dp", "tensor", None),
        P("dp", "tensor", None),
        P(),
        P(None, None, "tensor"),
        P("tensor", None),
        P(None, "tensor"),
        P("tensor", None),
        P(),
        P(),
    )
    return jax.shard_map(
        functools.partial(per_device, mesh.shape["dp"]), mesh=mesh, in_specs=in_specs, out_specs=out_specs, check_vma=False
    )
```

```python
import functools
import math

import jax
import jax.numpy as jnp
import numpy as np
from jax import lax
from jax.experimental import pallas as pl
from jax.experimental.pallas import tpu as pltpu
from jax.sharding import PartitionSpec as P

HD = 64
TEMB = 128
EPS = 1e-05
MASKED = -1000000000.0
f32 = jnp.float32
bf16 = jnp.bfloat16
VMEM_LIMIT = 61 * 1024 * 1024


def dot_nn(a, b):
    return lax.dot_general(a, b, (((1,), (0,)), ((), ())), preferred_element_type=f32)


def dot_nt(a, b):
    return lax.dot_general(a, b, (((1,), (1,)), ((), ())), preferred_element_type=f32)


def dot_tn(a, b):
    return lax.dot_general(a, b, (((0,), (0,)), ((), ())), preferred_element_type=f32)


def norm_parts(values):
    centred = values - jnp.mean(values, axis=-1, keepdims=True)
    variance = jnp.mean(centred * centred, axis=-1, keepdims=True)
    inverse = lax.rsqrt(variance + EPS)
    return centred * inverse, inverse


def norm_back(grad, normed, inverse):
    return inverse * (
        grad
        - jnp.mean(grad, axis=-1, keepdims=True)
        - normed * jnp.mean(grad * normed, axis=-1, keepdims=True)
    )


def rotary_np(length):
    half = HD // 2
    position = np.arange(length, dtype=np.float32)
    frequency = (10000.0 ** (-np.arange(half, dtype=np.float32) / half)).astype(np.float32)
    angles = position[:, None] * frequency[None, :]
    cosine, sine = np.cos(angles), np.sin(angles)
    cosine = np.concatenate([cosine, cosine] * 2, axis=1).astype(np.float32)
    sine = np.concatenate([-sine, sine] * 2, axis=1).astype(np.float32)
    return cosine, sine


def swap_halves(values):
    lane = lax.broadcasted_iota(jnp.int32, values.shape, 1)
    first = (lane % HD) < (HD // 2)
    return jnp.where(first, pltpu.roll(values, 128 - HD // 2, 1), pltpu.roll(values, HD // 2, 1))


def params(**kw):
    return pltpu.CompilerParams(vmem_limit_bytes=VMEM_LIMIT, **kw)


def cost(flops, nbytes, trans=0):
    return pl.CostEstimate(flops=int(flops), bytes_accessed=int(nbytes), transcendentals=int(trans))


BITS = {"core": 1, "y": 2, "zl": 4, "zh": 8}
MESH = pl.DeviceIdType.MESH


class Place:
    def __init__(self):
        self.me = lax.axis_index("dp")
        self.side = lax.axis_index("tensor")
        self.bit = {axis: (self.me // bit) % 2 for axis, bit in BITS.items()}
        self.partner = {
            axis: {"dp": self.me + bit * (1 - 2 * self.bit[axis])} for axis, bit in BITS.items()
        }
        self.partner["x"] = {"tensor": 1 - self.side}

    def greet(self, axes):
        barrier = pltpu.get_barrier_semaphore()
        for axis in axes:
            pl.semaphore_signal(barrier, inc=1, device_id=self.partner[axis], device_id_type=MESH)
        pl.semaphore_wait(barrier, len(axes))


ALL_AXES = ("core", "y", "zl", "zh", "x")


def remote(src, dst, send, recv, partner):
    return pltpu.make_async_remote_copy(
        src_ref=src, dst_ref=dst, send_sem=send, recv_sem=recv, device_id=partner, device_id_type=MESH
    )


class Reducer:
    STAGES = 5

    def __init__(self, place, view, rows, refs, order):
        self.place, self.view, self.order = place, view, order
        self.received, self.sends, self.recvs = refs[:5], refs[5], refs[6]
        self.cross = order.index("x")
        base, n = 0, rows
        self.spans = []
        for axis in order:
            if axis == "x":
                span = pl.ds(pl.multiple_of(base, 16), n)
                self.spans.append((span, span))
            else:
                n //= 2
                bit = place.bit[axis]
                keep = pl.ds(pl.multiple_of(base + bit * n, 16), n)
                send = pl.ds(pl.multiple_of(base + (1 - bit) * n, 16), n)
                self.spans.append((keep, send))
                base = base + bit * n

    @staticmethod
    def scratch(count, slots, rows, cols, order):
        shapes, n, cross = [], rows, False
        for slots, axis in zip(slots, order):
            if axis == "x":
                cross = True
            else:
                n //= 2
            shapes.append((slots, n, cols) if cross else (slots, 2, n, cols))
        return [pltpu.VMEM(shape, bf16) for shape in shapes] + [pltpu.SemaphoreType.DMA((count, 5))] * 2

    def slot(self, stage, c):
        return self.received[stage].at[c % self.received[stage].shape[0]]

    def copy(self, stage, c):
        send = self.spans[stage][1]
        if stage < self.cross:
            source = self.view(c).at[:, send, :]
        else:
            source = self.view(c).at[1 if stage == self.cross else 0, send, :]
        return remote(
            source,
            self.slot(stage, c),
            self.sends.at[c, stage],
            self.recvs.at[c, stage],
            self.place.partner[self.order[stage]],
        )

    def start(self, stage, c):
        self.copy(stage, c).start()

    def finish(self, stage, c, put=None):
        self.copy(stage, c).wait()
        keep = self.spans[stage][0]
        came, chunk = self.slot(stage, c), self.view(c)
        if stage < self.cross:
            for half in range(2):
                chunk[half, keep, :] += came[half]
        elif stage < 4:
            chunk[0, keep, :] += came[...]
        else:
            put(c, chunk[0, keep, :] + came[...])

    def step(self, stage, c, put=None):
        self.finish(stage, c, put)
        if stage + 1 < self.STAGES:
            self.start(stage + 1, c)


class Gatherer:
    STAGES = 4

    def __init__(self, place, view, rows, order, sends, recvs):
        self.place, self.view, self.sends, self.recvs = place, view, sends, recvs
        self.order = [axis for axis in order if axis != "x"][::-1]
        self.size = rows // 16
        bits = [place.bit[axis] for axis in self.order]
        self.bases = [sum(bits[j] * 2**j for j in range(stage, 4)) for stage in range(4)]

    def span(self, stage):
        n = self.size
        return self.view(pl.ds(pl.multiple_of(self.bases[stage] * n, 16), 2**stage * n))

    def copy(self, stage):
        span = self.span(stage)
        return remote(
            span, span, self.sends.at[stage], self.recvs.at[stage], self.place.partner[self.order[stage]]
        )

    def start(self, stage):
        self.copy(stage).start()

    def finish(self, stage):
        self.copy(stage).wait()


class Fetch:
    def __init__(self, place, own, other, rows, axes, sends, recvs):
        self.place, self.own, self.other, self.axes = place, own, other, axes
        self.sends, self.recvs = sends, recvs
        self.size = rows // 2 ** len(axes)
        bits = [place.bit[axis] for axis in axes]
        self.bases = [sum(bits[j] * 2**j for j in range(s, len(axes))) for s in range(len(axes))]

    def copy(self, stage):
        level = max(stage - 1, 0)
        n = self.size
        span = pl.ds(pl.multiple_of(self.bases[level] * n, 16), 2**level * n)
        source = self.own(span) if stage == 0 else self.other(span)
        axis = "x" if stage == 0 else self.axes[stage - 1]
        return remote(
            source, self.other(span), self.sends.at[stage], self.recvs.at[stage], self.place.partner[axis]
        )

    def start(self, stage):
        self.copy(stage).start()

    def step(self, stage):
        self.copy(stage).wait()
        if stage < len(self.axes):
            self.copy(stage + 1).start()


def qkv_rows(row, rows, x_ref, gain_ref, w_ref, cos_ref, sin_ref, n_ref, q_ref, k_ref, v_ref, first):
    span = pl.ds(row, rows)
    pairs = w_ref.shape[2] // 128
    if n_ref is None:
        normed = x_ref[span, :]
    else:
        normed, _ = norm_parts(x_ref[span, :].astype(f32))
        normed = (normed * gain_ref[...]).astype(bf16)
        n_ref[span, :] = normed
    cosine, sine = cos_ref[span, :], sin_ref[span, :]
    for which, out in ((0, q_ref), (1, k_ref)):
        raw = dot_nn(normed, w_ref[which])
        for pair in range(pairs):
            part = raw[:, pair * 128 : pair * 128 + 128]
            turned = (part * cosine + swap_halves(part) * sine).astype(bf16)
            if which == 0:
                turned = turned * jnp.asarray(0.125, bf16)
            out[first + pair, span, :] = turned
    raw = dot_nn(normed, w_ref[2]).astype(bf16)
    for pair in range(pairs):
        v_ref[first + pair, span, :] = raw[:, pair * 128 : pair * 128 + 128]


def attend_rows(pair, row, rows, q_ref, k_ref, v_ref, segc_ref, segr_ref, o_ref, lse_ref):
    lane = lax.broadcasted_iota(jnp.int32, (1, 128), 1)
    low = lane < HD
    span = pl.ds(row, rows)
    q, k, v = q_ref[pair, span, :], k_ref[pair], v_ref[pair]
    column = segc_ref[span, :]
    mask = jnp.concatenate([column] * (k.shape[0] // 128), axis=1) == segr_ref[...]
    parts = []
    for head in range(2):
        mine = low if head == 0 else jnp.logical_not(low)
        scores = dot_nt(jnp.where(mine, q, jnp.zeros_like(q)), k)
        scores = jnp.where(mask, scores, MASKED)
        largest = jnp.max(scores, axis=1, keepdims=True)
        weights = jnp.exp(scores - largest).astype(bf16)
        mixed = dot_nn(weights, jnp.where(mine, v, jnp.ones_like(v)))
        total = pltpu.roll(mixed, HD, 1)
        parts.append((mixed / total, largest + jnp.log(total)))
    o_ref[span, pl.ds(pl.multiple_of(pair * 128, 128), 128)] = jnp.where(
        low, parts[0][0], parts[1][0]
    ).astype(bf16)
    lse = jnp.where(low, parts[0][1], parts[1][1]).T
    lse_ref[pair, 0:1, span] = lse[0:1, :]
    lse_ref[pair, 1:2, span] = lse[HD : HD + 1, :]


def gelu_both(u):
    c0 = math.sqrt(2.0 / math.pi)
    square = u * u
    t = jnp.tanh(u * (c0 + (c0 * 0.044715) * square))
    half = 0.5 + 0.5 * t
    act = u * half
    slope = half + (0.5 * u) * (1.0 - t * t) * (c0 + (3.0 * c0 * 0.044715) * square)
    return act, slope


FEED_STEPS = 6
UP_ORDER = ("core", "y", "zl", "x", "zh")
DOWN_ORDER = ("core", "x", "zl", "y", "zh")
QKV_ORDERS = (
    ("core", "y", "x", "zl", "zh"),
    ("core", "x", "y", "zl", "zh"),
    ("core", "zl", "x", "y", "zh"),
)


def attend_back(
    pair, q_ref, k_ref, v_ref, o_ref, do_ref, lse_ref, segc_ref, segr, cos_ref, sin_ref, acc_ref, poll
):
    length = o_ref.shape[0]
    rows = 256
    lane = lax.broadcasted_iota(jnp.int32, (1, 128), 1)
    low = lane < HD
    lanes = pl.ds(pl.multiple_of(pair * 128, 128), 128)
    q, do = q_ref[pair], do_ref[:, lanes]
    product = do.astype(f32) * o_ref[:, lanes].astype(f32)
    high_part = product.astype(bf16)
    low_part = (product - high_part.astype(f32)).astype(bf16)
    row8 = lax.broadcasted_iota(jnp.int32, (8, 128), 0)
    lane8 = lax.broadcasted_iota(jnp.int32, (8, 128), 1)
    select = jnp.where((lane8 // HD) == row8, 1.0, 0.0).astype(bf16)
    delta = dot_nt(select, high_part) + dot_nt(select, low_part)
    lse = lse_ref[pair]
    zero = jnp.zeros_like(q)
    q_heads = (jnp.where(low, q, zero), jnp.where(low, zero, q))
    do_heads = (jnp.where(low, do, zero), jnp.where(low, zero, do))
    acc_ref[...] = jnp.zeros_like(acc_ref)
    for block in range(length // rows):
        if block == 2:
            poll()
        span = pl.ds(block * rows, rows)
        k, v = k_ref[pair, span, :], v_ref[pair, span, :]
        mask = jnp.concatenate([segc_ref[span, :]] * (length // 128), axis=1) == segr
        dv = jnp.zeros((rows, 128), f32)
        dk = jnp.zeros((rows, 128), f32)
        dq = jnp.zeros((128, length), f32)
        for head in range(2):
            mine = low if head == 0 else jnp.logical_not(low)
            kh = jnp.where(mine, k, jnp.zeros_like(k))
            vh = jnp.where(mine, v, jnp.zeros_like(v))
            scores = jnp.where(mask, dot_nt(kh, q), MASKED)
            probs = jnp.exp(scores - lse[head : head + 1, :])
            dv = dv + dot_nn(probs.astype(bf16), do_heads[head])
            d_probs = dot_nt(vh, do)
            d_scores = (probs * (d_probs - delta[head : head + 1, :])).astype(bf16)
            dk = dk + dot_nn(d_scores, q_heads[head])
            dq = dq + dot_tn(kh, d_scores)
        acc_ref[...] += dq
        cosine, sine = cos_ref[span, :], sin_ref[span, :]
        k_ref[pair, span, :] = (dk * cosine - swap_halves(dk) * sine).astype(bf16)
        v_ref[pair, span, :] = dv.astype(bf16)
    dq = acc_ref[...].T * 0.125
    q_ref[pair] = (dq * cos_ref[...] - swap_halves(dq) * sin_ref[...]).astype(bf16)


SPREAD_ORDER = ("x", "core", "y", "zl", "zh")


def layer_kernel(
    tok, cot_in, wq, wo, wu, wd, gain_ref, seg_ref, cos_ref, sin_ref, emb_ref, ada_ref, bias_ref,
    oq, oo, ou, od, up_out, down_out, out_out, qkv_out, mixed_out, dtok_out, dada_out, dbias_ref, dgain_ref,
    xs, ns, qs, ks, vs, os, ls, segc, wqs, wos, cot, mod,
    hidden, modul, modul_t, dbranch, branch, dmod, acts, dups, upbuf, downbuf, acc,
    ups, downs, fin_up, fin_down, fin_out, fin_qkv, every, gains, gains_in,
    local, xsend, xrecv, wsend, wrecv, loads,
    fsend, frecv, asend, arecv, gsend, grecv, ssend, srecv, *reducing,
):
    place = Place()
    side = place.side
    length, width = xs.shape
    half = length // 2
    rows = 256
    blocks = length // rows
    block = wu.shape[1] // FEED_STEPS
    heads = wo.shape[0]
    hid = wu.shape[1]
    tiles = 3 * width // 128
    own_rows = pl.ds(pl.multiple_of(side * half, half), half)
    other_rows = pl.ds(pl.multiple_of((1 - side) * half, half), half)

    def copy_here(src, dst, index):
        copy = pltpu.make_async_copy(src, dst, local.at[index])
        copy.start()
        return copy

    place.greet(ALL_AXES)
    send_tok = remote(tok.at[1 - side], xs.at[own_rows, :], xsend.at[0], xrecv.at[0], place.partner["x"])
    send_cot = remote(cot_in.at[1 - side], cot.at[own_rows, :], xsend.at[1], xrecv.at[1], place.partner["x"])

    def up_view(g):
        return lambda r, s: r.at[s, pl.ds(g * hid // 3, hid // 3)]

    def down_view(g):
        return lambda r, s: r.at[pl.ds(g * hid // 3, hid // 3)].at[s, :]

    plan = (
        (lambda r, s: r.at[2, s, :], wq, oq, width, ("y", "zl", "core")),
        (lambda r, s: r.at[0, s, :], wq, oq, width, ("y", "core")),
        (lambda r, s: r.at[1, s, :], wq, oq, width, ("zl", "core")),
        (lambda r, s: r.at[s, :], wo, oo, heads, ("y", "core")),
        (up_view(0), wu, ou, width, ("y", "zl", "core")),
        (down_view(0), wd, od, hid // 3, ("zl", "y", "core")),
        (up_view(1), wu, ou, width, ("y", "zl", "core")),
        (down_view(1), wd, od, hid // 3, ("zl", "y", "core")),
        (up_view(2), wu, ou, width, ("y", "zl", "core")),
        (down_view(2), wd, od, hid // 3, ("zl", "y", "core")),
    )
    V, Q, K, OUT, UP0, DN0, UP1, DN1, UP2, DN2 = range(10)
    fetches = [
        Fetch(place, functools.partial(view, own), functools.partial(view, other), n, axes, wsend.at[i], wrecv.at[i])
        for i, (view, own, other, n, axes) in enumerate(plan)
    ]
    send_tok.start()
    for index in (V, Q, K, UP0, DN0, OUT):
        fetches[index].start(0)
    send_cot.start()
    for index in (UP1, DN1, UP2, DN2):
        fetches[index].start(0)

    get_x = copy_here(tok.at[side], xs.at[own_rows, :], 0)
    get_w = copy_here(wq, wqs.at[0], 1)
    get_cot = copy_here(cot_in.at[side], cot.at[own_rows, :], 2)
    get_wo = copy_here(wo, wos.at[pl.ds(0, heads), :], 3)

    segr = seg_ref[pl.ds(side, 1), :].astype(f32)
    segc[...] = jnp.broadcast_to(segr, (128, length)).T
    emb = jnp.broadcast_to(emb_ref[pl.ds(side, 1), :], (TEMB, TEMB)).T
    for tile in range(tiles):
        span = slice(tile * 128, tile * 128 + 128)
        value = jnp.sum(emb * ada_ref[:, span].astype(f32), axis=0, keepdims=True) + bias_ref[:, span]
        start = tile * 128 % width
        mod[tile * 128 // width : tile * 128 // width + 1, start : start + 128] = value
    get_x.wait()
    get_w.wait()

    def qkv_half(base, w_ref, w_first, n_ref):
        def step(i, carry):
            row = pl.multiple_of(base + i * rows, rows)
            qkv_rows(
                row, rows, xs if n_ref is not None else ns, gain_ref, w_ref, cos_ref, sin_ref,
                n_ref, qs, ks, vs, w_first,
            )
            return carry

        lax.fori_loop(0, half // rows, step, 0)

    qkv_half(side * half, wqs.at[0], 0, ns)
    send_tok.wait()
    qkv_half((1 - side) * half, wqs.at[0], 0, ns)

    per_pair = 2
    steps = 6 * per_pair
    events = {
        0: ((V, 0),),
        1: ((Q, 0),),
        2: ((V, 1), (K, 0)),
        4: ((Q, 1), (UP0, 0)),
        5: ((V, 2), (K, 1), (DN0, 0)),
        7: ((UP0, 1), (OUT, 0)),
        8: ((DN0, 1),),
        10: ((UP0, 2), (OUT, 1)),
        11: ((DN0, 2),),
    }

    def attend(step, carry):
        pair = step // per_pair

        @pl.when(step == steps // 2)
        def _():
            for index in (V, Q, K):
                fetches[index].step(len(fetches[index].axes))
            copy = copy_here(oq, wqs.at[1], 1)
            copy.wait()
            qkv_half(0, wqs.at[1], 3, None)
            qkv_half(half, wqs.at[1], 3, None)

        for at, moves in events.items():

            @pl.when(step == at)
            def _(moves=moves):
                for index, stage in moves:
                    fetches[index].step(stage)

        for b in range(blocks // per_pair):
            row = pl.multiple_of((step % per_pair) * (length // per_pair) + b * rows, rows)
            attend_rows(pair, row, rows, qs, ks, vs, segc, segr, os, ls)
        return carry

    lax.fori_loop(0, steps, attend, 0)

    def load_weights(step):
        slot = step % 2
        span = pl.ds(pl.multiple_of(step * block, 128), block)
        return [
            pltpu.make_async_copy(wu.at[:, span], upbuf.at[slot, :, pl.ds(0, block)], loads.at[slot, 0]),
            pltpu.make_async_copy(ou.at[:, span], upbuf.at[slot, :, pl.ds(block, block)], loads.at[slot, 1]),
            pltpu.make_async_copy(wd.at[span, :], downbuf.at[slot, pl.ds(0, block), :], loads.at[slot, 2]),
            pltpu.make_async_copy(od.at[span, :], downbuf.at[slot, pl.ds(block, block), :], loads.at[slot, 3]),
        ]

    fetches[OUT].step(2)
    get_wo.wait()
    copy_here(oo, wos.at[pl.ds(heads, heads), :], 3).wait()
    get_cot.wait()
    send_cot.wait()
    fetches[UP0].step(3)
    fetches[DN0].step(3)
    for copy in load_weights(0):
        copy.start()
    fetches[UP1].step(0)
    fetches[DN1].step(0)

    def middle(i, carry):
        span = pl.ds(pl.multiple_of(i * rows, rows), rows)
        shift, scale, gate = mod[0:1, :], mod[1:2, :], mod[2:3, :]
        h = xs[span, :].astype(f32) + dot_nn(os[span, :], wos[...])
        hidden[span, :] = h
        normed, _ = norm_parts(h)
        m = (normed * (1.0 + scale) + shift).astype(bf16)
        modul[span, :] = m
        modul_t[:, span] = m.T
        dbranch[span, :] = (cot[span, :].astype(f32) * gate).astype(bf16)
        branch[span, :] = jnp.zeros((rows, width), f32)
        dmod[span, :] = jnp.zeros((rows, width), f32)
        return carry

    lax.fori_loop(0, blocks, middle, 0)

    def track(c, t):
        index = 3 * c + t
        return ups.at[index // 2, :, :, pl.ds(pl.multiple_of((index % 2) * 128, 128), 128)]

    feeders = [
        Reducer(place, lambda c: ups.at[c], width, reducing[0:7], UP_ORDER),
        Reducer(place, lambda c: downs.at[c], block, reducing[7:14], DOWN_ORDER),
    ]
    movers = [
        Reducer(
            place, functools.partial(track, t=t), width, reducing[14 + 7 * t : 21 + 7 * t], QKV_ORDERS[t]
        )
        for t in range(3)
    ]

    def put_up(c, value):
        fin_up[:, pl.ds(pl.multiple_of(c * block, 128), block)] = value

    def put_down(c, value):
        fin_down[c] = value

    def feed_event(stage, c):
        for reducer, put in zip(feeders, (put_up, put_down)):
            reducer.step(stage, c, put)

    def put_final(t):
        def put(c, value):
            if c == 0:
                fin_out[t] = value
            else:
                fin_qkv[c - 1, t] = value

        return put

    def move_event(stage, c):
        for t, reducer in enumerate(movers):
            reducer.step(stage, c, put_final(t))

    FIRST = (3, 6, 8, 10, 12)

    def feed_polls(t, stages):
        for stage in stages:
            since = t - FIRST[stage]

            @pl.when(jnp.logical_and(since >= 0, since < 2 * FEED_STEPS))
            def _(stage=stage, c=since // 2):
                feed_event(stage, c)

    def feed(step, carry):
        feed_polls(2 * step, (4, 3, 2, 1))

        @pl.when(step == 1)
        def _():
            for index in (UP1, DN1):
                fetches[index].step(2)
                fetches[index].step(3)
            for index in (UP2, DN2):
                fetches[index].step(1)

        @pl.when(step == 3)
        def _():
            for index in (UP2, DN2):
                fetches[index].step(3)

        for copy in load_weights(step):
            copy.wait()

        @pl.when(step + 1 < FEED_STEPS)
        def _():
            for copy in load_weights(step + 1):
                copy.start()

        slot = step % 2
        up, down = upbuf.at[slot], downbuf.at[slot]
        for i in range(blocks):
            span = pl.ds(i * rows, rows)
            u = dot_nn(modul[span, :], up[...])
            act, slope = gelu_both(u)
            act = act.astype(bf16)
            acts[span, :] = act
            d_act = dot_nt(dbranch[span, :], down[...])
            d_up = (d_act * slope).astype(bf16)
            dups[span, :] = d_up
            branch[span, :] += dot_nn(act, down[...])
            dmod[span, :] += dot_nt(d_up, up[...])
        feed_polls(2 * step + 1, (0,))

        @pl.when(step == 0)
        def _():
            for index in (UP1, DN1):
                fetches[index].step(1)
            for index in (UP2, DN2):
                fetches[index].step(0)

        @pl.when(step == 2)
        def _():
            for index in (UP2, DN2):
                fetches[index].step(2)

        grad = dot_nn(modul_t[...], dups[...]).astype(bf16)
        ups[step, 0] = grad[:, :block]
        ups[step, 1] = grad[:, block:]
        feeders[0].start(0, step)
        grad = dot_tn(acts[...], dbranch[...]).astype(bf16)
        downs[step, 0] = grad[:block]
        downs[step, 1] = grad[block:]
        feeders[1].start(0, step)
        return carry

    lax.fori_loop(0, FEED_STEPS, feed, 0)

    feed_schedule = {}
    for c in range(FEED_STEPS):
        for stage in range(Reducer.STAGES):
            feed_schedule.setdefault(2 * c + FIRST[stage], []).append((stage, c))

    def feed_static(t):
        for stage, c in feed_schedule.get(t, []):
            feed_event(stage, c)

    sums = dgain_ref
    sums[...] = jnp.zeros_like(sums)
    for i in range(blocks):
        feed_static(2 * FEED_STEPS + i)
        span = pl.ds(i * rows, rows)
        scale, gate = mod[1:2, :], mod[2:3, :]
        h = hidden[span, :]
        dout = cot[span, :].astype(f32)
        br = branch[span, :]
        cot[span, :] = (h + gate * br).astype(bf16)
        normed, inverse = norm_parts(h)
        dm = dmod[span, :]
        sums[0:1, :] += jnp.sum(dm, axis=0, keepdims=True)
        sums[1:2, :] += jnp.sum(dm * normed, axis=0, keepdims=True)
        sums[2:3, :] += jnp.sum(dout * br, axis=0, keepdims=True)
        dh = dout + norm_back(dm * (1.0 + scale), normed, inverse)
        hidden[span, :] = dh
        dattn = dh.astype(bf16)
        modul[span, :] = dattn
        dbranch[span, :] = dot_nt(dattn, wos[...]).astype(bf16)
    grad = dot_tn(os[...], modul[...]).astype(bf16)
    for t in range(3):
        chunk = track(0, t)
        for i in range(2):
            part = grad[i * heads : (i + 1) * heads]
            chunk[i, :heads, :] = part[:, t * 128 : t * 128 + 128]
            chunk[i, heads:, :] = part[:, heads + t * 128 : heads + t * 128 + 128]
        movers[t].start(0, 0)
    feed_static(16)

    number = 2 * place.me % 32 + side
    every[pl.ds(number, 1)] = jnp.zeros((1,) + every.shape[1:], f32)
    for tile in range(tiles):
        line, lane = tile * 128 // width, tile * 128 % width
        every[pl.ds(number, 1), tile : tile + 1, :] = sums[line : line + 1, lane : lane + 128][None]
    every[pl.ds(number, 1), tiles : tiles + 1, :] = emb_ref[pl.ds(side, 1), :][None]

    def spread(stage):
        span = every.at[pl.ds(number - number % 2**stage, 2**stage)]
        return remote(span, span, ssend.at[stage], srecv.at[stage], place.partner[SPREAD_ORDER[stage]])

    spread(0).start()

    def send_mixed(i):
        n = half // 4
        span = pl.ds(pl.multiple_of((1 - side) * half + i * n, n), n)
        return remote(
            cot.at[span, :], mixed_out.at[side, pl.ds(i * n, n), :],
            xsend.at[2 + i], xrecv.at[2 + i], place.partner["x"],
        )

    keep_mixed = copy_here(cot.at[own_rows, :], mixed_out.at[side], 4)
    modul_t[...] = ns[...].T

    def gather_ffn(g):
        cols = hid // 2
        return [
            Gatherer(
                place, lambda s: up_out.at[s, pl.ds(g * cols, cols)], width, UP_ORDER, fsend.at[g, 0], frecv.at[g, 0]
            ),
            Gatherer(
                place, lambda s: down_out.at[pl.ds(3 * g, 3), s, :], block, DOWN_ORDER, fsend.at[g, 1], frecv.at[g, 1]
            ),
        ]

    def gather_qkv(t, first, count):
        lanes = pl.ds((first - 1) * 128, count * 128)
        return Gatherer(
            place, lambda s: qkv_out.at[t, s, lanes], width, QKV_ORDERS[t],
            asend.at[first - 1, t], arecv.at[first - 1, t],
        )

    def gather_out(t):
        lanes = pl.ds(t * 128, 128)
        return Gatherer(
            place, lambda s: out_out.at[s, lanes], width, QKV_ORDERS[t], asend.at[3, t], arecv.at[3, t]
        )

    def put_pieces(gathers, sources):
        copies = [
            pltpu.make_async_copy(source, gather.span(0), local.at[8 + i])
            for i, (gather, source) in enumerate(zip(gathers, sources))
        ]
        for copy in copies:
            copy.start()
        for copy in copies:
            copy.wait()

    def gather_event(gathers, stage):
        for gather in gathers:
            if stage >= 0:
                gather.finish(stage)
            if stage + 1 < Gatherer.STAGES:
                gather.start(stage + 1)

    ffn = [gather_ffn(0), gather_ffn(1)]

    def start_ffn(g):
        cols = hid // 2
        put_pieces(ffn[g], [fin_up.at[:, pl.ds(g * cols, cols)], fin_down.at[pl.ds(3 * g, 3)]])
        gather_event(ffn[g], -1)

    back_events = {}

    def at(t, event, *operands):
        back_events.setdefault(t, []).append(functools.partial(event, *operands))

    for t, moves in feed_schedule.items():
        for stage, c in moves:
            if t > 16:
                at(t, feed_event, stage, c)
    for stage in range(5):
        at(17 + 2 * stage, move_event, stage, 0)
    at(17, start_ffn, 0)
    for stage, t in enumerate((20, 22, 25, 27)):
        at(t, gather_event, ffn[0], stage)
    at(22, start_ffn, 1)
    for stage, t in enumerate((25, 27)):
        at(t, gather_event, ffn[1], stage)
    for c in (1, 2):
        for stage in range(5):
            if 18 + 4 * c + 2 * stage < 29:
                at(18 + 4 * c + 2 * stage, move_event, stage, c)

    def spread_event(stage):
        spread(stage).wait()
        if stage < 4:
            spread(stage + 1).start()

    for stage in range(5):
        at(18 + 2 * stage, spread_event, stage)
    for i in range(4):
        at(18 + 2 * i, lambda i: send_mixed(i).start(), i)

    def back_polls(step, which):
        for t, moves in back_events.items():
            if t >= 17 and (t - 17) % 2 == which:

                @pl.when(step == (t - 17) // 2)
                def _(moves=moves):
                    for move in moves:
                        move()

    def back(step, carry):
        pair = step // 2 + 3 * (step % 2)
        back_polls(step, 0)
        attend_back(
            pair, qs, ks, vs, os, dbranch, ls, segc, segr, cos_ref, sin_ref, acc,
            lambda: back_polls(step, 1),
        )
        for t, ref in enumerate((qs, ks, vs)):
            grad = dot_nn(modul_t[...], ref[pair]).astype(bf16)
            track(1 + step // 2, t)[step % 2] = grad

        @pl.when(step % 2 == 1)
        def _():
            for reducer in movers:
                reducer.start(0, 1 + step // 2)

        return carry

    lax.fori_loop(0, 6, back, 0)

    def gain_copy(stage):
        return remote(
            gains.at[stage], gains_in.at[stage], gsend.at[stage], grecv.at[stage],
            place.partner[ALL_AXES[stage]],
        )

    send_dtok = remote(modul.at[other_rows, :], dtok_out.at[side], xsend.at[6], xrecv.at[6], place.partner["x"])
    early = [gather_out(t) for t in range(3)] + [gather_qkv(t, 1, 1) for t in range(3)]
    late = [gather_qkv(t, 2, 2) for t in range(3)]

    def last_rows(i):
        b = ((1 - side) * (blocks // 2) + i) % blocks
        span = pl.ds(pl.multiple_of(b * rows, rows), rows)
        dnormed = jnp.zeros((rows, width), f32)
        for which, ref in enumerate((qs, ks, vs)):
            for group in range(2):
                grad = jnp.concatenate([ref[3 * group + p, span, :] for p in range(3)], axis=1)
                dnormed = dnormed + dot_nt(grad, wqs[group, which])
        normed, inverse = norm_parts(xs[span, :].astype(f32))
        gains[0, 0:1, :] += jnp.sum(dnormed * normed, axis=0, keepdims=True)
        modul[span, :] = (
            hidden[span, :] + norm_back(dnormed * gain_ref[...], normed, inverse)
        ).astype(bf16)

    gains[0] = jnp.zeros(gains.shape[1:], f32)
    last_rows(0)
    move_event(0, 3)
    move_event(4, 1)
    move_event(2, 2)
    put_pieces(early, [fin_out.at[t] for t in range(3)] + [fin_qkv.at[0, t] for t in range(3)])
    gather_event(early, -1)
    last_rows(1)
    gather_event(ffn[1], 2)
    move_event(1, 3)
    move_event(3, 2)
    last_rows(2)
    send_dtok.start()
    gather_event(early, 0)
    last_rows(3)
    gain_copy(0).start()
    keep_dtok = copy_here(modul.at[own_rows, :], dtok_out.at[side], 5)
    move_event(4, 2)
    move_event(2, 3)
    gather_event(early, 1)
    put_pieces([gather_qkv(t, 2, 1) for t in range(3)], [fin_qkv.at[1, t] for t in range(3)])
    embeddings = every[:, tiles, :]
    for tile in range(tiles):
        part = every[:, tile, :]
        lane = slice(tile * 128, tile * 128 + 128)
        line, start = tile * 128 // width, tile * 128 % width
        branch[line * TEMB : (line + 1) * TEMB, start : start + 128] = lax.dot_general(
            embeddings, part, (((0,), (0,)), ((), ())),
            preferred_element_type=f32, precision=lax.Precision.HIGHEST,
        )
        dbias_ref[0:1, lane] = jnp.sum(part, axis=0, keepdims=True)
    put_dada = copy_here(branch.at[pl.ds(0, 3 * TEMB), :], dada_out, 6)
    move_event(3, 3)
    gather_event(early, 2)
    gather_event(ffn[1], 3)
    move_event(4, 3)
    put_pieces([gather_qkv(t, 3, 1) for t in range(3)], [fin_qkv.at[2, t] for t in range(3)])
    gather_event(late, -1)
    gather_event(early, 3)
    for stage in range(5):
        gain_copy(stage).wait()
        total = gains[stage] + gains_in[stage]
        if stage < 4:
            gains[stage + 1] = total
            gain_copy(stage + 1).start()
            gather_event(late, stage)
        else:
            dgain_ref[...] = total
    for i in range(4):
        send_mixed(i).wait()
    keep_mixed.wait()
    send_dtok.wait()
    keep_dtok.wait()
    put_dada.wait()


def layer_call(tokens, cot, wq, wo, wu, wd, gain, segments, cosine, sine, embedding, ada, bias):
    length, width = 2 * tokens.shape[1], tokens.shape[2]
    half, hid = wq.shape[2], wu.shape[1]
    block = hid // FEED_STEPS
    pairs = width // 128
    any_ = pl.BlockSpec(memory_space=pl.ANY)
    vm = pl.BlockSpec(memory_space=pltpu.VMEM)
    shape = jax.ShapeDtypeStruct
    dma = pltpu.SemaphoreType.DMA
    low = lambda *dims: pltpu.VMEM(dims, bf16)
    full = lambda *dims: pltpu.VMEM(dims, f32)
    slots = (2, 4, 2, 2, 2)
    reducing = Reducer.scratch(FEED_STEPS, slots, width, block, UP_ORDER)
    reducing += Reducer.scratch(FEED_STEPS, slots, block, width, DOWN_ORDER)
    for order in QKV_ORDERS:
        reducing += Reducer.scratch(4, (2, 4, 4, 4, 4), width, 128, order)
    return pl.pallas_call(
        layer_kernel,
        in_specs=[any_] * 6 + [vm] * 7,
        out_specs=[any_] * 11 + [vm] * 2,
        out_shape=[
            shape(wq.shape, bf16),
            shape(wo.shape, bf16),
            shape(wu.shape, bf16),
            shape(wd.shape, bf16),
            shape((width, hid), bf16),
            shape((FEED_STEPS, block, width), bf16),
            shape((width, half), bf16),
            shape(wq.shape, bf16),
            shape((2, length // 2, width), bf16),
            shape((2, length // 2, width), bf16),
            shape((3 * TEMB, width), f32),
            shape((8, 3 * width), f32),
            shape((8, width), f32),
        ],
        scratch_shapes=[
            low(length, width),
            low(length, width),
            low(pairs, length, 128),
            low(pairs, length, 128),
            low(pairs, length, 128),
            low(length, width),
            full(pairs, 8, length),
            full(length, 128),
            low(2, *wq.shape),
            low(width, width),
            low(length, width),
            full(8, width),
            full(length, width),
            low(length, width),
            low(width, length),
            low(length, width),
            full(length, width),
            full(length, width),
            low(length, 2 * block),
            low(length, 2 * block),
            low(2, width, 2 * block),
            low(2, 2 * block, width),
            full(128, length),
            low(FEED_STEPS, 2, width, block),
            low(FEED_STEPS, 2, block, width),
            low(width // 16, hid),
            low(FEED_STEPS, block // 16, width),
            low(3, width // 16, 128),
            low(3, 3, width // 16, 128),
            full(32, 24, 128),
            full(5, 8, width),
            full(5, 8, width),
            dma((14,)),
            dma((7,)),
            dma((7,)),
            dma((10, 4)),
            dma((10, 4)),
            dma((2, 4)),
            dma((2, 2, 4)),
            dma((2, 2, 4)),
            dma((4, 3, 4)),
            dma((4, 3, 4)),
            dma((5,)),
            dma((5,)),
            dma((5,)),
            dma((5,)),
        ]
        + reducing,
        compiler_params=params(collective_id=0, has_side_effects=True),
        name="layer",
    )(tokens, cot, wq, wo, wu, wd, gain, segments, cosine, sine, embedding, ada, bias)


def time_embedding(timestep):
    half = TEMB // 2
    frequency = jnp.exp(-math.log(10000.0) * jnp.arange(half, dtype=f32) / half)
    angles = timestep.astype(f32)[:, None] * frequency[None, :]
    return jnp.concatenate([jnp.cos(angles), jnp.sin(angles)], axis=-1)


def per_device(
    groups, tokens, segment_ids, timestep, ln_gain, w_qkv, w_out, w_up, w_down, ada_weight, ada_bias, cotangent
):
    half, width = tokens.shape[1], tokens.shape[2]
    length = 2 * half
    gain = ln_gain.reshape(1, width)
    cosine, sine = (jnp.asarray(a) for a in rotary_np(length))
    embedding = time_embedding(timestep)

    _, _, _, _, d_up, d_down, d_out, d_qkv, mixed, dtok, d_ada_weight, d_ada_bias, dgain = layer_call(
        tokens, cotangent, w_qkv, w_out, w_up, w_down, gain, segment_ids, cosine, sine,
        embedding, ada_weight, ada_bias.reshape(1, 3 * width),
    )
    d_ada_weight = jnp.concatenate([d_ada_weight[TEMB * i : TEMB * (i + 1)] for i in range(3)], axis=1)
    d_ada_bias, d_gain = d_ada_bias[0], dgain[0]
    d_up, d_qkv = d_up.astype(f32), d_qkv.astype(f32)
    d_down = d_down.reshape(-1, width).astype(f32)
    heads = d_out.shape[1]
    d_out = jnp.concatenate([d_out[:heads], d_out[heads:]], axis=1).astype(f32)

    def rest(a):
        bit = 16
        while bit < groups:
            a = a + lax.ppermute(a, "dp", [(i, i ^ bit) for i in range(groups)])
            bit *= 2
        return a

    return (
        mixed,
        dtok,
        rest(d_gain),
        rest(d_qkv),
        rest(d_out),
        rest(d_up),
        rest(d_down),
        rest(d_ada_weight),
        rest(d_ada_bias),
    )


def solution(mesh):
    in_specs = (
        P("dp", "tensor", None),
        P("dp", None),
        P("dp"),
        P(),
        P(None, None, "tensor"),
        P("tensor", None),
        P(None, "tensor"),
        P("tensor", None),
        P(),
        P(),
        P("dp", "tensor", None),
    )
    out_specs = (
        P("dp", "tensor", None),
        P("dp", "tensor", None),
        P(),
        P(None, None, "tensor"),
        P("tensor", None),
        P(None, "tensor"),
        P("tensor", None),
        P(),
        P(),
    )
    return jax.shard_map(
        functools.partial(per_device, mesh.shape["dp"]), mesh=mesh, in_specs=in_specs, out_specs=out_specs, check_vma=False
    )
```

```python
import functools
import math

import jax
import jax.numpy as jnp
import numpy as np
from jax import lax
from jax.experimental import pallas as pl
from jax.experimental.pallas import tpu as pltpu
from jax.sharding import PartitionSpec as P

HD = 64
TEMB = 128
EPS = 1e-05
MASKED = -1000000000.0
f32 = jnp.float32
bf16 = jnp.bfloat16
VMEM_LIMIT = 62 * 1024 * 1024


def dot_nn(a, b):
    return lax.dot_general(a, b, (((1,), (0,)), ((), ())), preferred_element_type=f32)


def dot_nt(a, b):
    return lax.dot_general(a, b, (((1,), (1,)), ((), ())), preferred_element_type=f32)


def dot_tn(a, b):
    return lax.dot_general(a, b, (((0,), (0,)), ((), ())), preferred_element_type=f32)


def norm_parts(values):
    centred = values - jnp.mean(values, axis=-1, keepdims=True)
    variance = jnp.mean(centred * centred, axis=-1, keepdims=True)
    inverse = lax.rsqrt(variance + EPS)
    return centred * inverse, inverse


def norm_back(grad, normed, inverse):
    return inverse * (
        grad
        - jnp.mean(grad, axis=-1, keepdims=True)
        - normed * jnp.mean(grad * normed, axis=-1, keepdims=True)
    )


def rotary_np(length):
    half = HD // 2
    position = np.arange(length, dtype=np.float32)
    frequency = (10000.0 ** (-np.arange(half, dtype=np.float32) / half)).astype(np.float32)
    angles = position[:, None] * frequency[None, :]
    cosine, sine = np.cos(angles), np.sin(angles)
    cosine = np.concatenate([cosine, cosine] * 2, axis=1).astype(np.float32)
    sine = np.concatenate([-sine, sine] * 2, axis=1).astype(np.float32)
    return cosine, sine


def swap_halves(values):
    lane = lax.broadcasted_iota(jnp.int32, values.shape, 1)
    first = (lane % HD) < (HD // 2)
    return jnp.where(first, pltpu.roll(values, 128 - HD // 2, 1), pltpu.roll(values, HD // 2, 1))


def params(**kw):
    return pltpu.CompilerParams(vmem_limit_bytes=VMEM_LIMIT, **kw)


def cost(flops, nbytes, trans=0):
    return pl.CostEstimate(flops=int(flops), bytes_accessed=int(nbytes), transcendentals=int(trans))


BITS = {"core": 1, "y": 2, "zl": 4, "zh": 8}
MESH = pl.DeviceIdType.MESH


class Place:
    def __init__(self):
        self.me = lax.axis_index("dp")
        self.side = lax.axis_index("tensor")
        self.bit = {axis: (self.me // bit) % 2 for axis, bit in BITS.items()}
        self.partner = {
            axis: {"dp": self.me + bit * (1 - 2 * self.bit[axis])} for axis, bit in BITS.items()
        }
        self.partner["x"] = {"tensor": 1 - self.side}

    def greet(self, axes):
        barrier = pltpu.get_barrier_semaphore()
        for axis in axes:
            pl.semaphore_signal(barrier, inc=1, device_id=self.partner[axis], device_id_type=MESH)
        pl.semaphore_wait(barrier, len(axes))


ALL_AXES = ("core", "y", "zl", "zh", "x")


def remote(src, dst, send, recv, partner):
    return pltpu.make_async_remote_copy(
        src_ref=src, dst_ref=dst, send_sem=send, recv_sem=recv, device_id=partner, device_id_type=MESH
    )


class Reducer:
    STAGES = 5

    def __init__(self, place, view, rows, refs, order):
        self.place, self.view, self.order = place, view, order
        self.received, self.sends, self.recvs = refs[:5], refs[5], refs[6]
        self.cross = order.index("x")
        base, n = 0, rows
        self.spans = []
        for axis in order:
            if axis == "x":
                span = pl.ds(pl.multiple_of(base, 16), n)
                self.spans.append((span, span))
            else:
                n //= 2
                bit = place.bit[axis]
                keep = pl.ds(pl.multiple_of(base + bit * n, 16), n)
                send = pl.ds(pl.multiple_of(base + (1 - bit) * n, 16), n)
                self.spans.append((keep, send))
                base = base + bit * n

    @staticmethod
    def scratch(counts, rows, cols, order):
        shapes, n, cross = [], rows, False
        for slots, axis in zip(counts, order):
            if axis == "x":
                cross = True
            else:
                n //= 2
            shapes.append((slots, n, cols) if cross else (slots, 2, n, cols))
        return [pltpu.VMEM(shape, bf16) for shape in shapes] + [pltpu.SemaphoreType.DMA((sum(counts),))] * 2

    def slot(self, stage, c):
        return self.received[stage].at[c % self.received[stage].shape[0]]

    def flag(self, stage, c):
        before = sum(self.received[s].shape[0] for s in range(stage))
        return before + c % self.received[stage].shape[0]

    def copy(self, stage, c):
        send = self.spans[stage][1]
        if stage < self.cross:
            source = self.view(c).at[:, send, :]
        else:
            source = self.view(c).at[1 if stage == self.cross else 0, send, :]
        return remote(
            source,
            self.slot(stage, c),
            self.sends.at[self.flag(stage, c)],
            self.recvs.at[self.flag(stage, c)],
            self.place.partner[self.order[stage]],
        )

    def start(self, stage, c):
        self.copy(stage, c).start()

    def finish(self, stage, c, put=None):
        self.copy(stage, c).wait()
        keep = self.spans[stage][0]
        came, chunk = self.slot(stage, c), self.view(c)
        if stage < self.cross:
            for half in range(2):
                chunk[half, keep, :] += came[half]
        elif stage < 4:
            chunk[0, keep, :] += came[...]
        else:
            put(c, chunk[0, keep, :] + came[...])

    def step(self, stage, c, put=None):
        self.finish(stage, c, put)
        if stage + 1 < self.STAGES:
            self.start(stage + 1, c)


class Gatherer:
    STAGES = 4

    def __init__(self, place, view, rows, order, sends, recvs):
        self.place, self.view, self.sends, self.recvs = place, view, sends, recvs
        self.order = [axis for axis in order if axis != "x"][::-1]
        self.size = rows // 16
        bits = [place.bit[axis] for axis in self.order]
        self.bases = [sum(bits[j] * 2**j for j in range(stage, 4)) for stage in range(4)]

    def span(self, stage):
        n = self.size
        return self.view(pl.ds(pl.multiple_of(self.bases[stage] * n, 16), 2**stage * n))

    def copy(self, stage):
        span = self.span(stage)
        return remote(
            span, span, self.sends.at[stage], self.recvs.at[stage], self.place.partner[self.order[stage]]
        )

    def start(self, stage):
        self.copy(stage).start()

    def finish(self, stage):
        self.copy(stage).wait()


class Fetch:
    def __init__(self, place, own, other, rows, axes, sends, recvs):
        self.place, self.own, self.other, self.axes = place, own, other, axes
        self.sends, self.recvs = sends, recvs
        self.size = rows // 2 ** len(axes)
        bits = [place.bit[axis] for axis in axes]
        self.bases = [sum(bits[j] * 2**j for j in range(s, len(axes))) for s in range(len(axes))]

    def copy(self, stage):
        level = max(stage - 1, 0)
        n = self.size
        span = pl.ds(pl.multiple_of(self.bases[level] * n, 16), 2**level * n)
        source = self.own(span) if stage == 0 else self.other(span)
        axis = "x" if stage == 0 else self.axes[stage - 1]
        return remote(
            source, self.other(span), self.sends.at[stage], self.recvs.at[stage], self.place.partner[axis]
        )

    def start(self, stage):
        self.copy(stage).start()

    def step(self, stage):
        self.copy(stage).wait()
        if stage < len(self.axes):
            self.copy(stage + 1).start()


def qkv_rows(row, rows, x_ref, gain_ref, w_ref, cos_ref, sin_ref, n_ref, q_ref, k_ref, v_ref, first):
    span = pl.ds(row, rows)
    pairs = w_ref.shape[2] // 128
    if n_ref is None:
        normed = x_ref[span, :]
    else:
        normed, _ = norm_parts(x_ref[span, :].astype(f32))
        normed = (normed * gain_ref[...].reshape(1, -1)).astype(bf16)
        n_ref[span, :] = normed
    cosine, sine = cos_ref[span, :], sin_ref[span, :]
    for which, out in ((0, q_ref), (1, k_ref)):
        raw = dot_nn(normed, w_ref[which])
        for pair in range(pairs):
            part = raw[:, pair * 128 : pair * 128 + 128]
            turned = (part * cosine + swap_halves(part) * sine).astype(bf16)
            if which == 0:
                turned = turned * jnp.asarray(0.125, bf16)
            out[first + pair, span, :] = turned
    raw = dot_nn(normed, w_ref[2]).astype(bf16)
    for pair in range(pairs):
        v_ref[first + pair, span, :] = raw[:, pair * 128 : pair * 128 + 128]


EDGE = 256


def mask_scores(scores, inner, column, segr):
    length = scores.shape[1]
    last = length - EDGE
    middle = segr[:, length // 2 : length // 2 + 128]
    if inner:
        bias = jnp.where(jnp.concatenate([middle] * (length // 128), axis=1) == segr, 0.0, MASKED)
        parts = [scores[:, :EDGE] + bias[:, :EDGE], scores[:, EDGE:last], scores[:, last:] + bias[:, last:]]
    else:
        wide = jnp.concatenate([column] * (EDGE // 128), axis=1)
        inside = column == middle
        parts = (
            [jnp.where(wide == segr[:, :EDGE], scores[:, :EDGE], MASKED)]
            + [jnp.where(inside, scores[:, j : j + 128], MASKED) for j in range(EDGE, last, 128)]
            + [jnp.where(wide == segr[:, last:], scores[:, last:], MASKED)]
        )
    return jnp.concatenate(parts, axis=1)


def attend_rows(pair, spans, q_ref, k_ref, v_ref, segc_ref, segr, o_ref, lse_ref):
    lane = lax.broadcasted_iota(jnp.int32, (1, 128), 1)
    low = lane < HD
    mine = (low, jnp.logical_not(low))
    k, v = k_ref[pair], v_ref[pair]
    one = jnp.ones_like(v)
    values = [jnp.where(m, v, one) for m in mine]
    units = [(span, inner, head) for span, inner in spans for head in range(2)]

    def score(unit):
        span, _, head = unit
        q = q_ref[pair, span, :]
        return dot_nt(jnp.where(mine[head], q, jnp.zeros_like(q)), k)

    ahead = 2
    scores = [score(unit) for unit in units[:ahead]]
    parts = []
    for i, (span, inner, head) in enumerate(units):
        if i + ahead < len(units):
            scores.append(score(units[i + ahead]))
        masked = mask_scores(scores[i], inner, segc_ref[span, :], segr)
        largest = jnp.max(masked, axis=1, keepdims=True)
        weights = jnp.exp(masked - largest).astype(bf16)
        mixed = dot_nn(weights, values[head])
        total = pltpu.roll(mixed, HD, 1)
        parts.append((mixed / total, largest + jnp.log(total)))
        if head == 1:
            (out0, lse0), (out1, lse1) = parts[-2:]
            o_ref[span, pl.ds(pl.multiple_of(pair * 128, 128), 128)] = jnp.where(low, out0, out1).astype(bf16)
            lse = jnp.where(low, lse0, lse1).T
            lse_ref[pair, 0:1, span] = lse[0:1, :]
            lse_ref[pair, 1:2, span] = lse[HD : HD + 1, :]


def gelu_both(u):
    c0 = math.sqrt(2.0 / math.pi)
    square = u * u
    t = jnp.tanh(u * (c0 + (c0 * 0.044715) * square))
    half = 0.5 + 0.5 * t
    act = u * half
    slope = half + (0.5 * u) * (1.0 - t * t) * (c0 + (3.0 * c0 * 0.044715) * square)
    return act, slope


FEED_STEPS = 6
UP_ORDER = ("core", "y", "zl", "x", "zh")
DOWN_ORDER = ("core", "x", "zl", "y", "zh")
QKV_ORDERS = (
    ("core", "y", "x", "zl", "zh"),
    ("core", "x", "y", "zl", "zh"),
    ("core", "zl", "x", "y", "zh"),
)


def attend_back(
    pair, q_ref, k_ref, v_ref, o_ref, do_ref, lse_ref, segc_ref, segr, cos_ref, sin_ref, acc_ref, poll
):
    length = o_ref.shape[0]
    rows = 256
    lane = lax.broadcasted_iota(jnp.int32, (1, 128), 1)
    low = lane < HD
    lanes = pl.ds(pl.multiple_of(pair * 128, 128), 128)
    q, do = q_ref[pair], do_ref[:, lanes]
    product = do.astype(f32) * o_ref[:, lanes].astype(f32)
    high_part = product.astype(bf16)
    low_part = (product - high_part.astype(f32)).astype(bf16)
    row8 = lax.broadcasted_iota(jnp.int32, (8, 128), 0)
    lane8 = lax.broadcasted_iota(jnp.int32, (8, 128), 1)
    select = jnp.where((lane8 // HD) == row8, 1.0, 0.0).astype(bf16)
    delta = dot_nt(select, high_part) + dot_nt(select, low_part)
    lse = lse_ref[pair]
    zero = jnp.zeros_like(q)
    q_heads = (jnp.where(low, q, zero), jnp.where(low, zero, q))
    do_heads = (jnp.where(low, do, zero), jnp.where(low, zero, do))
    acc_ref[...] = jnp.zeros_like(acc_ref)
    mine = (low, jnp.logical_not(low))
    blocks = length // rows
    for group in range(2):
        if group == 1:
            poll()
        units = [(block, head) for block in (3 * group, 1 + group) for head in range(2)]

        def products(unit):
            block, head = unit
            span = pl.ds(block * rows, rows)
            k, v = k_ref[pair, span, :], v_ref[pair, span, :]
            kh = jnp.where(mine[head], k, jnp.zeros_like(k))
            vh = jnp.where(mine[head], v, jnp.zeros_like(v))
            return kh, dot_nt(kh, q), dot_nt(vh, do)

        ahead = 1
        ready = [products(unit) for unit in units[:ahead]]
        dq = jnp.zeros((128, length), f32)
        for i, (block, head) in enumerate(units):
            if i + ahead < len(units):
                ready.append(products(units[i + ahead]))
            kh, scores, d_probs = ready[i]
            span = pl.ds(block * rows, rows)
            inner = block * rows >= EDGE and (block + 1) * rows <= length - EDGE
            scores = mask_scores(scores, inner, segc_ref[span, :], segr)
            probs = jnp.exp(scores - lse[head : head + 1, :])
            part_v = dot_nn(probs.astype(bf16), do_heads[head])
            d_scores = (probs * (d_probs - delta[head : head + 1, :])).astype(bf16)
            part_k = dot_nn(d_scores, q_heads[head])
            dq = dq + dot_tn(kh, d_scores)
            if head == 0:
                dv, dk = part_v, part_k
            else:
                dv, dk = dv + part_v, dk + part_k
                cosine, sine = cos_ref[span, :], sin_ref[span, :]
                k_ref[pair, span, :] = (dk * cosine - swap_halves(dk) * sine).astype(bf16)
                v_ref[pair, span, :] = dv.astype(bf16)
        acc_ref[...] += dq
    dq = acc_ref[...].T * 0.125
    q_ref[pair] = (dq * cos_ref[...] - swap_halves(dq) * sin_ref[...]).astype(bf16)


SPREAD_ORDER = ("zh", "zl", "y", "x", "core")


def layer_kernel(
    tok, cot_in, wq, wo, wu, wd, gain_ref, seg_ref, cos_ref, sin_ref, emb_ref, ada_ref, bias_ref,
    oq, oo, ou, od, up_out, down_out, out_out, qkv_out, mixed_out, dtok_out, dada_out, dbias_ref, dgain_ref,
    xs, ns, qs, ks, vs, os, ls, segc, wqs, wos, cot, mod,
    hidden, modul, modul_t, dbranch, branch, dmod, acts, dups, upbuf, downbuf, acc,
    ups, downs, fin_up, fin_down, fin_out, fin_qkv, every, gains, gains_in,
    local, xsend, xrecv, wsend, wrecv, loads,
    fsend, frecv, asend, arecv, gsend, grecv, ssend, srecv, *reducing,
):
    place = Place()
    side = place.side
    length, width = xs.shape
    half = length // 2
    rows = 256
    blocks = length // rows
    block = wu.shape[1] // FEED_STEPS
    heads = wo.shape[0]
    hid = wu.shape[1]
    tiles = 3 * width // 128
    own_rows = pl.ds(pl.multiple_of(side * half, half), half)
    other_rows = pl.ds(pl.multiple_of((1 - side) * half, half), half)

    def copy_here(src, dst, index):
        copy = pltpu.make_async_copy(src, dst, local.at[index])
        copy.start()
        return copy

    place.greet(ALL_AXES)
    send_tok = remote(tok.at[1 - side], xs.at[own_rows, :], xsend.at[0], xrecv.at[0], place.partner["x"])
    send_cot = remote(cot_in.at[1 - side], cot.at[own_rows, :], xsend.at[1], xrecv.at[1], place.partner["x"])

    def up_view(g):
        return lambda r, s: r.at[s, pl.ds(g * hid // 3, hid // 3)]

    def down_view(g):
        return lambda r, s: r.at[pl.ds(g * hid // 3, hid // 3)].at[s, :]

    plan = (
        (lambda r, s: r.at[2, s, :], wq, oq, width, ("y", "zl", "core")),
        (lambda r, s: r.at[0, s, :], wq, oq, width, ("y", "core")),
        (lambda r, s: r.at[1, s, :], wq, oq, width, ("zl", "core")),
        (lambda r, s: r.at[s, :], wo, oo, heads, ("y", "zl", "core")),
        (up_view(0), wu, ou, width, ("y", "zl", "core")),
        (down_view(0), wd, od, hid // 3, ("zl", "y", "core")),
        (up_view(1), wu, ou, width, ("y", "zl", "core")),
        (down_view(1), wd, od, hid // 3, ("zl", "y", "core")),
        (up_view(2), wu, ou, width, ("y", "zl", "core")),
        (down_view(2), wd, od, hid // 3, ("zl", "y", "core")),
    )
    V, Q, K, OUT, UP0, DN0, UP1, DN1, UP2, DN2 = range(10)
    fetches = [
        Fetch(place, functools.partial(view, own), functools.partial(view, other), n, axes, wsend.at[i], wrecv.at[i])
        for i, (view, own, other, n, axes) in enumerate(plan)
    ]
    send_tok.start()
    for index in (V, Q, K, OUT, UP0, DN0, UP1, DN1):
        fetches[index].start(0)
    send_cot.start()
    for index in (UP2, DN2):
        fetches[index].start(0)

    get_x = copy_here(tok.at[side], xs.at[own_rows, :], 0)
    get_w = copy_here(wq, wqs.at[0], 1)
    get_cot = copy_here(cot_in.at[side], cot.at[own_rows, :], 2)
    get_wo = copy_here(wo, wos.at[pl.ds(0, heads), :], 3)

    segr = seg_ref[pl.ds(side, 1), :].astype(f32)
    segc[...] = jnp.broadcast_to(segr, (128, length)).T
    emb = jnp.broadcast_to(emb_ref[pl.ds(side, 1), :], (TEMB, TEMB)).T
    for tile in range(tiles):
        span = slice(tile * 128, tile * 128 + 128)
        value = jnp.sum(emb * ada_ref[:, span].astype(f32), axis=0, keepdims=True) + bias_ref[span].reshape(1, -1)
        start = tile * 128 % width
        mod[tile * 128 // width : tile * 128 // width + 1, start : start + 128] = value
    get_x.wait()
    get_w.wait()

    def qkv_half(base, w_ref, w_first, n_ref):
        def step(i, carry):
            row = pl.multiple_of(base + i * rows, rows)
            qkv_rows(
                row, rows, xs if n_ref is not None else ns, gain_ref, w_ref, cos_ref, sin_ref,
                n_ref, qs, ks, vs, w_first,
            )
            return carry

        lax.fori_loop(0, half // rows, step, 0)

    qkv_half(side * half, wqs.at[0], 0, ns)
    send_tok.wait()
    qkv_half((1 - side) * half, wqs.at[0], 0, ns)

    per_pair = 2
    steps = 6 * per_pair
    events = {
        0: ((V, 0),),
        2: ((V, 1), (Q, 0)),
        3: ((K, 0),),
        4: ((OUT, 0),),
        5: ((V, 2), (Q, 1), (UP0, 0)),
        6: ((OUT, 1), (UP0, 1), (DN0, 1)),
        7: ((UP1, 0), (DN1, 0)),
        10: ((DN0, 2), (OUT, 2)),
        11: ((UP0, 2), (UP1, 1)),
    }

    def attend(step, carry):
        pair = step // per_pair

        @pl.when(step == steps // 2)
        def _():
            fetches[K].step(1)
            fetches[DN0].step(0)
            for index in (V, Q, K):
                fetches[index].step(len(fetches[index].axes))
            copy = copy_here(oq, wqs.at[1], 1)
            copy.wait()
            qkv_half(0, wqs.at[1], 3, None)
            qkv_half(half, wqs.at[1], 3, None)

        for at, moves in events.items():

            @pl.when(step == at)
            def _(moves=moves):
                for index, stage in moves:
                    fetches[index].step(stage)

        part = step % per_pair
        edge = pl.ds(pl.multiple_of(part * (length - rows), rows), rows)
        inner = pl.ds(pl.multiple_of((1 + part) * rows, rows), rows)
        attend_rows(pair, ((edge, False), (inner, True)), qs, ks, vs, segc, segr, os, ls)
        return carry

    lax.fori_loop(0, steps, attend, 0)

    def load_weights(step):
        slot = step % 2
        span = pl.ds(pl.multiple_of(step * block, 128), block)
        return [
            pltpu.make_async_copy(wu.at[:, span], upbuf.at[slot, :, pl.ds(0, block)], loads.at[slot, 0]),
            pltpu.make_async_copy(ou.at[:, span], upbuf.at[slot, :, pl.ds(block, block)], loads.at[slot, 1]),
            pltpu.make_async_copy(wd.at[span, :], downbuf.at[slot, pl.ds(0, block), :], loads.at[slot, 2]),
            pltpu.make_async_copy(od.at[span, :], downbuf.at[slot, pl.ds(block, block), :], loads.at[slot, 3]),
        ]

    fetches[OUT].step(3)
    get_wo.wait()
    copy_here(oo, wos.at[pl.ds(heads, heads), :], 3).wait()
    get_cot.wait()
    fetches[DN1].step(1)
    fetches[UP0].step(3)
    fetches[DN0].step(3)
    for copy in load_weights(0):
        copy.start()

    def middle(i, carry):
        span = pl.ds(pl.multiple_of(i * rows, rows), rows)
        shift, scale = mod[0:1, :], mod[1:2, :]
        h = xs[span, :].astype(f32) + dot_nn(os[span, :], wos[...])
        hidden[span, :] = h
        normed, _ = norm_parts(h)
        m = (normed * (1.0 + scale) + shift).astype(bf16)
        modul[span, :] = m
        modul_t[:, span] = m.T
        branch[span, :] = jnp.zeros((rows, width), f32)
        dmod[span, :] = jnp.zeros((rows, width), f32)
        return carry

    lax.fori_loop(0, blocks, middle, 0)

    def to_branch(part):
        span = own_rows if part == 0 else other_rows
        dbranch[span, :] = (cot[span, :].astype(f32) * mod[2:3, :]).astype(bf16)

    to_branch(0)
    send_cot.wait()
    to_branch(1)

    def track(c, t):
        if isinstance(c, int) and c == 0:
            return upbuf.at[:, :, pl.ds(t * 128, 128)]
        index = 3 * (c - 1) + t
        return ups.at[index // 2, :, :, pl.ds(pl.multiple_of((index % 2) * 128, 128), 128)]

    feeders = [
        Reducer(place, lambda c: ups.at[c], width, reducing[0:7], UP_ORDER),
        Reducer(place, lambda c: downs.at[c], block, reducing[7:14], DOWN_ORDER),
    ]
    movers = [
        Reducer(
            place, functools.partial(track, t=t), width, reducing[14 + 7 * t : 21 + 7 * t], QKV_ORDERS[t]
        )
        for t in range(3)
    ]

    def put_up(c, value):
        fin_up[:, pl.ds(pl.multiple_of(c * block, 128), block)] = value

    def put_down(c, value):
        fin_down[c] = value

    def feed_event(stage, c):
        for reducer, put in zip(feeders, (put_up, put_down)):
            reducer.step(stage, c, put)

    def put_final(t):
        def put(c, value):
            if c == 0:
                fin_out[t] = value
            else:
                fin_qkv[c - 1, t] = value

        return put

    def move_event(stage, c):
        for t, reducer in enumerate(movers):
            reducer.step(stage, c, put_final(t))

    FIRST = (3, 6, 9)
    LATER = {
        0: {3: 12, 4: 15},
        1: {3: 14, 4: 17},
        2: {2: 13, 3: 16, 4: 18},
        3: {1: 12, 2: 16, 3: 18, 4: 20},
        4: {1: 14, 2: 18, 3: 20, 4: 22},
        5: {0: 13, 1: 18, 2: 20, 3: 22, 4: 23},
    }

    def feed_polls(t, stages):
        for stage in stages:
            since = t - FIRST[stage]

            @pl.when(since >= 0)
            def _(stage=stage, c=since // 2):
                feed_event(stage, c)

    def feed(step, carry):
        feed_polls(2 * step, (1,))
        @pl.when(step == 1)
        def _():
            fetches[UP1].step(3)
            fetches[DN1].step(3)

        @pl.when(step == 3)
        def _():
            fetches[UP2].step(2)
            fetches[DN2].step(2)

        for copy in load_weights(step):
            copy.wait()

        slot = step % 2
        up, down = upbuf.at[slot], downbuf.at[slot]
        for i in range(blocks):
            span = pl.ds(i * rows, rows)
            u = dot_nn(modul[span, :], up[...])
            act, slope = gelu_both(u)
            act = act.astype(bf16)
            acts[span, :] = act
            d_act = dot_nt(dbranch[span, :], down[...])
            d_up = (d_act * slope).astype(bf16)
            dups[span, :] = d_up
            branch[span, :] += dot_nn(act, down[...])
            dmod[span, :] += dot_nt(d_up, up[...])
        feed_polls(2 * step + 1, (2, 0))

        @pl.when(step == 0)
        def _():
            fetches[UP1].step(2)
            fetches[DN1].step(2)
            fetches[UP2].step(0)
            fetches[DN2].step(0)

        @pl.when(step == 1)
        def _():
            fetches[UP2].step(1)
            fetches[DN2].step(1)

        @pl.when(step == 3)
        def _():
            fetches[UP2].step(3)
            fetches[DN2].step(3)

        @pl.when(step + 1 < FEED_STEPS)
        def _():
            for copy in load_weights(step + 1):
                copy.start()

        grad = dot_nn(modul_t[...], dups[...]).astype(bf16)
        ups[step, 0] = grad[:, :block]
        ups[step, 1] = grad[:, block:]
        feeders[0].start(0, step)
        grad = dot_tn(acts[...], dbranch[...]).astype(bf16)
        downs[step, 0] = grad[:block]
        downs[step, 1] = grad[block:]
        feeders[1].start(0, step)
        return carry

    lax.fori_loop(0, FEED_STEPS, feed, 0)

    feed_schedule = {}
    for c, ends in LATER.items():
        for stage, t in ends.items():
            feed_schedule.setdefault(t, []).append((stage, c))

    def feed_static(t):
        for stage, c in feed_schedule.get(t, []):
            feed_event(stage, c)

    sums = dgain_ref
    sums[...] = jnp.zeros_like(sums)
    def between(i, carry):
        for k in range(blocks):

            @pl.when(i == k)
            def _(k=k):
                feed_static(2 * FEED_STEPS + k)

        span = pl.ds(pl.multiple_of(i * rows, rows), rows)
        scale, gate = mod[1:2, :], mod[2:3, :]
        h = hidden[span, :]
        dout = cot[span, :].astype(f32)
        br = branch[span, :]
        cot[span, :] = (h + gate * br).astype(bf16)
        normed, inverse = norm_parts(h)
        dm = dmod[span, :]
        sums[0:1, :] += jnp.sum(dm, axis=0, keepdims=True)
        sums[1:2, :] += jnp.sum(dm * normed, axis=0, keepdims=True)
        sums[2:3, :] += jnp.sum(dout * br, axis=0, keepdims=True)
        dh = dout + norm_back(dm * (1.0 + scale), normed, inverse)
        hidden[span, :] = dh
        dattn = dh.astype(bf16)
        modul[span, :] = dattn
        dbranch[span, :] = dot_nt(dattn, wos[...]).astype(bf16)
        return carry

    lax.fori_loop(0, blocks, between, 0)
    grad = dot_tn(os[...], modul[...]).astype(bf16)
    for t in range(3):
        chunk = track(0, t)
        for i in range(2):
            part = grad[i * heads : (i + 1) * heads]
            chunk[i, :heads, :] = part[:, t * 128 : t * 128 + 128]
            chunk[i, heads:, :] = part[:, heads + t * 128 : heads + t * 128 + 128]
        movers[t].start(0, 0)
    feed_static(16)

    number = sum(
        (side if axis == "x" else place.bit[axis]) * 2**i for i, axis in enumerate(SPREAD_ORDER)
    )
    every[pl.ds(number, 1)] = jnp.zeros((1,) + every.shape[1:], f32)
    for tile in range(tiles):
        line, lane = tile * 128 // width, tile * 128 % width
        every[pl.ds(number, 1), tile : tile + 1, :] = sums[line : line + 1, lane : lane + 128][None]
    every[pl.ds(number, 1), tiles : tiles + 1, :] = emb_ref[pl.ds(side, 1), :][None]

    def spread(stage):
        span = every.at[pl.ds(number - number % 2**stage, 2**stage)]
        return remote(span, span, ssend.at[stage], srecv.at[stage], place.partner[SPREAD_ORDER[stage]])

    spread(0).start()

    def send_mixed(i):
        n = half // 4
        span = pl.ds(pl.multiple_of((1 - side) * half + i * n, n), n)
        return remote(
            cot.at[span, :], mixed_out.at[side, pl.ds(i * n, n), :],
            xsend.at[2 + i], xrecv.at[2 + i], place.partner["x"],
        )

    keep_mixed = copy_here(cot.at[own_rows, :], mixed_out.at[side], 4)
    modul_t[...] = ns[...].T

    def gather_ffn(g):
        cols = hid // 2
        return [
            Gatherer(
                place, lambda s: up_out.at[s, pl.ds(g * cols, cols)], width, UP_ORDER, fsend.at[g, 0], frecv.at[g, 0]
            ),
            Gatherer(
                place, lambda s: down_out.at[pl.ds(3 * g, 3), s, :], block, DOWN_ORDER, fsend.at[g, 1], frecv.at[g, 1]
            ),
        ]

    def gather_qkv(t, first, count):
        lanes = pl.ds((first - 1) * 128, count * 128)
        return Gatherer(
            place, lambda s: qkv_out.at[t, s, lanes], width, QKV_ORDERS[t],
            asend.at[first - 1, t], arecv.at[first - 1, t],
        )

    def gather_out(t):
        lanes = pl.ds(t * 128, 128)
        return Gatherer(
            place, lambda s: out_out.at[s, lanes], width, QKV_ORDERS[t], asend.at[1, t], arecv.at[1, t]
        )

    def put_pieces(gathers, sources):
        copies = [
            pltpu.make_async_copy(source, gather.span(0), local.at[8 + i])
            for i, (gather, source) in enumerate(zip(gathers, sources))
        ]
        for copy in copies:
            copy.start()
        for copy in copies:
            copy.wait()

    def gather_event(gathers, stage):
        for gather in gathers:
            if stage >= 0:
                gather.finish(stage)
            if stage + 1 < Gatherer.STAGES:
                gather.start(stage + 1)

    ffn = [gather_ffn(0), gather_ffn(1)]

    def start_ffn(g):
        cols = hid // 2
        put_pieces(ffn[g], [fin_up.at[:, pl.ds(g * cols, cols)], fin_down.at[pl.ds(3 * g, 3)]])
        gather_event(ffn[g], -1)

    outs = [gather_out(t) for t in range(3)]
    gathers = {c: [gather_qkv(t, c, 1) for t in range(3)] for c in (1, 2, 3)}

    def start_qkv(c):
        put_pieces(gathers[c], [fin_qkv.at[c - 1, t] for t in range(3)])
        gather_event(gathers[c], -1)

    def start_out():
        put_pieces(outs, [fin_out.at[t] for t in range(3)])
        gather_event(outs, -1)

    back_events = {}

    def at(t, event, *operands):
        back_events.setdefault(t, []).append(functools.partial(event, *operands))

    for t, moves in feed_schedule.items():
        for stage, c in moves:
            if t > 16:
                at(t, feed_event, stage, c)
    for c, times in ((0, (17, 20, 21, 22, 24)), (1, (22, 24, 25, 26, 28)), (2, (26, 28))):
        for stage, t in enumerate(times):
            at(t, move_event, stage, c)
    at(19, start_ffn, 0)
    for stage, t in enumerate((22, 25, 27, 28)):
        at(t, gather_event, ffn[0], stage)
    at(23, start_ffn, 1)
    for stage, t in enumerate((26, 28)):
        at(t, gather_event, ffn[1], stage)
    at(24, start_out)
    for stage, t in enumerate((26, 28)):
        at(t, gather_event, outs, stage)
    at(28, lambda: start_qkv(1))

    def spread_event(stage):
        spread(stage).wait()
        if stage < 4:
            spread(stage + 1).start()

    for stage in range(5):
        at(18 + 2 * stage, spread_event, stage)
    for i in range(4):
        at(18 + 2 * i, lambda i: send_mixed(i).start(), i)

    def back_polls(step, which):
        for t, moves in back_events.items():
            if t >= 17 and (t - 17) % 2 == which:

                @pl.when(step == (t - 17) // 2)
                def _(moves=moves):
                    for move in moves:
                        move()

    def back(step, carry):
        pair = step // 2 + 3 * (step % 2)
        back_polls(step, 0)
        attend_back(
            pair, qs, ks, vs, os, dbranch, ls, segc, segr, cos_ref, sin_ref, acc,
            lambda: back_polls(step, 1),
        )
        for t, ref in enumerate((qs, ks, vs)):
            grad = dot_nn(modul_t[...], ref[pair]).astype(bf16)
            track(1 + step // 2, t)[step % 2] = grad

        @pl.when(step % 2 == 1)
        def _():
            for reducer in movers:
                reducer.start(0, 1 + step // 2)

        return carry

    lax.fori_loop(0, 6, back, 0)

    def gain_copy(stage):
        return remote(
            gains.at[stage], gains_in.at[stage], gsend.at[stage], grecv.at[stage],
            place.partner[ALL_AXES[stage]],
        )

    send_dtok = remote(modul.at[other_rows, :], dtok_out.at[side], xsend.at[6], xrecv.at[6], place.partner["x"])
    def gain_event(stage):
        gain_copy(stage).wait()
        total = gains[stage] + gains_in[stage]
        if stage < 4:
            gains[stage + 1] = total
            gain_copy(stage + 1).start()
        else:
            dgain_ref[...] = total

    def last_rows(i):
        b = ((1 - side) * (blocks // 2) + i) % blocks
        span = pl.ds(pl.multiple_of(b * rows, rows), rows)
        dnormed = jnp.zeros((rows, width), f32)
        for which, ref in enumerate((qs, ks, vs)):
            for group in range(2):
                grad = jnp.concatenate([ref[3 * group + p, span, :] for p in range(3)], axis=1)
                dnormed = dnormed + dot_nt(grad, wqs[group, which])
        normed, inverse = norm_parts(xs[span, :].astype(f32))
        gains[0, 0:1, :] += jnp.sum(dnormed * normed, axis=0, keepdims=True)
        modul[span, :] = (
            hidden[span, :] + norm_back(dnormed * gain_ref[...].reshape(1, -1), normed, inverse)
        ).astype(bf16)

    gains[0] = jnp.zeros(gains.shape[1:], f32)
    move_event(2, 2)
    gather_event(outs, 2)
    move_event(0, 3)

    def after_rows(i):
        if i == 0:
            move_event(3, 2)
            gather_event(gathers[1], 0)
            gather_event(ffn[1], 2)
        elif i == 1:
            gather_event(outs, 3)
            move_event(1, 3)
            send_dtok.start()
            move_event(4, 2)
            start_qkv(2)
            gather_event(ffn[1], 3)
        elif i == 2:
            gather_event(gathers[1], 1)

    def last_step(i, carry):
        last_rows(i)
        for k in range(blocks - 1):

            @pl.when(i == k)
            def _(k=k):
                after_rows(k)

        return carry

    lax.fori_loop(0, blocks, last_step, 0)
    move_event(2, 3)
    gather_event(gathers[2], 0)
    gain_copy(0).start()
    keep_dtok = copy_here(modul.at[own_rows, :], dtok_out.at[side], 5)
    gather_event(gathers[1], 2)
    embeddings = every[:, tiles, :]
    for tile in range(tiles):
        part = every[:, tile, :]
        lane = slice(tile * 128, tile * 128 + 128)
        line, start = tile * 128 // width, tile * 128 % width
        branch[line * TEMB : (line + 1) * TEMB, start : start + 128] = lax.dot_general(
            embeddings, part, (((0,), (0,)), ((), ())),
            preferred_element_type=f32, precision=lax.Precision.HIGHEST,
        )
        dbias_ref[0:1, lane] = jnp.sum(part, axis=0, keepdims=True)
    put_dada = copy_here(branch.at[pl.ds(0, 3 * TEMB), :], dada_out, 6)
    move_event(3, 3)
    gain_event(0)
    gather_event(gathers[2], 1)
    gather_event(gathers[1], 3)
    move_event(4, 3)
    start_qkv(3)
    gain_event(1)
    gather_event(gathers[2], 2)
    gather_event(gathers[3], 0)
    gain_event(2)
    gather_event(gathers[2], 3)
    gather_event(gathers[3], 1)
    gain_event(3)
    gather_event(gathers[3], 2)
    gather_event(gathers[3], 3)
    gain_event(4)
    for i in range(4):
        send_mixed(i).wait()
    keep_mixed.wait()
    send_dtok.wait()
    keep_dtok.wait()
    put_dada.wait()


def layer_call(tokens, cot, wq, wo, wu, wd, gain, segments, cosine, sine, embedding, ada, bias):
    length, width = 2 * tokens.shape[1], tokens.shape[2]
    half, hid = wq.shape[2], wu.shape[1]
    block = hid // FEED_STEPS
    pairs = width // 128
    any_ = pl.BlockSpec(memory_space=pl.ANY)
    vm = pl.BlockSpec(memory_space=pltpu.VMEM)
    shape = jax.ShapeDtypeStruct
    dma = pltpu.SemaphoreType.DMA
    low = lambda *dims: pltpu.VMEM(dims, bf16)
    full = lambda *dims: pltpu.VMEM(dims, f32)
    slots = (2, 4, 4, 4, 4)
    reducing = Reducer.scratch(slots, width, block, UP_ORDER)
    reducing += Reducer.scratch(slots, block, width, DOWN_ORDER)
    for order in QKV_ORDERS:
        reducing += Reducer.scratch((2,) * 5, width, 128, order)
    return pl.pallas_call(
        layer_kernel,
        in_specs=[any_] * 6 + [vm] * 7,
        out_specs=[any_] * 11 + [vm] * 2,
        out_shape=[
            shape(wq.shape, bf16),
            shape(wo.shape, bf16),
            shape(wu.shape, bf16),
            shape(wd.shape, bf16),
            shape((width, hid), bf16),
            shape((FEED_STEPS, block, width), bf16),
            shape((width, half), bf16),
            shape(wq.shape, bf16),
            shape((2, length // 2, width), bf16),
            shape((2, length // 2, width), bf16),
            shape((3 * TEMB, width), f32),
            shape((8, 3 * width), f32),
            shape((8, width), f32),
        ],
        scratch_shapes=[
            low(length, width),
            low(length, width),
            low(pairs, length, 128),
            low(pairs, length, 128),
            low(pairs, length, 128),
            low(length, width),
            full(pairs, 8, length),
            full(length, 128),
            low(2, *wq.shape),
            low(width, width),
            low(length, width),
            full(8, width),
            full(length, width),
            low(length, width),
            low(width, length),
            low(length, width),
            full(length, width),
            full(length, width),
            low(length, 2 * block),
            low(length, 2 * block),
            low(2, width, 2 * block),
            low(2, 2 * block, width),
            full(128, length),
            low(FEED_STEPS, 2, width, block),
            low(FEED_STEPS, 2, block, width),
            low(width // 16, hid),
            low(FEED_STEPS, block // 16, width),
            low(3, width // 16, 128),
            low(3, 3, width // 16, 128),
            full(32, 24, 128),
            full(5, 8, width),
            full(5, 8, width),
            dma((14,)),
            dma((7,)),
            dma((7,)),
            dma((10, 4)),
            dma((10, 4)),
            dma((2, 4)),
            dma((2, 2, 4)),
            dma((2, 2, 4)),
            dma((3, 3, 4)),
            dma((3, 3, 4)),
            dma((5,)),
            dma((5,)),
            dma((5,)),
            dma((5,)),
        ]
        + reducing,
        compiler_params=params(collective_id=0, has_side_effects=True),
        name="layer",
    )(tokens, cot, wq, wo, wu, wd, gain, segments, cosine, sine, embedding, ada, bias)


def finish_kernel(
    up_ref, down_ref, left_ref, right_ref, qkv_ref, mixed_ref, dtok_ref, dada_ref, dbias_ref, dgain_ref,
    up_out, down_out, out_out, qkv_out, mixed_out, dtok_out, dada_out, dbias_out, dgain_out,
):
    dbias_out[...] = dbias_ref[0, :]
    dgain_out[...] = dgain_ref[0, :]
    up_out[...] = up_ref[...].astype(f32)
    down_out[...] = down_ref[...].astype(f32)
    out_out[...] = jnp.concatenate([left_ref[...], right_ref[...]], axis=1).astype(f32)
    qkv_out[...] = qkv_ref[...].astype(f32)
    mixed_out[...] = mixed_ref[...]
    dtok_out[...] = dtok_ref[...]
    dada_out[...] = jnp.concatenate([dada_ref[i] for i in range(3)], axis=1)


def finish_call(up, down, out, qkv, mixed, dtok, dada, dbias, dgain):
    steps = 8
    shape = jax.ShapeDtypeStruct
    halves, half = out.shape[0] // 2, out.shape[1]

    def rows(a):
        return pl.BlockSpec((a.shape[0] // steps, a.shape[1]), lambda i: (i, 0))

    def middle(a):
        return pl.BlockSpec((a.shape[0], a.shape[1] // steps, a.shape[2]), lambda i: (0, i, 0))

    part = (halves // steps, half)
    outs = [
        shape(up.shape, f32),
        shape(down.shape, f32),
        shape((halves, 2 * half), f32),
        shape(qkv.shape, f32),
        shape(mixed.shape, bf16),
        shape(dtok.shape, bf16),
        shape((dada.shape[1], 3 * dada.shape[2]), f32),
        shape(dbias.shape[1:], f32),
        shape(dgain.shape[1:], f32),
    ]

    def placed(a):
        if len(a.shape) == 1:
            return pl.BlockSpec(a.shape, lambda i: (0,))
        return rows(a) if len(a.shape) == 2 else middle(a)

    def whole(a):
        return pl.BlockSpec(a.shape, lambda i: (0, 0))

    return pl.pallas_call(
        finish_kernel,
        grid=(steps,),
        in_specs=[
            rows(up),
            rows(down),
            pl.BlockSpec(part, lambda i: (i, 0)),
            pl.BlockSpec(part, lambda i: (i + steps, 0)),
            middle(qkv),
            middle(mixed),
            middle(dtok),
            middle(dada),
            whole(dbias),
            whole(dgain),
        ],
        out_specs=[placed(o) for o in outs],
        out_shape=outs,
        compiler_params=params(),
        name="finish",
    )(up, down, out, out, qkv, mixed, dtok, dada, dbias, dgain)


def time_embedding(timestep):
    half = TEMB // 2
    frequency = jnp.exp(-math.log(10000.0) * jnp.arange(half, dtype=f32) / half)
    angles = timestep.astype(f32)[:, None] * frequency[None, :]
    return jnp.concatenate([jnp.cos(angles), jnp.sin(angles)], axis=-1)


def per_device(
    groups, tokens, segment_ids, timestep, ln_gain, w_qkv, w_out, w_up, w_down, ada_weight, ada_bias, cotangent
):
    half, width = tokens.shape[1], tokens.shape[2]
    length = 2 * half
    cosine, sine = (jnp.asarray(a) for a in rotary_np(length))
    embedding = time_embedding(timestep)

    _, _, _, _, d_up, d_down, d_out, d_qkv, mixed, dtok, d_ada_weight, d_ada_bias, dgain = layer_call(
        tokens, cotangent, w_qkv, w_out, w_up, w_down, ln_gain, segment_ids, cosine, sine,
        embedding, ada_weight, ada_bias,
    )
    d_up, d_down, d_out, d_qkv, mixed, dtok, d_ada_weight, d_ada_bias, d_gain = finish_call(
        d_up, d_down.reshape(-1, width), d_out, d_qkv, mixed, dtok, d_ada_weight.reshape(3, TEMB, width),
        d_ada_bias, dgain,
    )

    def rest(a):
        bit = 16
        while bit < groups:
            a = a + lax.ppermute(a, "dp", [(i, i ^ bit) for i in range(groups)])
            bit *= 2
        return a

    return (
        mixed,
        dtok,
        rest(d_gain),
        rest(d_qkv),
        rest(d_out),
        rest(d_up),
        rest(d_down),
        rest(d_ada_weight),
        rest(d_ada_bias),
    )


def solution(mesh):
    in_specs = (
        P("dp", "tensor", None),
        P("dp", None),
        P("dp"),
        P(),
        P(None, None, "tensor"),
        P("tensor", None),
        P(None, "tensor"),
        P("tensor", None),
        P(),
        P(),
        P("dp", "tensor", None),
    )
    out_specs = (
        P("dp", "tensor", None),
        P("dp", "tensor", None),
        P(),
        P(None, None, "tensor"),
        P("tensor", None),
        P(None, "tensor"),
        P("tensor", None),
        P(),
        P(),
    )
    return jax.shard_map(
        functools.partial(per_device, mesh.shape["dp"]), mesh=mesh, in_specs=in_specs, out_specs=out_specs, check_vma=False
    )
```

```python
import functools
import math

import jax
import jax.numpy as jnp
import numpy as np
from jax import lax
from jax.experimental import pallas as pl
from jax.experimental.pallas import tpu as pltpu
from jax.sharding import PartitionSpec as P

HD = 64
TEMB = 128
EPS = 1e-05
MASKED = -1000000000.0
f32 = jnp.float32
bf16 = jnp.bfloat16
VMEM_LIMIT = 62 * 1024 * 1024


def dot_nn(a, b):
    return lax.dot_general(a, b, (((1,), (0,)), ((), ())), preferred_element_type=f32)


def dot_nt(a, b):
    return lax.dot_general(a, b, (((1,), (1,)), ((), ())), preferred_element_type=f32)


def dot_tn(a, b):
    return lax.dot_general(a, b, (((0,), (0,)), ((), ())), preferred_element_type=f32)


def norm_parts(values):
    centred = values - jnp.mean(values, axis=-1, keepdims=True)
    variance = jnp.mean(centred * centred, axis=-1, keepdims=True)
    inverse = lax.rsqrt(variance + EPS)
    return centred * inverse, inverse


def norm_back(grad, normed, inverse):
    return inverse * (
        grad
        - jnp.mean(grad, axis=-1, keepdims=True)
        - normed * jnp.mean(grad * normed, axis=-1, keepdims=True)
    )


def rotary_np(length):
    half = HD // 2
    position = np.arange(length, dtype=np.float32)
    frequency = (10000.0 ** (-np.arange(half, dtype=np.float32) / half)).astype(np.float32)
    angles = position[:, None] * frequency[None, :]
    cosine, sine = np.cos(angles), np.sin(angles)
    cosine = np.concatenate([cosine, cosine] * 2, axis=1).astype(np.float32)
    sine = np.concatenate([-sine, sine] * 2, axis=1).astype(np.float32)
    return cosine, sine


def swap_halves(values):
    lane = lax.broadcasted_iota(jnp.int32, values.shape, 1)
    first = (lane % HD) < (HD // 2)
    return jnp.where(first, pltpu.roll(values, 128 - HD // 2, 1), pltpu.roll(values, HD // 2, 1))


def params(**kw):
    return pltpu.CompilerParams(vmem_limit_bytes=VMEM_LIMIT, **kw)


def cost(flops, nbytes, trans=0):
    return pl.CostEstimate(flops=int(flops), bytes_accessed=int(nbytes), transcendentals=int(trans))


BITS = {"core": 1, "y": 2, "zl": 4, "zh": 8}
MESH = pl.DeviceIdType.MESH


class Place:
    def __init__(self):
        self.me = lax.axis_index("dp")
        self.side = lax.axis_index("tensor")
        self.bit = {axis: (self.me // bit) % 2 for axis, bit in BITS.items()}
        self.partner = {
            axis: {"dp": self.me + bit * (1 - 2 * self.bit[axis])} for axis, bit in BITS.items()
        }
        self.partner["x"] = {"tensor": 1 - self.side}

    def greet(self, axes):
        barrier = pltpu.get_barrier_semaphore()
        for axis in axes:
            pl.semaphore_signal(barrier, inc=1, device_id=self.partner[axis], device_id_type=MESH)
        pl.semaphore_wait(barrier, len(axes))


ALL_AXES = ("core", "y", "zl", "zh", "x")


def remote(src, dst, send, recv, partner):
    return pltpu.make_async_remote_copy(
        src_ref=src, dst_ref=dst, send_sem=send, recv_sem=recv, device_id=partner, device_id_type=MESH
    )


class Reducer:
    STAGES = 5

    def __init__(self, place, view, rows, refs, order):
        self.place, self.view, self.order = place, view, order
        self.received, self.sends, self.recvs = refs[:5], refs[5], refs[6]
        self.cross = order.index("x")
        base, n = 0, rows
        self.spans = []
        for axis in order:
            if axis == "x":
                span = pl.ds(pl.multiple_of(base, 16), n)
                self.spans.append((span, span))
            else:
                n //= 2
                bit = place.bit[axis]
                keep = pl.ds(pl.multiple_of(base + bit * n, 16), n)
                send = pl.ds(pl.multiple_of(base + (1 - bit) * n, 16), n)
                self.spans.append((keep, send))
                base = base + bit * n

    @staticmethod
    def scratch(counts, rows, cols, order):
        shapes, n, cross = [], rows, False
        for slots, axis in zip(counts, order):
            if axis == "x":
                cross = True
            else:
                n //= 2
            shapes.append((slots, n, cols) if cross else (slots, 2, n, cols))
        return [pltpu.VMEM(shape, bf16) for shape in shapes] + [pltpu.SemaphoreType.DMA((sum(counts),))] * 2

    def slot(self, stage, c):
        return self.received[stage].at[c % self.received[stage].shape[0]]

    def flag(self, stage, c):
        before = sum(self.received[s].shape[0] for s in range(stage))
        return before + c % self.received[stage].shape[0]

    def copy(self, stage, c):
        send = self.spans[stage][1]
        if stage < self.cross:
            source = self.view(c).at[:, send, :]
        else:
            source = self.view(c).at[1 if stage == self.cross else 0, send, :]
        return remote(
            source,
            self.slot(stage, c),
            self.sends.at[self.flag(stage, c)],
            self.recvs.at[self.flag(stage, c)],
            self.place.partner[self.order[stage]],
        )

    def start(self, stage, c):
        self.copy(stage, c).start()

    def finish(self, stage, c, put=None):
        self.copy(stage, c).wait()
        keep = self.spans[stage][0]
        came, chunk = self.slot(stage, c), self.view(c)
        if stage < self.cross:
            for half in range(2):
                chunk[half, keep, :] += came[half]
        elif stage < 4:
            chunk[0, keep, :] += came[...]
        else:
            put(c, chunk[0, keep, :] + came[...])

    def step(self, stage, c, put=None):
        self.finish(stage, c, put)
        if stage + 1 < self.STAGES:
            self.start(stage + 1, c)


class Gatherer:
    STAGES = 4

    def __init__(self, place, view, rows, order, sends, recvs):
        self.place, self.view, self.sends, self.recvs = place, view, sends, recvs
        self.order = [axis for axis in order if axis != "x"][::-1]
        self.size = rows // 16
        bits = [place.bit[axis] for axis in self.order]
        self.bases = [sum(bits[j] * 2**j for j in range(stage, 4)) for stage in range(4)]

    def span(self, stage):
        n = self.size
        return self.view(pl.ds(pl.multiple_of(self.bases[stage] * n, 16), 2**stage * n))

    def copy(self, stage):
        span = self.span(stage)
        return remote(
            span, span, self.sends.at[stage], self.recvs.at[stage], self.place.partner[self.order[stage]]
        )

    def start(self, stage):
        self.copy(stage).start()

    def finish(self, stage):
        self.copy(stage).wait()


class Fetch:
    def __init__(self, place, own, other, rows, axes, sends, recvs):
        self.place, self.own, self.other, self.axes = place, own, other, axes
        self.sends, self.recvs = sends, recvs
        self.size = rows // 2 ** len(axes)
        bits = [place.bit[axis] for axis in axes]
        self.bases = [sum(bits[j] * 2**j for j in range(s, len(axes))) for s in range(len(axes))]

    def copy(self, stage):
        level = max(stage - 1, 0)
        n = self.size
        span = pl.ds(pl.multiple_of(self.bases[level] * n, 16), 2**level * n)
        source = self.own(span) if stage == 0 else self.other(span)
        axis = "x" if stage == 0 else self.axes[stage - 1]
        return remote(
            source, self.other(span), self.sends.at[stage], self.recvs.at[stage], self.place.partner[axis]
        )

    def start(self, stage):
        self.copy(stage).start()

    def step(self, stage):
        self.copy(stage).wait()
        if stage < len(self.axes):
            self.copy(stage + 1).start()


def qkv_rows(row, rows, x_ref, gain_ref, w_ref, cos_ref, sin_ref, n_ref, q_ref, k_ref, v_ref, first):
    span = pl.ds(row, rows)
    pairs = w_ref.shape[2] // 128
    if n_ref is None:
        normed = x_ref[span, :]
    else:
        normed, _ = norm_parts(x_ref[span, :].astype(f32))
        normed = (normed * gain_ref[...].reshape(1, -1)).astype(bf16)
        n_ref[span, :] = normed
    cosine, sine = cos_ref[span, :], sin_ref[span, :]
    for which, out in ((0, q_ref), (1, k_ref)):
        raw = dot_nn(normed, w_ref[which])
        for pair in range(pairs):
            part = raw[:, pair * 128 : pair * 128 + 128]
            turned = (part * cosine + swap_halves(part) * sine).astype(bf16)
            if which == 0:
                turned = turned * jnp.asarray(0.125, bf16)
            out[first + pair, span, :] = turned
    raw = dot_nn(normed, w_ref[2]).astype(bf16)
    for pair in range(pairs):
        v_ref[first + pair, span, :] = raw[:, pair * 128 : pair * 128 + 128]


EDGE = 256


def mask_scores(scores, inner, column, segr):
    length = scores.shape[1]
    last = length - EDGE
    middle = segr[:, length // 2 : length // 2 + 128]
    if inner:
        bias = jnp.where(jnp.concatenate([middle] * (length // 128), axis=1) == segr, 0.0, MASKED)
        parts = [scores[:, :EDGE] + bias[:, :EDGE], scores[:, EDGE:last], scores[:, last:] + bias[:, last:]]
    else:
        wide = jnp.concatenate([column] * (EDGE // 128), axis=1)
        inside = column == middle
        parts = (
            [jnp.where(wide == segr[:, :EDGE], scores[:, :EDGE], MASKED)]
            + [jnp.where(inside, scores[:, j : j + 128], MASKED) for j in range(EDGE, last, 128)]
            + [jnp.where(wide == segr[:, last:], scores[:, last:], MASKED)]
        )
    return jnp.concatenate(parts, axis=1)


def attend_rows(pair, spans, q_ref, k_ref, v_ref, segc_ref, segr, o_ref, lse_ref):
    lane = lax.broadcasted_iota(jnp.int32, (1, 128), 1)
    low = lane < HD
    mine = (low, jnp.logical_not(low))
    k, v = k_ref[pair], v_ref[pair]
    one = jnp.ones_like(v)
    values = [jnp.where(m, v, one) for m in mine]
    units = [(span, inner, head) for span, inner in spans for head in range(2)]

    def score(unit):
        span, _, head = unit
        q = q_ref[pair, span, :]
        return dot_nt(jnp.where(mine[head], q, jnp.zeros_like(q)), k)

    ahead = 2
    scores = [score(unit) for unit in units[:ahead]]
    parts = []
    for i, (span, inner, head) in enumerate(units):
        if i + ahead < len(units):
            scores.append(score(units[i + ahead]))
        masked = mask_scores(scores[i], inner, segc_ref[span, :], segr)
        largest = jnp.max(masked, axis=1, keepdims=True)
        weights = jnp.exp(masked - largest).astype(bf16)
        mixed = dot_nn(weights, values[head])
        total = pltpu.roll(mixed, HD, 1)
        parts.append((mixed / total, largest + jnp.log(total)))
        if head == 1:
            (out0, lse0), (out1, lse1) = parts[-2:]
            o_ref[span, pl.ds(pl.multiple_of(pair * 128, 128), 128)] = jnp.where(low, out0, out1).astype(bf16)
            lse = jnp.where(low, lse0, lse1).T
            lse_ref[pair, 0:1, span] = lse[0:1, :]
            lse_ref[pair, 1:2, span] = lse[HD : HD + 1, :]


def gelu_both(u):
    c0 = math.sqrt(2.0 / math.pi)
    square = u * u
    t = jnp.tanh(u * (c0 + (c0 * 0.044715) * square))
    half = 0.5 + 0.5 * t
    act = u * half
    slope = half + (0.5 * u) * (1.0 - t * t) * (c0 + (3.0 * c0 * 0.044715) * square)
    return act, slope


FEED_STEPS = 6
UP_ORDER = ("core", "y", "zl", "x", "zh")
DOWN_ORDER = ("core", "x", "zl", "y", "zh")
QKV_ORDERS = (
    ("core", "y", "x", "zl", "zh"),
    ("core", "x", "y", "zl", "zh"),
    ("core", "zl", "x", "y", "zh"),
)


def attend_back(
    pair, q_ref, k_ref, v_ref, o_ref, do_ref, lse_ref, segc_ref, segr, cos_ref, sin_ref, acc_ref, poll
):
    length = o_ref.shape[0]
    rows = 256
    lane = lax.broadcasted_iota(jnp.int32, (1, 128), 1)
    low = lane < HD
    lanes = pl.ds(pl.multiple_of(pair * 128, 128), 128)
    q, do = q_ref[pair], do_ref[:, lanes]
    product = do.astype(f32) * o_ref[:, lanes].astype(f32)
    high_part = product.astype(bf16)
    low_part = (product - high_part.astype(f32)).astype(bf16)
    row8 = lax.broadcasted_iota(jnp.int32, (8, 128), 0)
    lane8 = lax.broadcasted_iota(jnp.int32, (8, 128), 1)
    select = jnp.where((lane8 // HD) == row8, 1.0, 0.0).astype(bf16)
    delta = dot_nt(select, high_part) + dot_nt(select, low_part)
    lse = lse_ref[pair]
    zero = jnp.zeros_like(q)
    q_heads = (jnp.where(low, q, zero), jnp.where(low, zero, q))
    do_heads = (jnp.where(low, do, zero), jnp.where(low, zero, do))
    acc_ref[...] = jnp.zeros_like(acc_ref)
    mine = (low, jnp.logical_not(low))
    blocks = length // rows
    for group in range(2):
        if group == 1:
            poll()
        units = [(block, head) for block in (3 * group, 1 + group) for head in range(2)]

        def products(unit):
            block, head = unit
            span = pl.ds(block * rows, rows)
            k, v = k_ref[pair, span, :], v_ref[pair, span, :]
            kh = jnp.where(mine[head], k, jnp.zeros_like(k))
            vh = jnp.where(mine[head], v, jnp.zeros_like(v))
            return kh, dot_nt(kh, q), dot_nt(vh, do)

        ahead = 1
        ready = [products(unit) for unit in units[:ahead]]
        dq = jnp.zeros((128, length), f32)
        for i, (block, head) in enumerate(units):
            if i + ahead < len(units):
                ready.append(products(units[i + ahead]))
            kh, scores, d_probs = ready[i]
            span = pl.ds(block * rows, rows)
            inner = block * rows >= EDGE and (block + 1) * rows <= length - EDGE
            scores = mask_scores(scores, inner, segc_ref[span, :], segr)
            probs = jnp.exp(scores - lse[head : head + 1, :])
            part_v = dot_nn(probs.astype(bf16), do_heads[head])
            d_scores = (probs * (d_probs - delta[head : head + 1, :])).astype(bf16)
            part_k = dot_nn(d_scores, q_heads[head])
            dq = dq + dot_tn(kh, d_scores)
            if head == 0:
                dv, dk = part_v, part_k
            else:
                dv, dk = dv + part_v, dk + part_k
                cosine, sine = cos_ref[span, :], sin_ref[span, :]
                k_ref[pair, span, :] = (dk * cosine - swap_halves(dk) * sine).astype(bf16)
                v_ref[pair, span, :] = dv.astype(bf16)
        acc_ref[...] += dq
    dq = acc_ref[...].T * 0.125
    q_ref[pair] = (dq * cos_ref[...] - swap_halves(dq) * sin_ref[...]).astype(bf16)


SPREAD_ORDER = ("zh", "zl", "y", "x", "core")


def layer_kernel(
    tok, cot_in, wq, wo, wu, wd, gain_ref, seg_ref, cos_ref, sin_ref, emb_ref, ada_ref, bias_ref,
    oq, oo, ou, od, up_out, down_out, out_out, qkv_out, mixed_out, dtok_out, dada_out, dbias_ref, dgain_ref,
    xs, ns, qs, ks, vs, os, ls, segc, wqs, wos, cot, mod,
    hidden, modul, modul_t, dbranch, branch, dmod, acts, dups, upbuf, downbuf, acc,
    ups, downs, fin_up, fin_down, fin_out, fin_qkv, every, gains, gains_in,
    local, xsend, xrecv, wsend, wrecv, loads,
    fsend, frecv, asend, arecv, gsend, grecv, ssend, srecv, *reducing,
):
    place = Place()
    side = place.side
    length, width = xs.shape
    half = length // 2
    rows = 256
    blocks = length // rows
    block = wu.shape[1] // FEED_STEPS
    heads = wo.shape[0]
    hid = wu.shape[1]
    tiles = 3 * width // 128
    own_rows = pl.ds(pl.multiple_of(side * half, half), half)
    other_rows = pl.ds(pl.multiple_of((1 - side) * half, half), half)

    def copy_here(src, dst, index):
        copy = pltpu.make_async_copy(src, dst, local.at[index])
        copy.start()
        return copy

    place.greet(ALL_AXES)
    send_tok = remote(tok.at[1 - side], xs.at[own_rows, :], xsend.at[0], xrecv.at[0], place.partner["x"])
    send_cot = remote(cot_in.at[1 - side], cot.at[own_rows, :], xsend.at[1], xrecv.at[1], place.partner["x"])

    def up_view(g):
        return lambda r, s: r.at[s, pl.ds(g * hid // 3, hid // 3)]

    def down_view(g):
        return lambda r, s: r.at[pl.ds(g * hid // 3, hid // 3)].at[s, :]

    plan = (
        (lambda r, s: r.at[2, s, :], wq, oq, width, ("y", "zl", "core")),
        (lambda r, s: r.at[0, s, :], wq, oq, width, ("y", "core")),
        (lambda r, s: r.at[1, s, :], wq, oq, width, ("zl", "core")),
        (lambda r, s: r.at[s, :], wo, oo, heads, ("y", "zl", "core")),
        (up_view(0), wu, ou, width, ("y", "zl", "core")),
        (down_view(0), wd, od, hid // 3, ("zl", "y", "core")),
        (up_view(1), wu, ou, width, ("y", "zl", "core")),
        (down_view(1), wd, od, hid // 3, ("zl", "y", "core")),
        (up_view(2), wu, ou, width, ("y", "zl", "core")),
        (down_view(2), wd, od, hid // 3, ("zl", "y", "core")),
    )
    V, Q, K, OUT, UP0, DN0, UP1, DN1, UP2, DN2 = range(10)
    fetches = [
        Fetch(place, functools.partial(view, own), functools.partial(view, other), n, axes, wsend.at[i], wrecv.at[i])
        for i, (view, own, other, n, axes) in enumerate(plan)
    ]
    send_tok.start()
    for index in (V, Q, K, OUT, UP0, DN0, UP1, DN1):
        fetches[index].start(0)
    send_cot.start()
    for index in (UP2, DN2):
        fetches[index].start(0)

    get_x = copy_here(tok.at[side], xs.at[own_rows, :], 0)
    get_w = copy_here(wq, wqs.at[0], 1)
    get_cot = copy_here(cot_in.at[side], cot.at[own_rows, :], 2)
    get_wo = copy_here(wo, wos.at[pl.ds(0, heads), :], 3)

    segr = seg_ref[pl.ds(side, 1), :].astype(f32)
    segc[...] = jnp.broadcast_to(segr, (128, length)).T
    emb = jnp.broadcast_to(emb_ref[pl.ds(side, 1), :], (TEMB, TEMB)).T
    for tile in range(tiles):
        span = slice(tile * 128, tile * 128 + 128)
        value = jnp.sum(emb * ada_ref[:, span].astype(f32), axis=0, keepdims=True) + bias_ref[span].reshape(1, -1)
        start = tile * 128 % width
        mod[tile * 128 // width : tile * 128 // width + 1, start : start + 128] = value
    get_x.wait()
    get_w.wait()

    def qkv_half(base, w_ref, w_first, n_ref):
        def step(i, carry):
            row = pl.multiple_of(base + i * rows, rows)
            qkv_rows(
                row, rows, xs if n_ref is not None else ns, gain_ref, w_ref, cos_ref, sin_ref,
                n_ref, qs, ks, vs, w_first,
            )
            return carry

        lax.fori_loop(0, half // rows, step, 0)

    qkv_half(side * half, wqs.at[0], 0, ns)
    send_tok.wait()
    qkv_half((1 - side) * half, wqs.at[0], 0, ns)

    per_pair = 2
    steps = 6 * per_pair
    events = {
        0: ((V, 0),),
        2: ((V, 1), (Q, 0)),
        3: ((K, 0),),
        4: ((OUT, 0),),
        5: ((V, 2), (Q, 1), (UP0, 0)),
        6: ((OUT, 1), (UP0, 1), (DN0, 1)),
        7: ((UP1, 0), (DN1, 0)),
        10: ((DN0, 2), (OUT, 2)),
        11: ((UP0, 2), (UP1, 1)),
    }

    def attend(step, carry):
        pair = step // per_pair

        @pl.when(step == steps // 2)
        def _():
            fetches[K].step(1)
            fetches[DN0].step(0)
            for index in (V, Q, K):
                fetches[index].step(len(fetches[index].axes))
            copy = copy_here(oq, wqs.at[1], 1)
            copy.wait()
            qkv_half(0, wqs.at[1], 3, None)
            qkv_half(half, wqs.at[1], 3, None)

        for at, moves in events.items():

            @pl.when(step == at)
            def _(moves=moves):
                for index, stage in moves:
                    fetches[index].step(stage)

        part = step % per_pair
        edge = pl.ds(pl.multiple_of(part * (length - rows), rows), rows)
        inner = pl.ds(pl.multiple_of((1 + part) * rows, rows), rows)
        attend_rows(pair, ((edge, False), (inner, True)), qs, ks, vs, segc, segr, os, ls)
        return carry

    lax.fori_loop(0, steps, attend, 0)

    def load_weights(step):
        slot = step % 2
        span = pl.ds(pl.multiple_of(step * block, 128), block)
        return [
            pltpu.make_async_copy(wu.at[:, span], upbuf.at[slot, :, pl.ds(0, block)], loads.at[slot, 0]),
            pltpu.make_async_copy(ou.at[:, span], upbuf.at[slot, :, pl.ds(block, block)], loads.at[slot, 1]),
            pltpu.make_async_copy(wd.at[span, :], downbuf.at[slot, pl.ds(0, block), :], loads.at[slot, 2]),
            pltpu.make_async_copy(od.at[span, :], downbuf.at[slot, pl.ds(block, block), :], loads.at[slot, 3]),
        ]

    fetches[OUT].step(3)
    get_wo.wait()
    copy_here(oo, wos.at[pl.ds(heads, heads), :], 3).wait()
    get_cot.wait()
    fetches[DN1].step(1)
    fetches[UP0].step(3)
    fetches[DN0].step(3)
    for copy in load_weights(0):
        copy.start()

    def middle(i, carry):
        span = pl.ds(pl.multiple_of(i * rows, rows), rows)
        shift, scale = mod[0:1, :], mod[1:2, :]
        h = xs[span, :].astype(f32) + dot_nn(os[span, :], wos[...])
        hidden[span, :] = h
        normed, _ = norm_parts(h)
        m = (normed * (1.0 + scale) + shift).astype(bf16)
        modul[span, :] = m
        modul_t[:, span] = m.T
        branch[span, :] = jnp.zeros((rows, width), f32)
        dmod[span, :] = jnp.zeros((rows, width), f32)
        return carry

    lax.fori_loop(0, blocks, middle, 0)

    def to_branch(part):
        span = own_rows if part == 0 else other_rows
        dbranch[span, :] = (cot[span, :].astype(f32) * mod[2:3, :]).astype(bf16)

    to_branch(0)
    send_cot.wait()
    to_branch(1)

    def track(c, t):
        if isinstance(c, int) and c == 0:
            return upbuf.at[:, :, pl.ds(t * 128, 128)]
        index = 3 * (c - 1) + t
        return ups.at[index // 2, :, :, pl.ds(pl.multiple_of((index % 2) * 128, 128), 128)]

    feeders = [
        Reducer(place, lambda c: ups.at[c], width, reducing[0:7], UP_ORDER),
        Reducer(place, lambda c: downs.at[c], block, reducing[7:14], DOWN_ORDER),
    ]
    movers = [
        Reducer(
            place, functools.partial(track, t=t), width, reducing[14 + 7 * t : 21 + 7 * t], QKV_ORDERS[t]
        )
        for t in range(3)
    ]

    def put_up(c, value):
        fin_up[:, pl.ds(pl.multiple_of(c * block, 128), block)] = value

    def put_down(c, value):
        fin_down[c] = value

    def feed_event(stage, c):
        for reducer, put in zip(feeders, (put_up, put_down)):
            reducer.step(stage, c, put)

    def put_final(t):
        def put(c, value):
            if c == 0:
                fin_out[t] = value
            else:
                fin_qkv[c - 1, t] = value

        return put

    def move_event(stage, c):
        for t, reducer in enumerate(movers):
            reducer.step(stage, c, put_final(t))

    FIRST = (3, 6, 9)
    LATER = {
        0: {3: 12, 4: 15},
        1: {3: 14, 4: 17},
        2: {2: 13, 3: 16, 4: 18},
        3: {1: 12, 2: 16, 3: 18, 4: 20},
        4: {1: 14, 2: 18, 3: 20, 4: 22},
        5: {0: 13, 1: 18, 2: 20, 3: 22, 4: 23},
    }

    def feed_polls(t, stages):
        for stage in stages:
            since = t - FIRST[stage]

            @pl.when(since >= 0)
            def _(stage=stage, c=since // 2):
                feed_event(stage, c)

    def feed(step, carry):
        feed_polls(2 * step, (1,))
        @pl.when(step == 1)
        def _():
            fetches[UP1].step(3)
            fetches[DN1].step(3)

        @pl.when(step == 3)
        def _():
            fetches[UP2].step(2)
            fetches[DN2].step(2)

        for copy in load_weights(step):
            copy.wait()

        slot = step % 2
        up, down = upbuf.at[slot], downbuf.at[slot]
        for i in range(blocks):
            span = pl.ds(i * rows, rows)
            u = dot_nn(modul[span, :], up[...])
            act, slope = gelu_both(u)
            act = act.astype(bf16)
            acts[span, :] = act
            d_act = dot_nt(dbranch[span, :], down[...])
            d_up = (d_act * slope).astype(bf16)
            dups[span, :] = d_up
            branch[span, :] += dot_nn(act, down[...])
            dmod[span, :] += dot_nt(d_up, up[...])
        feed_polls(2 * step + 1, (2, 0))

        @pl.when(step == 0)
        def _():
            fetches[UP1].step(2)
            fetches[DN1].step(2)
            fetches[UP2].step(0)
            fetches[DN2].step(0)

        @pl.when(step == 1)
        def _():
            fetches[UP2].step(1)
            fetches[DN2].step(1)

        @pl.when(step == 3)
        def _():
            fetches[UP2].step(3)
            fetches[DN2].step(3)

        @pl.when(step + 1 < FEED_STEPS)
        def _():
            for copy in load_weights(step + 1):
                copy.start()

        grad = dot_nn(modul_t[...], dups[...]).astype(bf16)
        ups[step, 0] = grad[:, :block]
        ups[step, 1] = grad[:, block:]
        feeders[0].start(0, step)
        grad = dot_tn(acts[...], dbranch[...]).astype(bf16)
        downs[step, 0] = grad[:block]
        downs[step, 1] = grad[block:]
        feeders[1].start(0, step)
        return carry

    lax.fori_loop(0, FEED_STEPS, feed, 0)

    feed_schedule = {}
    for c, ends in LATER.items():
        for stage, t in ends.items():
            feed_schedule.setdefault(t, []).append((stage, c))

    def feed_static(t):
        for stage, c in feed_schedule.get(t, []):
            feed_event(stage, c)

    sums = dgain_ref
    sums[...] = jnp.zeros_like(sums)
    def between(i, carry):
        for k in range(blocks):

            @pl.when(i == k)
            def _(k=k):
                feed_static(2 * FEED_STEPS + k)

        span = pl.ds(pl.multiple_of(i * rows, rows), rows)
        scale, gate = mod[1:2, :], mod[2:3, :]
        h = hidden[span, :]
        dout = cot[span, :].astype(f32)
        br = branch[span, :]
        cot[span, :] = (h + gate * br).astype(bf16)
        normed, inverse = norm_parts(h)
        dm = dmod[span, :]
        sums[0:1, :] += jnp.sum(dm, axis=0, keepdims=True)
        sums[1:2, :] += jnp.sum(dm * normed, axis=0, keepdims=True)
        sums[2:3, :] += jnp.sum(dout * br, axis=0, keepdims=True)
        dh = dout + norm_back(dm * (1.0 + scale), normed, inverse)
        hidden[span, :] = dh
        dattn = dh.astype(bf16)
        modul[span, :] = dattn
        dbranch[span, :] = dot_nt(dattn, wos[...]).astype(bf16)
        return carry

    lax.fori_loop(0, blocks, between, 0)
    grad = dot_tn(os[...], modul[...]).astype(bf16)
    for t in range(3):
        chunk = track(0, t)
        for i in range(2):
            part = grad[i * heads : (i + 1) * heads]
            chunk[i, :heads, :] = part[:, t * 128 : t * 128 + 128]
            chunk[i, heads:, :] = part[:, heads + t * 128 : heads + t * 128 + 128]
        movers[t].start(0, 0)
    feed_static(16)

    number = sum(
        (side if axis == "x" else place.bit[axis]) * 2**i for i, axis in enumerate(SPREAD_ORDER)
    )
    every[pl.ds(number, 1)] = jnp.zeros((1,) + every.shape[1:], f32)
    for tile in range(tiles):
        line, lane = tile * 128 // width, tile * 128 % width
        every[pl.ds(number, 1), tile : tile + 1, :] = sums[line : line + 1, lane : lane + 128][None]
    every[pl.ds(number, 1), tiles : tiles + 1, :] = emb_ref[pl.ds(side, 1), :][None]

    def spread(stage):
        span = every.at[pl.ds(number - number % 2**stage, 2**stage)]
        return remote(span, span, ssend.at[stage], srecv.at[stage], place.partner[SPREAD_ORDER[stage]])

    spread(0).start()

    def send_mixed(i):
        n = half // 4
        span = pl.ds(pl.multiple_of((1 - side) * half + i * n, n), n)
        return remote(
            cot.at[span, :], mixed_out.at[side, pl.ds(i * n, n), :],
            xsend.at[2 + i], xrecv.at[2 + i], place.partner["x"],
        )

    keep_mixed = copy_here(cot.at[own_rows, :], mixed_out.at[side], 4)
    modul_t[...] = ns[...].T

    def gather_ffn(g):
        cols = hid // 2
        return [
            Gatherer(
                place, lambda s: up_out.at[s, pl.ds(g * cols, cols)], width, UP_ORDER, fsend.at[g, 0], frecv.at[g, 0]
            ),
            Gatherer(
                place, lambda s: down_out.at[pl.ds(3 * g, 3), s, :], block, DOWN_ORDER, fsend.at[g, 1], frecv.at[g, 1]
            ),
        ]

    def gather_qkv(t, first, count):
        lanes = pl.ds((first - 1) * 128, count * 128)
        return Gatherer(
            place, lambda s: qkv_out.at[t, s, lanes], width, QKV_ORDERS[t],
            asend.at[first - 1, t], arecv.at[first - 1, t],
        )

    def gather_out(t):
        lanes = pl.ds(t * 128, 128)
        return Gatherer(
            place, lambda s: out_out.at[s, lanes], width, QKV_ORDERS[t], asend.at[1, t], arecv.at[1, t]
        )

    def put_pieces(gathers, sources):
        copies = [
            pltpu.make_async_copy(source, gather.span(0), local.at[8 + i])
            for i, (gather, source) in enumerate(zip(gathers, sources))
        ]
        for copy in copies:
            copy.start()
        for copy in copies:
            copy.wait()

    def gather_event(gathers, stage):
        for gather in gathers:
            if stage >= 0:
                gather.finish(stage)
            if stage + 1 < Gatherer.STAGES:
                gather.start(stage + 1)

    ffn = [gather_ffn(0), gather_ffn(1)]

    def start_ffn(g):
        cols = hid // 2
        put_pieces(ffn[g], [fin_up.at[:, pl.ds(g * cols, cols)], fin_down.at[pl.ds(3 * g, 3)]])
        gather_event(ffn[g], -1)

    outs = [gather_out(t) for t in range(3)]
    gathers = {c: [gather_qkv(t, c, 1) for t in range(3)] for c in (1, 2, 3)}

    def start_qkv(c):
        put_pieces(gathers[c], [fin_qkv.at[c - 1, t] for t in range(3)])
        gather_event(gathers[c], -1)

    def start_out():
        put_pieces(outs, [fin_out.at[t] for t in range(3)])
        gather_event(outs, -1)

    back_events = {}

    def at(t, event, *operands):
        back_events.setdefault(t, []).append(functools.partial(event, *operands))

    for t, moves in feed_schedule.items():
        for stage, c in moves:
            if t > 16:
                at(t, feed_event, stage, c)
    for c, times in ((0, (17, 20, 21, 22, 24)), (1, (22, 24, 25, 26, 28)), (2, (26, 28))):
        for stage, t in enumerate(times):
            at(t, move_event, stage, c)
    at(19, start_ffn, 0)
    for stage, t in enumerate((22, 25, 28)):
        at(t, gather_event, ffn[0], stage)
    at(23, start_ffn, 1)
    for stage, t in enumerate((26, 28)):
        at(t, gather_event, ffn[1], stage)
    at(24, start_out)
    for stage, t in enumerate((26, 28)):
        at(t, gather_event, outs, stage)
    at(28, lambda: start_qkv(1))

    def spread_event(stage):
        spread(stage).wait()
        if stage < 4:
            spread(stage + 1).start()

    for stage in range(5):
        at(18 + 2 * stage, spread_event, stage)
    for i in range(4):
        at(18 + 2 * i, lambda i: send_mixed(i).start(), i)

    def back_polls(step, which):
        for t, moves in back_events.items():
            if t >= 17 and (t - 17) % 2 == which:

                @pl.when(step == (t - 17) // 2)
                def _(moves=moves):
                    for move in moves:
                        move()

    def back(step, carry):
        pair = step // 2 + 3 * (step % 2)
        back_polls(step, 0)
        attend_back(
            pair, qs, ks, vs, os, dbranch, ls, segc, segr, cos_ref, sin_ref, acc,
            lambda: back_polls(step, 1),
        )
        for t, ref in enumerate((qs, ks, vs)):
            grad = dot_nn(modul_t[...], ref[pair]).astype(bf16)
            track(1 + step // 2, t)[step % 2] = grad

        @pl.when(step % 2 == 1)
        def _():
            for reducer in movers:
                reducer.start(0, 1 + step // 2)

        return carry

    lax.fori_loop(0, 6, back, 0)

    def gain_copy(stage):
        return remote(
            gains.at[stage], gains_in.at[stage], gsend.at[stage], grecv.at[stage],
            place.partner[ALL_AXES[stage]],
        )

    send_dtok = remote(modul.at[other_rows, :], dtok_out.at[side], xsend.at[6], xrecv.at[6], place.partner["x"])
    def gain_event(stage):
        gain_copy(stage).wait()
        total = gains[stage] + gains_in[stage]
        if stage < 4:
            gains[stage + 1] = total
            gain_copy(stage + 1).start()
        else:
            dgain_ref[...] = total

    def last_rows(i):
        b = ((1 - side) * (blocks // 2) + i) % blocks
        span = pl.ds(pl.multiple_of(b * rows, rows), rows)
        dnormed = jnp.zeros((rows, width), f32)
        for which, ref in enumerate((qs, ks, vs)):
            for group in range(2):
                grad = jnp.concatenate([ref[3 * group + p, span, :] for p in range(3)], axis=1)
                dnormed = dnormed + dot_nt(grad, wqs[group, which])
        normed, inverse = norm_parts(xs[span, :].astype(f32))
        gains[0, 0:1, :] += jnp.sum(dnormed * normed, axis=0, keepdims=True)
        modul[span, :] = (
            hidden[span, :] + norm_back(dnormed * gain_ref[...].reshape(1, -1), normed, inverse)
        ).astype(bf16)

    gains[0] = jnp.zeros(gains.shape[1:], f32)
    move_event(0, 3)
    move_event(2, 2)

    def after_rows(i):
        if i == 0:
            gather_event(gathers[1], 0)
            gather_event(ffn[0], 3)
        elif i == 1:
            move_event(1, 3)
            send_dtok.start()
            move_event(3, 2)
            gather_event(outs, 2)
        elif i == 2:
            gather_event(ffn[1], 2)
            gather_event(gathers[1], 1)

    def last_step(i, carry):
        last_rows(i)
        for k in range(blocks - 1):

            @pl.when(i == k)
            def _(k=k):
                after_rows(k)

        return carry

    lax.fori_loop(0, blocks, last_step, 0)
    move_event(2, 3)
    move_event(4, 2)
    start_qkv(2)
    gather_event(outs, 3)
    gain_copy(0).start()
    keep_dtok = copy_here(modul.at[own_rows, :], dtok_out.at[side], 5)
    gather_event(gathers[1], 2)
    embeddings = every[:, tiles, :]
    for tile in range(tiles):
        part = every[:, tile, :]
        lane = slice(tile * 128, tile * 128 + 128)
        line, start = tile * 128 // width, tile * 128 % width
        branch[line * TEMB : (line + 1) * TEMB, start : start + 128] = lax.dot_general(
            embeddings, part, (((0,), (0,)), ((), ())),
            preferred_element_type=f32, precision=lax.Precision.HIGHEST,
        )
        dbias_ref[0:1, lane] = jnp.sum(part, axis=0, keepdims=True)
    put_dada = copy_here(branch.at[pl.ds(0, 3 * TEMB), :], dada_out, 6)
    move_event(3, 3)
    gain_event(0)
    gather_event(ffn[1], 3)
    gather_event(gathers[1], 3)
    gather_event(gathers[2], 0)
    move_event(4, 3)
    start_qkv(3)
    gain_event(1)
    gather_event(gathers[2], 1)
    gather_event(gathers[3], 0)
    gain_event(2)
    gather_event(gathers[2], 2)
    gather_event(gathers[3], 1)
    gain_event(3)
    gather_event(gathers[2], 3)
    gather_event(gathers[3], 2)
    gather_event(gathers[3], 3)
    gain_event(4)
    for i in range(4):
        send_mixed(i).wait()
    keep_mixed.wait()
    send_dtok.wait()
    keep_dtok.wait()
    put_dada.wait()


def layer_call(tokens, cot, wq, wo, wu, wd, gain, segments, cosine, sine, embedding, ada, bias):
    length, width = 2 * tokens.shape[1], tokens.shape[2]
    half, hid = wq.shape[2], wu.shape[1]
    block = hid // FEED_STEPS
    pairs = width // 128
    any_ = pl.BlockSpec(memory_space=pl.ANY)
    vm = pl.BlockSpec(memory_space=pltpu.VMEM)
    shape = jax.ShapeDtypeStruct
    dma = pltpu.SemaphoreType.DMA
    low = lambda *dims: pltpu.VMEM(dims, bf16)
    full = lambda *dims: pltpu.VMEM(dims, f32)
    slots = (2, 4, 4, 4, 4)
    reducing = Reducer.scratch(slots, width, block, UP_ORDER)
    reducing += Reducer.scratch(slots, block, width, DOWN_ORDER)
    for order in QKV_ORDERS:
        reducing += Reducer.scratch((2,) * 5, width, 128, order)
    return pl.pallas_call(
        layer_kernel,
        in_specs=[any_] * 6 + [vm] * 7,
        out_specs=[any_] * 11 + [vm] * 2,
        out_shape=[
            shape(wq.shape, bf16),
            shape(wo.shape, bf16),
            shape(wu.shape, bf16),
            shape(wd.shape, bf16),
            shape((width, hid), bf16),
            shape((FEED_STEPS, block, width), bf16),
            shape((width, half), bf16),
            shape(wq.shape, bf16),
            shape((2, length // 2, width), bf16),
            shape((2, length // 2, width), bf16),
            shape((3 * TEMB, width), f32),
            shape((8, 3 * width), f32),
            shape((8, width), f32),
        ],
        scratch_shapes=[
            low(length, width),
            low(length, width),
            low(pairs, length, 128),
            low(pairs, length, 128),
            low(pairs, length, 128),
            low(length, width),
            full(pairs, 8, length),
            full(length, 128),
            low(2, *wq.shape),
            low(width, width),
            low(length, width),
            full(8, width),
            full(length, width),
            low(length, width),
            low(width, length),
            low(length, width),
            full(length, width),
            full(length, width),
            low(length, 2 * block),
            low(length, 2 * block),
            low(2, width, 2 * block),
            low(2, 2 * block, width),
            full(128, length),
            low(FEED_STEPS, 2, width, block),
            low(FEED_STEPS, 2, block, width),
            low(width // 16, hid),
            low(FEED_STEPS, block // 16, width),
            low(3, width // 16, 128),
            low(3, 3, width // 16, 128),
            full(32, 24, 128),
            full(5, 8, width),
            full(5, 8, width),
            dma((14,)),
            dma((7,)),
            dma((7,)),
            dma((10, 4)),
            dma((10, 4)),
            dma((2, 4)),
            dma((2, 2, 4)),
            dma((2, 2, 4)),
            dma((3, 3, 4)),
            dma((3, 3, 4)),
            dma((5,)),
            dma((5,)),
            dma((5,)),
            dma((5,)),
        ]
        + reducing,
        compiler_params=params(collective_id=0, has_side_effects=True),
        name="layer",
    )(tokens, cot, wq, wo, wu, wd, gain, segments, cosine, sine, embedding, ada, bias)


def finish_kernel(
    up_ref, down_ref, left_ref, right_ref, qkv_ref, mixed_ref, dtok_ref, dada_ref, dbias_ref, dgain_ref,
    up_out, down_out, out_out, qkv_out, mixed_out, dtok_out, dada_out, dbias_out, dgain_out,
):
    dbias_out[...] = dbias_ref[0, :]
    dgain_out[...] = dgain_ref[0, :]
    up_out[...] = up_ref[...].astype(f32)
    down_out[...] = down_ref[...].astype(f32)
    out_out[...] = jnp.concatenate([left_ref[...], right_ref[...]], axis=1).astype(f32)
    qkv_out[...] = qkv_ref[...].astype(f32)
    mixed_out[...] = mixed_ref[...]
    dtok_out[...] = dtok_ref[...]
    dada_out[...] = jnp.concatenate([dada_ref[i] for i in range(3)], axis=1)


def finish_call(up, down, out, qkv, mixed, dtok, dada, dbias, dgain):
    steps = 4
    shape = jax.ShapeDtypeStruct
    halves, half = out.shape[0] // 2, out.shape[1]

    def rows(a):
        return pl.BlockSpec((a.shape[0] // steps, a.shape[1]), lambda i: (i, 0))

    def middle(a):
        return pl.BlockSpec((a.shape[0], a.shape[1] // steps, a.shape[2]), lambda i: (0, i, 0))

    part = (halves // steps, half)
    outs = [
        shape(up.shape, f32),
        shape(down.shape, f32),
        shape((halves, 2 * half), f32),
        shape(qkv.shape, f32),
        shape(mixed.shape, bf16),
        shape(dtok.shape, bf16),
        shape((dada.shape[1], 3 * dada.shape[2]), f32),
        shape(dbias.shape[1:], f32),
        shape(dgain.shape[1:], f32),
    ]

    def placed(a):
        if len(a.shape) == 1:
            return pl.BlockSpec(a.shape, lambda i: (0,))
        return rows(a) if len(a.shape) == 2 else middle(a)

    def whole(a):
        return pl.BlockSpec(a.shape, lambda i: (0, 0))

    return pl.pallas_call(
        finish_kernel,
        grid=(steps,),
        in_specs=[
            rows(up),
            rows(down),
            pl.BlockSpec(part, lambda i: (i, 0)),
            pl.BlockSpec(part, lambda i: (i + steps, 0)),
            middle(qkv),
            middle(mixed),
            middle(dtok),
            middle(dada),
            whole(dbias),
            whole(dgain),
        ],
        out_specs=[placed(o) for o in outs],
        out_shape=outs,
        compiler_params=params(),
        name="finish",
    )(up, down, out, out, qkv, mixed, dtok, dada, dbias, dgain)


def time_embedding(timestep):
    half = TEMB // 2
    frequency = jnp.exp(-math.log(10000.0) * jnp.arange(half, dtype=f32) / half)
    angles = timestep.astype(f32)[:, None] * frequency[None, :]
    return jnp.concatenate([jnp.cos(angles), jnp.sin(angles)], axis=-1)


def per_device(
    groups, tokens, segment_ids, timestep, ln_gain, w_qkv, w_out, w_up, w_down, ada_weight, ada_bias, cotangent
):
    half, width = tokens.shape[1], tokens.shape[2]
    length = 2 * half
    cosine, sine = (jnp.asarray(a) for a in rotary_np(length))
    embedding = time_embedding(timestep)

    _, _, _, _, d_up, d_down, d_out, d_qkv, mixed, dtok, d_ada_weight, d_ada_bias, dgain = layer_call(
        tokens, cotangent, w_qkv, w_out, w_up, w_down, ln_gain, segment_ids, cosine, sine,
        embedding, ada_weight, ada_bias,
    )
    d_up, d_down, d_out, d_qkv, mixed, dtok, d_ada_weight, d_ada_bias, d_gain = finish_call(
        d_up, d_down.reshape(-1, width), d_out, d_qkv, mixed, dtok, d_ada_weight.reshape(3, TEMB, width),
        d_ada_bias, dgain,
    )

    def rest(a):
        bit = 16
        while bit < groups:
            a = a + lax.ppermute(a, "dp", [(i, i ^ bit) for i in range(groups)])
            bit *= 2
        return a

    return (
        mixed,
        dtok,
        rest(d_gain),
        rest(d_qkv),
        rest(d_out),
        rest(d_up),
        rest(d_down),
        rest(d_ada_weight),
        rest(d_ada_bias),
    )


def solution(mesh):
    in_specs = (
        P("dp", "tensor", None),
        P("dp", None),
        P("dp"),
        P(),
        P(None, None, "tensor"),
        P("tensor", None),
        P(None, "tensor"),
        P("tensor", None),
        P(),
        P(),
        P("dp", "tensor", None),
    )
    out_specs = (
        P("dp", "tensor", None),
        P("dp", "tensor", None),
        P(),
        P(None, None, "tensor"),
        P("tensor", None),
        P(None, "tensor"),
        P("tensor", None),
        P(),
        P(),
    )
    return jax.shard_map(
        functools.partial(per_device, mesh.shape["dp"]), mesh=mesh, in_specs=in_specs, out_specs=out_specs, check_vma=False
    )
```

```python
import functools
import math

import jax
import jax.numpy as jnp
import numpy as np
from jax import lax
from jax.experimental import pallas as pl
from jax.experimental.pallas import tpu as pltpu
from jax.sharding import PartitionSpec as P

HD = 64
TEMB = 128
EPS = 1e-05
MASKED = -1000000000.0
f32 = jnp.float32
bf16 = jnp.bfloat16
VMEM_LIMIT = 62 * 1024 * 1024


def dot_nn(a, b):
    return lax.dot_general(a, b, (((1,), (0,)), ((), ())), preferred_element_type=f32)


def dot_nt(a, b):
    return lax.dot_general(a, b, (((1,), (1,)), ((), ())), preferred_element_type=f32)


def dot_tn(a, b):
    return lax.dot_general(a, b, (((0,), (0,)), ((), ())), preferred_element_type=f32)


def norm_parts(values):
    centred = values - jnp.mean(values, axis=-1, keepdims=True)
    variance = jnp.mean(centred * centred, axis=-1, keepdims=True)
    inverse = lax.rsqrt(variance + EPS)
    return centred * inverse, inverse


def norm_back(grad, normed, inverse):
    return inverse * (
        grad
        - jnp.mean(grad, axis=-1, keepdims=True)
        - normed * jnp.mean(grad * normed, axis=-1, keepdims=True)
    )


def rotary_np(length):
    half = HD // 2
    position = np.arange(length, dtype=np.float32)
    frequency = (10000.0 ** (-np.arange(half, dtype=np.float32) / half)).astype(np.float32)
    angles = position[:, None] * frequency[None, :]
    cosine, sine = np.cos(angles), np.sin(angles)
    cosine = np.concatenate([cosine, cosine] * 2, axis=1).astype(np.float32)
    sine = np.concatenate([-sine, sine] * 2, axis=1).astype(np.float32)
    return cosine, sine


def swap_halves(values):
    lane = lax.broadcasted_iota(jnp.int32, values.shape, 1)
    first = (lane % HD) < (HD // 2)
    return jnp.where(first, pltpu.roll(values, 128 - HD // 2, 1), pltpu.roll(values, HD // 2, 1))


def params(**kw):
    return pltpu.CompilerParams(vmem_limit_bytes=VMEM_LIMIT, **kw)


def cost(flops, nbytes, trans=0):
    return pl.CostEstimate(flops=int(flops), bytes_accessed=int(nbytes), transcendentals=int(trans))


BITS = {"core": 1, "y": 2, "zl": 4, "zh": 8}
MESH = pl.DeviceIdType.MESH


class Place:
    def __init__(self):
        self.me = lax.axis_index("dp")
        self.side = lax.axis_index("tensor")
        self.bit = {axis: (self.me // bit) % 2 for axis, bit in BITS.items()}
        self.partner = {
            axis: {"dp": self.me + bit * (1 - 2 * self.bit[axis])} for axis, bit in BITS.items()
        }
        self.partner["x"] = {"tensor": 1 - self.side}

    def greet(self, axes):
        barrier = pltpu.get_barrier_semaphore()
        for axis in axes:
            pl.semaphore_signal(barrier, inc=1, device_id=self.partner[axis], device_id_type=MESH)
        pl.semaphore_wait(barrier, len(axes))


ALL_AXES = ("core", "y", "zl", "zh", "x")


def remote(src, dst, send, recv, partner):
    return pltpu.make_async_remote_copy(
        src_ref=src, dst_ref=dst, send_sem=send, recv_sem=recv, device_id=partner, device_id_type=MESH
    )


class Reducer:
    STAGES = 5

    def __init__(self, place, view, rows, refs, order):
        self.place, self.view, self.order = place, view, order
        self.received, self.sends, self.recvs = refs[:5], refs[5], refs[6]
        self.cross = order.index("x")
        base, n = 0, rows
        self.spans = []
        for axis in order:
            if axis == "x":
                span = pl.ds(pl.multiple_of(base, 16), n)
                self.spans.append((span, span))
            else:
                n //= 2
                bit = place.bit[axis]
                keep = pl.ds(pl.multiple_of(base + bit * n, 16), n)
                send = pl.ds(pl.multiple_of(base + (1 - bit) * n, 16), n)
                self.spans.append((keep, send))
                base = base + bit * n

    @staticmethod
    def scratch(counts, rows, cols, order):
        shapes, n, cross = [], rows, False
        for slots, axis in zip(counts, order):
            if axis == "x":
                cross = True
            else:
                n //= 2
            shapes.append((slots, n, cols) if cross else (slots, 2, n, cols))
        return [pltpu.VMEM(shape, bf16) for shape in shapes] + [pltpu.SemaphoreType.DMA((sum(counts),))] * 2

    def slot(self, stage, c):
        return self.received[stage].at[c % self.received[stage].shape[0]]

    def flag(self, stage, c):
        before = sum(self.received[s].shape[0] for s in range(stage))
        return before + c % self.received[stage].shape[0]

    def copy(self, stage, c):
        send = self.spans[stage][1]
        if stage < self.cross:
            source = self.view(c).at[:, send, :]
        else:
            source = self.view(c).at[1 if stage == self.cross else 0, send, :]
        return remote(
            source,
            self.slot(stage, c),
            self.sends.at[self.flag(stage, c)],
            self.recvs.at[self.flag(stage, c)],
            self.place.partner[self.order[stage]],
        )

    def start(self, stage, c):
        self.copy(stage, c).start()

    def finish(self, stage, c, put=None):
        self.copy(stage, c).wait()
        keep = self.spans[stage][0]
        came, chunk = self.slot(stage, c), self.view(c)
        if stage < self.cross:
            for half in range(2):
                chunk[half, keep, :] += came[half]
        elif stage < 4:
            chunk[0, keep, :] += came[...]
        else:
            put(c, chunk[0, keep, :] + came[...])

    def step(self, stage, c, put=None):
        self.finish(stage, c, put)
        if stage + 1 < self.STAGES:
            self.start(stage + 1, c)


class Gatherer:
    STAGES = 4

    def __init__(self, place, view, rows, order, sends, recvs):
        self.place, self.view, self.sends, self.recvs = place, view, sends, recvs
        self.order = [axis for axis in order if axis != "x"][::-1]
        self.size = rows // 16
        bits = [place.bit[axis] for axis in self.order]
        self.bases = [sum(bits[j] * 2**j for j in range(stage, 4)) for stage in range(4)]

    def span(self, stage):
        n = self.size
        return self.view(pl.ds(pl.multiple_of(self.bases[stage] * n, 16), 2**stage * n))

    def copy(self, stage):
        span = self.span(stage)
        return remote(
            span, span, self.sends.at[stage], self.recvs.at[stage], self.place.partner[self.order[stage]]
        )

    def start(self, stage):
        self.copy(stage).start()

    def finish(self, stage):
        self.copy(stage).wait()


class Fetch:
    def __init__(self, place, own, other, rows, axes, sends, recvs):
        self.place, self.own, self.other, self.axes = place, own, other, axes
        self.sends, self.recvs = sends, recvs
        self.size = rows // 2 ** len(axes)
        bits = [place.bit[axis] for axis in axes]
        self.bases = [sum(bits[j] * 2**j for j in range(s, len(axes))) for s in range(len(axes))]

    def copy(self, stage):
        level = max(stage - 1, 0)
        n = self.size
        span = pl.ds(pl.multiple_of(self.bases[level] * n, 16), 2**level * n)
        source = self.own(span) if stage == 0 else self.other(span)
        axis = "x" if stage == 0 else self.axes[stage - 1]
        return remote(
            source, self.other(span), self.sends.at[stage], self.recvs.at[stage], self.place.partner[axis]
        )

    def start(self, stage):
        self.copy(stage).start()

    def step(self, stage):
        self.copy(stage).wait()
        if stage < len(self.axes):
            self.copy(stage + 1).start()


def qkv_rows(row, rows, x_ref, gain_ref, w_ref, cos_ref, sin_ref, n_ref, q_ref, k_ref, v_ref, first):
    span = pl.ds(row, rows)
    pairs = w_ref.shape[2] // 128
    if n_ref is None:
        normed = x_ref[span, :]
    else:
        normed, _ = norm_parts(x_ref[span, :].astype(f32))
        normed = (normed * gain_ref[...].reshape(1, -1)).astype(bf16)
        n_ref[span, :] = normed
    cosine, sine = cos_ref[span, :], sin_ref[span, :]
    for which, out in ((0, q_ref), (1, k_ref)):
        raw = dot_nn(normed, w_ref[which])
        for pair in range(pairs):
            part = raw[:, pair * 128 : pair * 128 + 128]
            turned = (part * cosine + swap_halves(part) * sine).astype(bf16)
            if which == 0:
                turned = turned * jnp.asarray(0.125, bf16)
            out[first + pair, span, :] = turned
    raw = dot_nn(normed, w_ref[2]).astype(bf16)
    for pair in range(pairs):
        v_ref[first + pair, span, :] = raw[:, pair * 128 : pair * 128 + 128]


EDGE = 256


def mask_scores(scores, inner, column, segr):
    length = scores.shape[1]
    last = length - EDGE
    middle = segr[:, length // 2 : length // 2 + 128]
    if inner:
        bias = jnp.where(jnp.concatenate([middle] * (length // 128), axis=1) == segr, 0.0, MASKED)
        parts = [scores[:, :EDGE] + bias[:, :EDGE], scores[:, EDGE:last], scores[:, last:] + bias[:, last:]]
    else:
        wide = jnp.concatenate([column] * (EDGE // 128), axis=1)
        inside = column == middle
        parts = (
            [jnp.where(wide == segr[:, :EDGE], scores[:, :EDGE], MASKED)]
            + [jnp.where(inside, scores[:, j : j + 128], MASKED) for j in range(EDGE, last, 128)]
            + [jnp.where(wide == segr[:, last:], scores[:, last:], MASKED)]
        )
    return jnp.concatenate(parts, axis=1)


def attend_rows(pair, spans, q_ref, k_ref, v_ref, segc_ref, segr, o_ref, lse_ref):
    lane = lax.broadcasted_iota(jnp.int32, (1, 128), 1)
    low = lane < HD
    mine = (low, jnp.logical_not(low))
    k, v = k_ref[pair], v_ref[pair]
    one = jnp.ones_like(v)
    values = [jnp.where(m, v, one) for m in mine]
    units = [(span, inner, head) for span, inner in spans for head in range(2)]

    def score(unit):
        span, _, head = unit
        q = q_ref[pair, span, :]
        return dot_nt(jnp.where(mine[head], q, jnp.zeros_like(q)), k)

    ahead = 2
    scores = [score(unit) for unit in units[:ahead]]
    parts = []
    for i, (span, inner, head) in enumerate(units):
        if i + ahead < len(units):
            scores.append(score(units[i + ahead]))
        masked = mask_scores(scores[i], inner, segc_ref[span, :], segr)
        largest = jnp.max(masked, axis=1, keepdims=True)
        weights = jnp.exp(masked - largest).astype(bf16)
        mixed = dot_nn(weights, values[head])
        total = pltpu.roll(mixed, HD, 1)
        parts.append((mixed / total, largest + jnp.log(total)))
        if head == 1:
            (out0, lse0), (out1, lse1) = parts[-2:]
            o_ref[span, pl.ds(pl.multiple_of(pair * 128, 128), 128)] = jnp.where(low, out0, out1).astype(bf16)
            lse = jnp.where(low, lse0, lse1).T
            lse_ref[pair, 0:1, span] = lse[0:1, :]
            lse_ref[pair, 1:2, span] = lse[HD : HD + 1, :]


def gelu_both(u):
    c0 = math.sqrt(2.0 / math.pi)
    square = u * u
    t = jnp.tanh(u * (c0 + (c0 * 0.044715) * square))
    half = 0.5 + 0.5 * t
    act = u * half
    slope = half + (0.5 * u) * (1.0 - t * t) * (c0 + (3.0 * c0 * 0.044715) * square)
    return act, slope


FEED_STEPS = 6
UP_ORDER = ("core", "y", "zl", "x", "zh")
DOWN_ORDER = ("core", "x", "zl", "y", "zh")
QKV_ORDERS = (
    ("core", "y", "x", "zl", "zh"),
    ("core", "x", "y", "zl", "zh"),
    ("core", "zl", "x", "y", "zh"),
)


def attend_back(
    pair, q_ref, k_ref, v_ref, o_ref, do_ref, lse_ref, segc_ref, segr, cos_ref, sin_ref, acc_ref, poll
):
    length = o_ref.shape[0]
    rows = 256
    lane = lax.broadcasted_iota(jnp.int32, (1, 128), 1)
    low = lane < HD
    lanes = pl.ds(pl.multiple_of(pair * 128, 128), 128)
    q, do = q_ref[pair], do_ref[:, lanes]
    product = do.astype(f32) * o_ref[:, lanes].astype(f32)
    high_part = product.astype(bf16)
    low_part = (product - high_part.astype(f32)).astype(bf16)
    row8 = lax.broadcasted_iota(jnp.int32, (8, 128), 0)
    lane8 = lax.broadcasted_iota(jnp.int32, (8, 128), 1)
    select = jnp.where((lane8 // HD) == row8, 1.0, 0.0).astype(bf16)
    delta = dot_nt(select, high_part) + dot_nt(select, low_part)
    lse = lse_ref[pair]
    zero = jnp.zeros_like(q)
    q_heads = (jnp.where(low, q, zero), jnp.where(low, zero, q))
    do_heads = (jnp.where(low, do, zero), jnp.where(low, zero, do))
    acc_ref[...] = jnp.zeros_like(acc_ref)
    mine = (low, jnp.logical_not(low))
    blocks = length // rows
    for group in range(2):
        if group == 1:
            poll()
        units = [(block, head) for block in (3 * group, 1 + group) for head in range(2)]

        def products(unit):
            block, head = unit
            span = pl.ds(block * rows, rows)
            k, v = k_ref[pair, span, :], v_ref[pair, span, :]
            kh = jnp.where(mine[head], k, jnp.zeros_like(k))
            vh = jnp.where(mine[head], v, jnp.zeros_like(v))
            return kh, dot_nt(kh, q), dot_nt(vh, do)

        ahead = 1
        ready = [products(unit) for unit in units[:ahead]]
        dq = jnp.zeros((128, length), f32)
        for i, (block, head) in enumerate(units):
            if i + ahead < len(units):
                ready.append(products(units[i + ahead]))
            kh, scores, d_probs = ready[i]
            span = pl.ds(block * rows, rows)
            inner = block * rows >= EDGE and (block + 1) * rows <= length - EDGE
            scores = mask_scores(scores, inner, segc_ref[span, :], segr)
            probs = jnp.exp(scores - lse[head : head + 1, :])
            part_v = dot_nn(probs.astype(bf16), do_heads[head])
            d_scores = (probs * (d_probs - delta[head : head + 1, :])).astype(bf16)
            part_k = dot_nn(d_scores, q_heads[head])
            dq = dq + dot_tn(kh, d_scores)
            if head == 0:
                dv, dk = part_v, part_k
            else:
                dv, dk = dv + part_v, dk + part_k
                cosine, sine = cos_ref[span, :], sin_ref[span, :]
                k_ref[pair, span, :] = (dk * cosine - swap_halves(dk) * sine).astype(bf16)
                v_ref[pair, span, :] = dv.astype(bf16)
        acc_ref[...] += dq
    dq = acc_ref[...].T * 0.125
    q_ref[pair] = (dq * cos_ref[...] - swap_halves(dq) * sin_ref[...]).astype(bf16)


SPREAD_ORDER = ("zh", "zl", "y", "x", "core")


def layer_kernel(
    tok, cot_in, wq, wo, wu, wd, gain_ref, seg_ref, cos_ref, sin_ref, emb_ref, ada_ref, bias_ref,
    oq, oo, ou, od, up_out, down_out, out_out, qkv_out, mixed_out, dtok_out, dada_out, dbias_ref, dgain_ref,
    xs, ns, qs, ks, vs, os, ls, segc, wqs, wos, cot, mod,
    hidden, modul, modul_t, dbranch, branch, dmod, acts, dups, upbuf, downbuf, acc,
    ups, downs, fin_up, fin_down, fin_out, fin_qkv, every, gains, gains_in,
    local, xsend, xrecv, wsend, wrecv, loads,
    fsend, frecv, asend, arecv, gsend, grecv, ssend, srecv, *reducing,
):
    place = Place()
    side = place.side
    length, width = xs.shape
    half = length // 2
    rows = 256
    blocks = length // rows
    block = wu.shape[1] // FEED_STEPS
    heads = wo.shape[0]
    hid = wu.shape[1]
    tiles = 3 * width // 128
    own_rows = pl.ds(pl.multiple_of(side * half, half), half)
    other_rows = pl.ds(pl.multiple_of((1 - side) * half, half), half)

    def copy_here(src, dst, index):
        copy = pltpu.make_async_copy(src, dst, local.at[index])
        copy.start()
        return copy

    place.greet(ALL_AXES)
    send_tok = remote(tok.at[1 - side], xs.at[own_rows, :], xsend.at[0], xrecv.at[0], place.partner["x"])
    send_cot = remote(cot_in.at[1 - side], cot.at[own_rows, :], xsend.at[1], xrecv.at[1], place.partner["x"])

    def up_view(g):
        return lambda r, s: r.at[s, pl.ds(g * hid // 3, hid // 3)]

    def down_view(g):
        return lambda r, s: r.at[pl.ds(g * hid // 3, hid // 3)].at[s, :]

    plan = (
        (lambda r, s: r.at[2, s, :], wq, oq, width, ("y", "zl", "core")),
        (lambda r, s: r.at[0, s, :], wq, oq, width, ("y", "core")),
        (lambda r, s: r.at[1, s, :], wq, oq, width, ("zl", "core")),
        (lambda r, s: r.at[s, :], wo, oo, heads, ("y", "zl", "core")),
        (up_view(0), wu, ou, width, ("y", "zl", "core")),
        (down_view(0), wd, od, hid // 3, ("zl", "y", "core")),
        (up_view(1), wu, ou, width, ("y", "zl", "core")),
        (down_view(1), wd, od, hid // 3, ("zl", "y", "core")),
        (up_view(2), wu, ou, width, ("y", "zl", "core")),
        (down_view(2), wd, od, hid // 3, ("zl", "y", "core")),
    )
    V, Q, K, OUT, UP0, DN0, UP1, DN1, UP2, DN2 = range(10)
    fetches = [
        Fetch(place, functools.partial(view, own), functools.partial(view, other), n, axes, wsend.at[i], wrecv.at[i])
        for i, (view, own, other, n, axes) in enumerate(plan)
    ]
    send_tok.start()
    for index in (V, Q, K, OUT, UP0, DN0, UP1, DN1):
        fetches[index].start(0)
    send_cot.start()
    for index in (UP2, DN2):
        fetches[index].start(0)

    get_x = copy_here(tok.at[side], xs.at[own_rows, :], 0)
    get_w = copy_here(wq, wqs.at[0], 1)
    get_cot = copy_here(cot_in.at[side], cot.at[own_rows, :], 2)
    get_wo = copy_here(wo, wos.at[pl.ds(0, heads), :], 3)

    segr = seg_ref[pl.ds(side, 1), :].astype(f32)
    segc[...] = jnp.broadcast_to(segr, (128, length)).T
    emb = jnp.broadcast_to(emb_ref[pl.ds(side, 1), :], (TEMB, TEMB)).T
    for tile in range(tiles):
        span = slice(tile * 128, tile * 128 + 128)
        value = jnp.sum(emb * ada_ref[:, span].astype(f32), axis=0, keepdims=True) + bias_ref[span].reshape(1, -1)
        start = tile * 128 % width
        mod[tile * 128 // width : tile * 128 // width + 1, start : start + 128] = value
    get_x.wait()
    get_w.wait()

    def qkv_half(base, w_ref, w_first, n_ref):
        def step(i, carry):
            row = pl.multiple_of(base + i * rows, rows)
            qkv_rows(
                row, rows, xs if n_ref is not None else ns, gain_ref, w_ref, cos_ref, sin_ref,
                n_ref, qs, ks, vs, w_first,
            )
            return carry

        lax.fori_loop(0, half // rows, step, 0)

    qkv_half(side * half, wqs.at[0], 0, ns)
    send_tok.wait()
    qkv_half((1 - side) * half, wqs.at[0], 0, ns)

    per_pair = 2
    steps = 6 * per_pair
    events = {
        0: ((V, 0),),
        2: ((V, 1), (Q, 0)),
        3: ((K, 0),),
        4: ((OUT, 0),),
        5: ((V, 2), (Q, 1), (UP0, 0)),
        6: ((OUT, 1), (UP0, 1), (DN0, 1)),
        7: ((UP1, 0), (DN1, 0)),
        10: ((DN0, 2), (OUT, 2)),
        11: ((UP0, 2), (UP1, 1)),
    }

    def attend(step, carry):
        pair = step // per_pair

        @pl.when(step == steps // 2)
        def _():
            fetches[K].step(1)
            fetches[DN0].step(0)
            for index in (V, Q, K):
                fetches[index].step(len(fetches[index].axes))
            copy = copy_here(oq, wqs.at[1], 1)
            copy.wait()
            qkv_half(0, wqs.at[1], 3, None)
            qkv_half(half, wqs.at[1], 3, None)

        for at, moves in events.items():

            @pl.when(step == at)
            def _(moves=moves):
                for index, stage in moves:
                    fetches[index].step(stage)

        part = step % per_pair
        edge = pl.ds(pl.multiple_of(part * (length - rows), rows), rows)
        inner = pl.ds(pl.multiple_of((1 + part) * rows, rows), rows)
        attend_rows(pair, ((edge, False), (inner, True)), qs, ks, vs, segc, segr, os, ls)
        return carry

    lax.fori_loop(0, steps, attend, 0)

    def load_weights(step):
        slot = step % 2
        span = pl.ds(pl.multiple_of(step * block, 128), block)
        return [
            pltpu.make_async_copy(wu.at[:, span], upbuf.at[slot, :, pl.ds(0, block)], loads.at[slot, 0]),
            pltpu.make_async_copy(ou.at[:, span], upbuf.at[slot, :, pl.ds(block, block)], loads.at[slot, 1]),
            pltpu.make_async_copy(wd.at[span, :], downbuf.at[slot, pl.ds(0, block), :], loads.at[slot, 2]),
            pltpu.make_async_copy(od.at[span, :], downbuf.at[slot, pl.ds(block, block), :], loads.at[slot, 3]),
        ]

    fetches[OUT].step(3)
    get_wo.wait()
    copy_here(oo, wos.at[pl.ds(heads, heads), :], 3).wait()
    get_cot.wait()
    fetches[DN1].step(1)
    fetches[UP0].step(3)
    fetches[DN0].step(3)
    for copy in load_weights(0):
        copy.start()

    def middle(i, carry):
        span = pl.ds(pl.multiple_of(i * rows, rows), rows)
        shift, scale = mod[0:1, :], mod[1:2, :]
        h = xs[span, :].astype(f32) + dot_nn(os[span, :], wos[...])
        hidden[span, :] = h
        normed, _ = norm_parts(h)
        m = (normed * (1.0 + scale) + shift).astype(bf16)
        modul[span, :] = m
        modul_t[:, span] = m.T
        branch[span, :] = jnp.zeros((rows, width), f32)
        dmod[span, :] = jnp.zeros((rows, width), f32)
        return carry

    lax.fori_loop(0, blocks, middle, 0)

    def to_branch(part):
        span = own_rows if part == 0 else other_rows
        dbranch[span, :] = (cot[span, :].astype(f32) * mod[2:3, :]).astype(bf16)

    to_branch(0)
    send_cot.wait()
    to_branch(1)

    def track(c, t):
        if isinstance(c, int) and c == 0:
            return upbuf.at[:, :, pl.ds(t * 128, 128)]
        index = 3 * (c - 1) + t
        return ups.at[index // 2, :, :, pl.ds(pl.multiple_of((index % 2) * 128, 128), 128)]

    feeders = [
        Reducer(place, lambda c: ups.at[c], width, reducing[0:7], UP_ORDER),
        Reducer(place, lambda c: downs.at[c], block, reducing[7:14], DOWN_ORDER),
    ]
    movers = [
        Reducer(
            place, functools.partial(track, t=t), width, reducing[14 + 7 * t : 21 + 7 * t], QKV_ORDERS[t]
        )
        for t in range(3)
    ]

    def put_up(c, value):
        fin_up[:, pl.ds(pl.multiple_of(c * block, 128), block)] = value

    def put_down(c, value):
        fin_down[c] = value

    def feed_event(stage, c):
        for reducer, put in zip(feeders, (put_up, put_down)):
            reducer.step(stage, c, put)

    def put_final(t):
        def put(c, value):
            if c == 0:
                fin_out[t] = value
            else:
                fin_qkv[c - 1, t] = value

        return put

    def move_event(stage, c):
        for t, reducer in enumerate(movers):
            reducer.step(stage, c, put_final(t))

    FIRST = (3, 6, 9)
    LATER = {
        0: {3: 12, 4: 15},
        1: {3: 14, 4: 17},
        2: {2: 13, 3: 16, 4: 18},
        3: {1: 12, 2: 16, 3: 18, 4: 20},
        4: {1: 14, 2: 18, 3: 20, 4: 22},
        5: {0: 13, 1: 18, 2: 20, 3: 22, 4: 23},
    }

    def feed_polls(t, stages):
        for stage in stages:
            since = t - FIRST[stage]

            @pl.when(since >= 0)
            def _(stage=stage, c=since // 2):
                feed_event(stage, c)

    def feed(step, carry):
        feed_polls(2 * step, (1,))
        @pl.when(step == 1)
        def _():
            fetches[UP1].step(3)
            fetches[DN1].step(3)

        @pl.when(step == 3)
        def _():
            fetches[UP2].step(2)
            fetches[DN2].step(2)

        for copy in load_weights(step):
            copy.wait()

        slot = step % 2
        up, down = upbuf.at[slot], downbuf.at[slot]
        for i in range(blocks):
            span = pl.ds(i * rows, rows)
            u = dot_nn(modul[span, :], up[...])
            act, slope = gelu_both(u)
            act = act.astype(bf16)
            acts[span, :] = act
            d_act = dot_nt(dbranch[span, :], down[...])
            d_up = (d_act * slope).astype(bf16)
            dups[span, :] = d_up
            branch[span, :] += dot_nn(act, down[...])
            dmod[span, :] += dot_nt(d_up, up[...])
        feed_polls(2 * step + 1, (2, 0))

        @pl.when(step == 0)
        def _():
            fetches[UP1].step(2)
            fetches[DN1].step(2)
            fetches[UP2].step(0)
            fetches[DN2].step(0)

        @pl.when(step == 1)
        def _():
            fetches[UP2].step(1)
            fetches[DN2].step(1)

        @pl.when(step == 3)
        def _():
            fetches[UP2].step(3)
            fetches[DN2].step(3)

        @pl.when(step + 1 < FEED_STEPS)
        def _():
            for copy in load_weights(step + 1):
                copy.start()

        grad = dot_nn(modul_t[...], dups[...]).astype(bf16)
        ups[step, 0] = grad[:, :block]
        ups[step, 1] = grad[:, block:]
        feeders[0].start(0, step)
        grad = dot_tn(acts[...], dbranch[...]).astype(bf16)
        downs[step, 0] = grad[:block]
        downs[step, 1] = grad[block:]
        feeders[1].start(0, step)
        return carry

    lax.fori_loop(0, FEED_STEPS, feed, 0)

    feed_schedule = {}
    for c, ends in LATER.items():
        for stage, t in ends.items():
            feed_schedule.setdefault(t, []).append((stage, c))

    def feed_static(t):
        for stage, c in feed_schedule.get(t, []):
            feed_event(stage, c)

    sums = dgain_ref
    sums[...] = jnp.zeros_like(sums)
    def between(i, carry):
        for k in range(blocks):

            @pl.when(i == k)
            def _(k=k):
                feed_static(2 * FEED_STEPS + k)

        span = pl.ds(pl.multiple_of(i * rows, rows), rows)
        scale, gate = mod[1:2, :], mod[2:3, :]
        h = hidden[span, :]
        dout = cot[span, :].astype(f32)
        br = branch[span, :]
        cot[span, :] = (h + gate * br).astype(bf16)
        normed, inverse = norm_parts(h)
        dm = dmod[span, :]
        sums[0:1, :] += jnp.sum(dm, axis=0, keepdims=True)
        sums[1:2, :] += jnp.sum(dm * normed, axis=0, keepdims=True)
        sums[2:3, :] += jnp.sum(dout * br, axis=0, keepdims=True)
        dh = dout + norm_back(dm * (1.0 + scale), normed, inverse)
        hidden[span, :] = dh
        dattn = dh.astype(bf16)
        modul[span, :] = dattn
        dbranch[span, :] = dot_nt(dattn, wos[...]).astype(bf16)
        return carry

    lax.fori_loop(0, blocks, between, 0)
    grad = dot_tn(os[...], modul[...]).astype(bf16)
    for t in range(3):
        chunk = track(0, t)
        for i in range(2):
            part = grad[i * heads : (i + 1) * heads]
            chunk[i, :heads, :] = part[:, t * 128 : t * 128 + 128]
            chunk[i, heads:, :] = part[:, heads + t * 128 : heads + t * 128 + 128]
        movers[t].start(0, 0)
    feed_static(16)

    number = sum(
        (side if axis == "x" else place.bit[axis]) * 2**i for i, axis in enumerate(SPREAD_ORDER)
    )
    every[pl.ds(number, 1)] = jnp.zeros((1,) + every.shape[1:], f32)
    for tile in range(tiles):
        line, lane = tile * 128 // width, tile * 128 % width
        every[pl.ds(number, 1), tile : tile + 1, :] = sums[line : line + 1, lane : lane + 128][None]
    every[pl.ds(number, 1), tiles : tiles + 1, :] = emb_ref[pl.ds(side, 1), :][None]

    def spread(stage):
        span = every.at[pl.ds(number - number % 2**stage, 2**stage)]
        return remote(span, span, ssend.at[stage], srecv.at[stage], place.partner[SPREAD_ORDER[stage]])

    spread(0).start()

    def send_mixed(i):
        n = half // 4
        span = pl.ds(pl.multiple_of((1 - side) * half + i * n, n), n)
        return remote(
            cot.at[span, :], mixed_out.at[side, pl.ds(i * n, n), :],
            xsend.at[2 + i], xrecv.at[2 + i], place.partner["x"],
        )

    keep_mixed = copy_here(cot.at[own_rows, :], mixed_out.at[side], 4)
    modul_t[...] = ns[...].T

    def gather_ffn(g):
        cols = hid // 2
        return [
            Gatherer(
                place, lambda s: up_out.at[s, pl.ds(g * cols, cols)], width, UP_ORDER, fsend.at[g, 0], frecv.at[g, 0]
            ),
            Gatherer(
                place, lambda s: down_out.at[pl.ds(3 * g, 3), s, :], block, DOWN_ORDER, fsend.at[g, 1], frecv.at[g, 1]
            ),
        ]

    def gather_qkv(t, first, count):
        lanes = pl.ds((first - 1) * 128, count * 128)
        return Gatherer(
            place, lambda s: qkv_out.at[t, s, lanes], width, QKV_ORDERS[t],
            asend.at[first - 1, t], arecv.at[first - 1, t],
        )

    def gather_out(t):
        lanes = pl.ds(t * 128, 128)
        return Gatherer(
            place, lambda s: out_out.at[s, lanes], width, QKV_ORDERS[t], asend.at[1, t], arecv.at[1, t]
        )

    def put_pieces(gathers, sources):
        copies = [
            pltpu.make_async_copy(source, gather.span(0), local.at[8 + i])
            for i, (gather, source) in enumerate(zip(gathers, sources))
        ]
        for copy in copies:
            copy.start()
        for copy in copies:
            copy.wait()

    def gather_event(gathers, stage):
        for gather in gathers:
            if stage >= 0:
                gather.finish(stage)
            if stage + 1 < Gatherer.STAGES:
                gather.start(stage + 1)

    ffn = [gather_ffn(0), gather_ffn(1)]

    def start_ffn(g):
        cols = hid // 2
        put_pieces(ffn[g], [fin_up.at[:, pl.ds(g * cols, cols)], fin_down.at[pl.ds(3 * g, 3)]])
        gather_event(ffn[g], -1)

    outs = [gather_out(t) for t in range(3)]
    gathers = {c: [gather_qkv(t, c, 1) for t in range(3)] for c in (1, 2, 3)}

    def start_qkv(c):
        put_pieces(gathers[c], [fin_qkv.at[c - 1, t] for t in range(3)])
        gather_event(gathers[c], -1)

    def start_out():
        put_pieces(outs, [fin_out.at[t] for t in range(3)])
        gather_event(outs, -1)

    back_events = {}

    def at(t, event, *operands):
        back_events.setdefault(t, []).append(functools.partial(event, *operands))

    for t, moves in feed_schedule.items():
        for stage, c in moves:
            if t > 16:
                at(t, feed_event, stage, c)
    for c, times in ((0, (17, 20, 21, 22, 24)), (1, (22, 24, 25, 26, 28)), (2, (26, 28))):
        for stage, t in enumerate(times):
            at(t, move_event, stage, c)
    at(19, start_ffn, 0)
    for stage, t in enumerate((22, 25, 28)):
        at(t, gather_event, ffn[0], stage)
    at(23, start_ffn, 1)
    at(26, gather_event, ffn[1], 0)
    at(24, start_out)
    for stage, t in enumerate((26, 28)):
        at(t, gather_event, outs, stage)
    at(28, lambda: start_qkv(1))

    def spread_event(stage):
        spread(stage).wait()
        if stage < 4:
            spread(stage + 1).start()

    for stage in range(5):
        at(18 + 2 * stage, spread_event, stage)
    for i in range(4):
        at(18 + 2 * i, lambda i: send_mixed(i).start(), i)

    def back_polls(step, which):
        for t, moves in back_events.items():
            if t >= 17 and (t - 17) % 2 == which:

                @pl.when(step == (t - 17) // 2)
                def _(moves=moves):
                    for move in moves:
                        move()

    def back(step, carry):
        pair = step // 2 + 3 * (step % 2)
        back_polls(step, 0)
        attend_back(
            pair, qs, ks, vs, os, dbranch, ls, segc, segr, cos_ref, sin_ref, acc,
            lambda: back_polls(step, 1),
        )
        for t, ref in enumerate((qs, ks, vs)):
            grad = dot_nn(modul_t[...], ref[pair]).astype(bf16)
            track(1 + step // 2, t)[step % 2] = grad

        @pl.when(step % 2 == 1)
        def _():
            for reducer in movers:
                reducer.start(0, 1 + step // 2)

        return carry

    lax.fori_loop(0, 6, back, 0)

    def gain_copy(stage):
        return remote(
            gains.at[stage], gains_in.at[stage], gsend.at[stage], grecv.at[stage],
            place.partner[ALL_AXES[stage]],
        )

    send_dtok = remote(modul.at[other_rows, :], dtok_out.at[side], xsend.at[6], xrecv.at[6], place.partner["x"])
    def gain_event(stage):
        gain_copy(stage).wait()
        total = gains[stage] + gains_in[stage]
        if stage < 4:
            gains[stage + 1] = total
            gain_copy(stage + 1).start()
        else:
            dgain_ref[...] = total

    def last_rows(i):
        b = ((1 - side) * (blocks // 2) + i) % blocks
        span = pl.ds(pl.multiple_of(b * rows, rows), rows)
        dnormed = jnp.zeros((rows, width), f32)
        for which, ref in enumerate((qs, ks, vs)):
            for group in range(2):
                grad = jnp.concatenate([ref[3 * group + p, span, :] for p in range(3)], axis=1)
                dnormed = dnormed + dot_nt(grad, wqs[group, which])
        normed, inverse = norm_parts(xs[span, :].astype(f32))
        gains[0, 0:1, :] += jnp.sum(dnormed * normed, axis=0, keepdims=True)
        modul[span, :] = (
            hidden[span, :] + norm_back(dnormed * gain_ref[...].reshape(1, -1), normed, inverse)
        ).astype(bf16)

    gains[0] = jnp.zeros(gains.shape[1:], f32)
    move_event(0, 3)
    move_event(2, 2)

    def after_rows(i):
        if i == 0:
            gather_event(gathers[1], 0)
            gather_event(ffn[0], 3)
            gather_event(ffn[1], 1)
        elif i == 1:
            move_event(1, 3)
            send_dtok.start()
            move_event(3, 2)
            gather_event(outs, 2)
        elif i == 2:
            gather_event(gathers[1], 1)

    def last_step(i, carry):
        last_rows(i)
        for k in range(blocks - 1):

            @pl.when(i == k)
            def _(k=k):
                after_rows(k)

        return carry

    lax.fori_loop(0, blocks, last_step, 0)
    move_event(2, 3)
    move_event(4, 2)
    start_qkv(2)
    gather_event(outs, 3)
    gain_copy(0).start()
    keep_dtok = copy_here(modul.at[own_rows, :], dtok_out.at[side], 5)
    gather_event(gathers[1], 2)
    embeddings = every[:, tiles, :]
    for tile in range(tiles):
        part = every[:, tile, :]
        lane = slice(tile * 128, tile * 128 + 128)
        line, start = tile * 128 // width, tile * 128 % width
        branch[line * TEMB : (line + 1) * TEMB, start : start + 128] = lax.dot_general(
            embeddings, part, (((0,), (0,)), ((), ())),
            preferred_element_type=f32, precision=lax.Precision.HIGHEST,
        )
        dbias_ref[0:1, lane] = jnp.sum(part, axis=0, keepdims=True)
    put_dada = copy_here(branch.at[pl.ds(0, 3 * TEMB), :], dada_out, 6)
    move_event(3, 3)
    gain_event(0)
    gather_event(ffn[1], 2)
    gather_event(gathers[1], 3)
    gather_event(gathers[2], 0)
    move_event(4, 3)
    start_qkv(3)
    gain_event(1)
    gather_event(ffn[1], 3)
    gather_event(gathers[2], 1)
    gather_event(gathers[3], 0)
    gain_event(2)
    gather_event(gathers[2], 2)
    gather_event(gathers[3], 1)
    gain_event(3)
    gather_event(gathers[2], 3)
    gather_event(gathers[3], 2)
    gather_event(gathers[3], 3)
    gain_event(4)
    for i in range(4):
        send_mixed(i).wait()
    keep_mixed.wait()
    send_dtok.wait()
    keep_dtok.wait()
    put_dada.wait()


def layer_call(tokens, cot, wq, wo, wu, wd, gain, segments, cosine, sine, embedding, ada, bias):
    length, width = 2 * tokens.shape[1], tokens.shape[2]
    half, hid = wq.shape[2], wu.shape[1]
    block = hid // FEED_STEPS
    pairs = width // 128
    any_ = pl.BlockSpec(memory_space=pl.ANY)
    vm = pl.BlockSpec(memory_space=pltpu.VMEM)
    shape = jax.ShapeDtypeStruct
    dma = pltpu.SemaphoreType.DMA
    low = lambda *dims: pltpu.VMEM(dims, bf16)
    full = lambda *dims: pltpu.VMEM(dims, f32)
    slots = (2, 4, 4, 4, 4)
    reducing = Reducer.scratch(slots, width, block, UP_ORDER)
    reducing += Reducer.scratch(slots, block, width, DOWN_ORDER)
    for order in QKV_ORDERS:
        reducing += Reducer.scratch((2,) * 5, width, 128, order)
    return pl.pallas_call(
        layer_kernel,
        in_specs=[any_] * 6 + [vm] * 7,
        out_specs=[any_] * 11 + [vm] * 2,
        out_shape=[
            shape(wq.shape, bf16),
            shape(wo.shape, bf16),
            shape(wu.shape, bf16),
            shape(wd.shape, bf16),
            shape((width, hid), bf16),
            shape((FEED_STEPS, block, width), bf16),
            shape((width, half), bf16),
            shape(wq.shape, bf16),
            shape((2, length // 2, width), bf16),
            shape((2, length // 2, width), bf16),
            shape((3 * TEMB, width), f32),
            shape((8, 3 * width), f32),
            shape((8, width), f32),
        ],
        scratch_shapes=[
            low(length, width),
            low(length, width),
            low(pairs, length, 128),
            low(pairs, length, 128),
            low(pairs, length, 128),
            low(length, width),
            full(pairs, 8, length),
            full(length, 128),
            low(2, *wq.shape),
            low(width, width),
            low(length, width),
            full(8, width),
            full(length, width),
            low(length, width),
            low(width, length),
            low(length, width),
            full(length, width),
            full(length, width),
            low(length, 2 * block),
            low(length, 2 * block),
            low(2, width, 2 * block),
            low(2, 2 * block, width),
            full(128, length),
            low(FEED_STEPS, 2, width, block),
            low(FEED_STEPS, 2, block, width),
            low(width // 16, hid),
            low(FEED_STEPS, block // 16, width),
            low(3, width // 16, 128),
            low(3, 3, width // 16, 128),
            full(32, 24, 128),
            full(5, 8, width),
            full(5, 8, width),
            dma((14,)),
            dma((7,)),
            dma((7,)),
            dma((10, 4)),
            dma((10, 4)),
            dma((2, 4)),
            dma((2, 2, 4)),
            dma((2, 2, 4)),
            dma((3, 3, 4)),
            dma((3, 3, 4)),
            dma((5,)),
            dma((5,)),
            dma((5,)),
            dma((5,)),
        ]
        + reducing,
        compiler_params=params(collective_id=0, has_side_effects=True),
        name="layer",
    )(tokens, cot, wq, wo, wu, wd, gain, segments, cosine, sine, embedding, ada, bias)


def finish_kernel(
    up_ref, down_ref, left_ref, right_ref, qkv_ref, mixed_ref, dtok_ref, dada_ref, dbias_ref, dgain_ref,
    up_out, down_out, out_out, qkv_out, mixed_out, dtok_out, dada_out, dbias_out, dgain_out,
):
    dbias_out[...] = dbias_ref[0, :]
    dgain_out[...] = dgain_ref[0, :]
    up_out[...] = up_ref[...].astype(f32)
    down_out[...] = down_ref[...].astype(f32)
    out_out[...] = jnp.concatenate([left_ref[...], right_ref[...]], axis=1).astype(f32)
    qkv_out[...] = qkv_ref[...].astype(f32)
    mixed_out[...] = mixed_ref[...]
    dtok_out[...] = dtok_ref[...]
    dada_out[...] = jnp.concatenate([dada_ref[i] for i in range(3)], axis=1)


def finish_call(up, down, out, qkv, mixed, dtok, dada, dbias, dgain):
    steps = 4
    shape = jax.ShapeDtypeStruct
    halves, half = out.shape[0] // 2, out.shape[1]

    def rows(a):
        return pl.BlockSpec((a.shape[0] // steps, a.shape[1]), lambda i: (i, 0))

    def middle(a):
        return pl.BlockSpec((a.shape[0], a.shape[1] // steps, a.shape[2]), lambda i: (0, i, 0))

    part = (halves // steps, half)
    outs = [
        shape(up.shape, f32),
        shape(down.shape, f32),
        shape((halves, 2 * half), f32),
        shape(qkv.shape, f32),
        shape(mixed.shape, bf16),
        shape(dtok.shape, bf16),
        shape((dada.shape[1], 3 * dada.shape[2]), f32),
        shape(dbias.shape[1:], f32),
        shape(dgain.shape[1:], f32),
    ]

    def placed(a):
        if len(a.shape) == 1:
            return pl.BlockSpec(a.shape, lambda i: (0,))
        return rows(a) if len(a.shape) == 2 else middle(a)

    def whole(a):
        return pl.BlockSpec(a.shape, lambda i: (0, 0))

    return pl.pallas_call(
        finish_kernel,
        grid=(steps,),
        in_specs=[
            rows(up),
            rows(down),
            pl.BlockSpec(part, lambda i: (i, 0)),
            pl.BlockSpec(part, lambda i: (i + steps, 0)),
            middle(qkv),
            middle(mixed),
            middle(dtok),
            middle(dada),
            whole(dbias),
            whole(dgain),
        ],
        out_specs=[placed(o) for o in outs],
        out_shape=outs,
        compiler_params=params(),
        name="finish",
    )(up, down, out, out, qkv, mixed, dtok, dada, dbias, dgain)


def time_embedding(timestep):
    half = TEMB // 2
    frequency = jnp.exp(-math.log(10000.0) * jnp.arange(half, dtype=f32) / half)
    angles = timestep.astype(f32)[:, None] * frequency[None, :]
    return jnp.concatenate([jnp.cos(angles), jnp.sin(angles)], axis=-1)


def per_device(
    groups, tokens, segment_ids, timestep, ln_gain, w_qkv, w_out, w_up, w_down, ada_weight, ada_bias, cotangent
):
    half, width = tokens.shape[1], tokens.shape[2]
    length = 2 * half
    cosine, sine = (jnp.asarray(a) for a in rotary_np(length))
    embedding = time_embedding(timestep)

    _, _, _, _, d_up, d_down, d_out, d_qkv, mixed, dtok, d_ada_weight, d_ada_bias, dgain = layer_call(
        tokens, cotangent, w_qkv, w_out, w_up, w_down, ln_gain, segment_ids, cosine, sine,
        embedding, ada_weight, ada_bias,
    )
    d_up, d_down, d_out, d_qkv, mixed, dtok, d_ada_weight, d_ada_bias, d_gain = finish_call(
        d_up, d_down.reshape(-1, width), d_out, d_qkv, mixed, dtok, d_ada_weight.reshape(3, TEMB, width),
        d_ada_bias, dgain,
    )

    def rest(a):
        bit = 16
        while bit < groups:
            a = a + lax.ppermute(a, "dp", [(i, i ^ bit) for i in range(groups)])
            bit *= 2
        return a

    return (
        mixed,
        dtok,
        rest(d_gain),
        rest(d_qkv),
        rest(d_out),
        rest(d_up),
        rest(d_down),
        rest(d_ada_weight),
        rest(d_ada_bias),
    )


def solution(mesh):
    in_specs = (
        P("dp", "tensor", None),
        P("dp", None),
        P("dp"),
        P(),
        P(None, None, "tensor"),
        P("tensor", None),
        P(None, "tensor"),
        P("tensor", None),
        P(),
        P(),
        P("dp", "tensor", None),
    )
    out_specs = (
        P("dp", "tensor", None),
        P("dp", "tensor", None),
        P(),
        P(None, None, "tensor"),
        P("tensor", None),
        P(None, "tensor"),
        P("tensor", None),
        P(),
        P(),
    )
    return jax.shard_map(
        functools.partial(per_device, mesh.shape["dp"]), mesh=mesh, in_specs=in_specs, out_specs=out_specs, check_vma=False
    )
```
